512 devices in a mesh: learn: 32 (over z, y_lo), rep: 2 (over core), tp: 8 (over x, y_hi).
Axes of the slice: x: 4, y: 8 (y_hi: 2, y_lo: 4; y = y_hi * 4 + y_lo), z: 8, core: 2. Of those that a mesh axis runs over, the one named last changes fastest.
Arguments:
- master: float32 [5120, 8, 1280], P(('learn', 'rep'), 'tp'), may hold values from -6 to 6
- adam_first_moment: float32 [5120, 8, 1280], P(('learn', 'rep'), 'tp'), may hold values from -6 to 6
- adam_second_moment: float32 [5120, 8, 1280], P(('learn', 'rep'), 'tp'), may hold values from 0.05 to 1
- gradient: bfloat16 [5120, 8, 1280], P(('learn', 'rep'), 'tp'), may hold values from -6 to 6
- resync_order: int32 [64], replicated, may hold values from 0 to 63, each once
- inputs: bfloat16 [4, 128, 5120], P(None, ('learn', 'rep')), may hold values from -0.3125 to 0.3125
- in_gain: float32 [5120], replicated, may hold values from 0.1 to 1.9
- post_gain: float32 [5120], P('tp'), may hold values from 0.1 to 1.9
- lengths: int32 [128], P(('learn', 'rep')), may hold values from 256 to 2044, as said below
- cached_key_rows: bfloat16 [128, 8, 2048, 128], P(('learn', 'rep'), 'tp'), may hold values from -6 to 6
- cached_value_rows: bfloat16 [128, 8, 2048, 128], P(('learn', 'rep'), 'tp'), may hold values from -6 to 6
Outputs:
- new_master: float32 [5120, 8, 1280], P(('learn', 'rep'), 'tp')
- mixed: bfloat16 [4, 128, 5120], P(None, ('learn', 'rep'), 'tp')
The draws below stay inside these ranges and needn't reach their ends.
Inputs may be any that keep to these rules, and one draw needn't show every extreme that they name: `resync_order`: a permutation of the 64 row blocks. `lengths`: some row has exactly 2044 cached tokens.
All inputs are finite; a program needn't handle non-finite values.
Results may differ from the reference program's by a relative error of at most 0.018.
Values may be sent and summed in bfloat16 or wider, within the bound.
A program may use at most 64 MiB of HBM per device.

```python
import math
import jax
import jax.numpy as jnp
from jax import lax

MODEL_WIDTH = 5120
HEAD_SIZE = 128
KEY_VALUE_HEADS = 8
QUERY_PER_GROUP = 4
CACHE_SLOTS = 2048
STEPS = 4
GROUP_COLUMNS = 1280
LEARNER_BLOCKS = 64
DECODE_ROWS = 128


def draw_lengths(key, part):
    key = jax.random.fold_in(key, 7)
    first_key, second_key = jax.random.split(key)
    drawn = jax.random.randint(first_key, (DECODE_ROWS,), CACHE_SLOTS // 8, CACHE_SLOTS - STEPS + 1)
    chosen = jax.random.randint(second_key, (), 0, DECODE_ROWS)
    return jnp.where(jnp.arange(DECODE_ROWS) == chosen, CACHE_SLOTS - STEPS, drawn).astype(jnp.int32)


def block_levels(key, shape, cuts, smallest, top_value):
    def one(dim, parts):
        draws = jax.random.uniform(jax.random.fold_in(jax.random.fold_in(key, 6), dim), (parts,), jnp.float32, smallest / len(cuts), top_value / len(cuts))
        return jnp.repeat(jnp.exp(draws), shape[dim] // parts).reshape((-1,) + (1,) * (len(shape) - dim - 1))

    level = one(*cuts[0])
    for cut in cuts[1:]:
        level = level * one(*cut)
    return level


def bell_draw(rng, shape, deviation, bound, shards=(), held_as=jnp.bfloat16):
    values = jax.random.normal(rng, shape, jnp.float32) * deviation
    if len(shards) > 0:
        values = block_levels(rng, shape, shards, -0.22, 0.18) * values
    return jnp.clip(values, min=-bound, max=bound).astype(held_as)


def setup_inputs(seed: int = 0) -> dict:
    key_of = jax.random.split(jax.random.key(seed), 12)
    master = bell_draw(key_of[0], (MODEL_WIDTH, KEY_VALUE_HEADS, GROUP_COLUMNS), 1.0, 6.0, ((0, 64), (1, 8)), jnp.float32)
    adam_first_moment = bell_draw(key_of[1], (MODEL_WIDTH, KEY_VALUE_HEADS, GROUP_COLUMNS), 1.0, 6.0, ((0, 64), (1, 8)), jnp.float32)
    adam_second_moment = jnp.clip(jnp.exp(math.log(1.0) - 2.9957323 * jax.random.uniform(key_of[2], (MODEL_WIDTH, KEY_VALUE_HEADS, GROUP_COLUMNS), jnp.float32) ** block_levels(key_of[2], (MODEL_WIDTH, KEY_VALUE_HEADS, GROUP_COLUMNS), ((0, 64), (1, 8)), -0.2, 0.2)), 0.05, 1.0)
    gradient = bell_draw(key_of[3], (MODEL_WIDTH, KEY_VALUE_HEADS, GROUP_COLUMNS), 1.0, 6.0, ((0, 64), (1, 8)))
    resync_order = jax.random.permutation(key_of[4], LEARNER_BLOCKS).astype(jnp.int32)
    inputs = bell_draw(key_of[5], (STEPS, DECODE_ROWS, MODEL_WIDTH), 0.05, 0.3125, ((1, 64),))
    in_gain = jnp.clip(1.0 + 0.18 * jax.random.normal(key_of[6], (MODEL_WIDTH,), jnp.float32), 0.1, 1.9)
    post_gain = jnp.clip(1.0 + 0.18 * jax.random.normal(key_of[7], (MODEL_WIDTH,), jnp.float32), 0.1, 1.9)
    lengths = draw_lengths(jax.random.fold_in(key_of[11], 71), 0)
    cached_key_rows = bell_draw(key_of[9], (DECODE_ROWS, KEY_VALUE_HEADS, CACHE_SLOTS, HEAD_SIZE), 1.0, 6.0, ((0, 64), (1, 8)))
    cached_value_rows = bell_draw(key_of[10], (DECODE_ROWS, KEY_VALUE_HEADS, CACHE_SLOTS, HEAD_SIZE), 1.0, 6.0, ((0, 64), (1, 8)))
    return {"master": master, "adam_first_moment": adam_first_moment, "adam_second_moment": adam_second_moment, "gradient": gradient, "resync_order": resync_order, "inputs": inputs, "in_gain": in_gain, "post_gain": post_gain, "lengths": lengths, "cached_key_rows": cached_key_rows, "cached_value_rows": cached_value_rows}


beta_one = 0.9
beta_two = 0.95
adam_rate = 0.05
adam_decay = 0.1
adam_epsilon = 1e-08
correction_one = 1.0 - 0.9 ** 10
correction_two = 1.0 - 0.95 ** 10
norm_epsilon = 1e-06
rope_theta = 1000000.0

def adam_update(master, adam_first_moment, adam_second_moment, gradient):
    gradient_wide = gradient.astype(jnp.float32)
    first_moment = beta_one * adam_first_moment + (1.0 - beta_one) * gradient_wide
    second_moment = beta_two * adam_second_moment + (1.0 - beta_two) * gradient_wide * gradient_wide
    update = first_moment / correction_one / (jnp.sqrt(second_moment / correction_two) + adam_epsilon) + adam_decay * master
    return master - adam_rate * update

def inverse_order(order):
    places = jnp.arange(order.shape[0], dtype=jnp.int32)
    return lax.optimization_barrier(jnp.sum(jnp.where(order[None, :] == places[:, None], places[None, :], 0), axis=1)).astype(jnp.int32)

def head_norm_gain(values):
    return values * lax.rsqrt(lax.optimization_barrier(jnp.mean(values * values, axis=-1, keepdims=True)) + norm_epsilon)

def rotate(values, positions):
    half_size = values.shape[-1] // 2
    freqs = rope_theta ** (-(jnp.arange(half_size, dtype=jnp.float32) * 2.0 / values.shape[-1]))
    angles = positions.astype(jnp.float32)[:, None] * freqs[None, :]
    cosine = jnp.cos(angles)[:, None, None, :]
    sine = jnp.sin(angles)[:, None, None, :]
    front_half = values[..., :half_size]
    back_half = values[..., half_size:]
    return jnp.concatenate([front_half * cosine - back_half * sine, back_half * cosine + front_half * sine], axis=-1)

def rounded(values):
    return lax.optimization_barrier(values.astype(jnp.bfloat16)).astype(jnp.float32)

def attend_row(operands):
    query_row, recent_keys, recent_values, keys_row, values_row, length_row = operands
    scale = HEAD_SIZE ** (-0.5)
    keys_wide = keys_row.astype(jnp.float32)
    values_wide = values_row.astype(jnp.float32)
    past_scores = jnp.einsum('gqh,gph->gqp', query_row, keys_wide) * scale
    live_mask = jnp.arange(keys_row.shape[1], dtype=jnp.int32) < length_row
    past_exp = jnp.where(live_mask[None, None, :], jnp.exp(past_scores), 0.0)
    recent_exp = jnp.exp(jnp.einsum('gqh,gph->gqp', query_row, recent_keys) * scale)
    denominator = lax.optimization_barrier(jnp.sum(past_exp, axis=-1, keepdims=True)) + lax.optimization_barrier(jnp.sum(recent_exp, axis=-1, keepdims=True))
    past_weights = rounded(past_exp / denominator)
    recent_weights = rounded(recent_exp / denominator)
    head_split = jnp.einsum('gqp,gph->gqh', past_weights, values_wide) + jnp.einsum('gqp,gph->gqh', recent_weights, recent_values)
    return rounded(head_split)

def reference(master, adam_first_moment, adam_second_moment, gradient, resync_order, inputs, in_gain, post_gain, lengths, cached_key_rows, cached_value_rows):
    new_master = adam_update(master, adam_first_moment, adam_second_moment, gradient)
    fresh_token = new_master.astype(jnp.bfloat16)
    inverse_index = inverse_order(resync_order)
    learner_row_blocks = fresh_token.reshape(LEARNER_BLOCKS, MODEL_WIDTH // LEARNER_BLOCKS, KEY_VALUE_HEADS, GROUP_COLUMNS)
    weight_matrix = jnp.take(learner_row_blocks, inverse_index, axis=0).reshape(MODEL_WIDTH, KEY_VALUE_HEADS, GROUP_COLUMNS).astype(jnp.float32)
    query_columns = QUERY_PER_GROUP * HEAD_SIZE
    weights_in = weight_matrix[:, :, :query_columns + 2 * HEAD_SIZE]
    output_weight_matrix = weight_matrix[:, :, query_columns + 2 * HEAD_SIZE:]
    count_of_rows = inputs.shape[1]
    keys_so_far = []
    values_so_far = []
    results = []
    for step_index in range(STEPS):
        stream = inputs[step_index].astype(jnp.float32)
        normed_in = rounded(stream * lax.rsqrt(lax.optimization_barrier(jnp.mean(stream * stream, axis=-1, keepdims=True)) + norm_epsilon) * in_gain)
        projected_input = jnp.einsum('nd,dgc->ngc', normed_in, weights_in) / jnp.sqrt(jnp.float32(MODEL_WIDTH))
        query_rows = head_norm_gain(projected_input[:, :, :query_columns].reshape(count_of_rows, KEY_VALUE_HEADS, QUERY_PER_GROUP, HEAD_SIZE))
        latest_keys = head_norm_gain(projected_input[:, :, query_columns:query_columns + HEAD_SIZE].reshape(count_of_rows, KEY_VALUE_HEADS, 1, HEAD_SIZE))
        latest_values = projected_input[:, :, query_columns + HEAD_SIZE:].reshape(count_of_rows, KEY_VALUE_HEADS, 1, HEAD_SIZE)
        positions = lengths + step_index
        query_rows = rounded(rotate(query_rows, positions))
        latest_keys = rounded(rotate(latest_keys, positions))
        latest_values = rounded(latest_values)
        keys_so_far.append(latest_keys)
        values_so_far.append(latest_values)
        recent_keys = jnp.concatenate(keys_so_far, axis=2)
        recent_values = jnp.concatenate(values_so_far, axis=2)
        head_split = lax.map(attend_row, (query_rows, recent_keys, recent_values, cached_key_rows, cached_value_rows, lengths))
        head_split = head_split.reshape(count_of_rows, KEY_VALUE_HEADS, query_columns)
        attention_output = jnp.einsum('bae,oae->bo', head_split, output_weight_matrix) / jnp.sqrt(jnp.float32(KEY_VALUE_HEADS * query_columns))
        residual = stream + attention_output
        normed_out = residual * lax.rsqrt(lax.optimization_barrier(jnp.mean(residual * residual, axis=-1, keepdims=True)) + norm_epsilon) * post_gain
        results.append(normed_out.astype(jnp.bfloat16))
    return (new_master, jnp.stack(results))
```

```python
import functools

import jax
import jax.numpy as jnp
import numpy as np
from jax import lax
from jax.experimental import pallas as pl
from jax.experimental.pallas import tpu as pltpu
from jax.sharding import PartitionSpec as P

MODEL_WIDTH = 5120
HEAD_SIZE = 128
KEY_VALUE_HEADS = 8
QUERY_PER_GROUP = 4
STEPS = 4
CACHE_SLOTS = 2048
BLOCKS = 64
ROWS = 80
IN_COLUMNS = 768
OUT_COLUMNS = 512
TOKENS = 8
QPEERS = 16

beta_one = 0.9
beta_two = 0.95
adam_rate = 0.05
adam_decay = 0.1
adam_epsilon = 1e-08
correction_one = 1.0 - 0.9**10
correction_two = 1.0 - 0.95**10
norm_epsilon = 1e-06
rope_theta = 1000000.0

MESH = pl.DeviceIdType.MESH
F32 = jnp.float32
BF16 = jnp.bfloat16


def adam_update(master, first, second, gradient):
    first_moment = beta_one * first + (1.0 - beta_one) * gradient
    second_moment = beta_two * second + (1.0 - beta_two) * gradient * gradient
    update = (
        first_moment / correction_one / (jnp.sqrt(second_moment / correction_two) + adam_epsilon)
        + adam_decay * master
    )
    return master - adam_rate * update


def widen(block):
    return jnp.concatenate([block, jnp.zeros((block.shape[0], 128 - ROWS), block.dtype)], axis=1)


def kernel(
    order, lengths, x_in, gain_in, post_in, freq_in, master_in, first_in, second_in, gradient_in, keys_in, values_in,
    master_out, mixed_out,
    x_v, gain_v, xs, xblk, hblk, xperm, zblk, master_v, first_v, second_v, gradient_v, keys_v, values_v,
    hs, hr, wq, wo, ps, pr, os, orr, s4, r4, s5, r5,
    load_sem, out_sem, h_send, h_recv, wq_send, wq_recv, ring_send, ring_recv, twin_send, twin_recv,
    p_send, p_recv, o_send, o_recv, r4_send, r4_recv, r5_send, r5_self, r5_recv,
):
    l, r, t = lax.axis_index("learn"), lax.axis_index("rep"), lax.axis_index("tp")
    z, y = lax.div(l, 4), lax.rem(l, 4)
    yp, yy = lax.div(y, 2), lax.rem(y, 2)
    c = z * 2 + yp
    xx, yh = lax.div(t, 2), lax.rem(t, 2)

    def dev(z, y, r, t):
        return {"learn": z * 4 + y, "rep": r, "tp": t}

    def q_peer(d):
        other = lax.rem(c + d, QPEERS)
        return dev(lax.div(other, 2), lax.rem(other, 2) * 2 + yy, r, t)

    twin = dev(z, y, 1 - r, t)
    partner = dev(z, yp * 2 + 1 - yy, r, t)
    diagonal = dev(z, yp * 2 + 1 - yy, 1 - r, t)
    above = dev(lax.rem(z + 1, 8), y, r, t)
    below = dev(lax.rem(z + 7, 8), y, r, t)

    def y_peer(d):
        return dev(z, lax.rem(y + d, 4), r, t)

    def x_peer(e):
        return dev(z, y, r, lax.rem(xx + e, 4) * 2 + yh)

    loads = [
        pltpu.make_async_copy(src, dst, load_sem.at[i])
        for i, (src, dst) in enumerate(
            [
                (x_in, x_v), (gain_in, gain_v), (master_in, master_v), (first_in, first_v), (second_in, second_v),
                (gradient_in, gradient_v), (keys_in, keys_v), (values_in, values_v),
            ]
        )
    ]
    for load in loads:
        load.start()

    barrier = pltpu.get_barrier_semaphore()

    def greet(device):
        pl.semaphore_signal(barrier, inc=1, device_id=device, device_id_type=MESH)

    def greet_q(d, carry):
        greet(q_peer(d))
        return carry

    lax.fori_loop(1, QPEERS, greet_q, 0)
    for device in (twin, partner, diagonal, above, below):
        greet(device)
    for d in range(1, 4):
        greet(y_peer(d))
        greet(x_peer(d))
    for e in range(8):
        there = lax.rem(t + e, 8)
        device = dev(z, lax.rem(y + lax.div(there, 2), 4), r, there)
        if e == 0:
            pl.when(xx != 0)(functools.partial(greet, device))
        else:
            greet(device)
    greetings = (QPEERS - 1) + 5 + 6 + 7 + jnp.where(xx != 0, 1, 0)

    loads[0].wait()
    loads[1].wait()
    for s in range(STEPS):
        xs[2 * s : 2 * s + 2, :] = x_v[s].astype(F32)
    stream = xs[...]
    rscale = lax.rsqrt(jnp.mean(stream * stream, axis=1, keepdims=True) + norm_epsilon)
    for b in range(BLOCKS):
        block = xs[:, b * ROWS : (b + 1) * ROWS]
        xblk[b] = widen(block)
        hblk[b] = widen(block * rscale * gain_v[:, b * ROWS : (b + 1) * ROWS])
    for d in range(QPEERS):
        other = lax.rem(c + d, QPEERS)
        parts = []
        for m in range(4):
            my, mr = m // 2, m % 2
            w = lax.rem(yy + my, 2) * 2 + lax.rem(r + mr, 2)
            parts.append(hblk[order[other * 4 + w]])
        piece = jnp.concatenate(parts, axis=0).astype(BF16)
        if d == 0:
            hr[0] = piece
        else:
            hs[d] = piece

    wq[:, ROWS:, :] = jnp.zeros((4, 128 - ROWS, IN_COLUMNS), BF16)
    for i in range(2, 6):
        loads[i].wait()
    for j in range(10):
        rows = pl.ds(j, ROWS, stride=10)
        fresh = adam_update(
            master_v[rows, :], first_v[rows, :], second_v[rows, :], gradient_v[:, j * 128 : (j + 1) * 128].astype(F32)
        )
        master_v[rows, :] = fresh
        if j < 6:
            wq[0, 0:ROWS, j * 128 : (j + 1) * 128] = fresh.astype(BF16)
        else:
            wo[0, 0, :, (j - 6) * 128 : (j - 5) * 128] = fresh.astype(BF16)
    write_master = pltpu.make_async_copy(master_v, master_out, out_sem)
    write_master.start()

    pl.semaphore_wait(barrier, greetings)

    def send_h(d, carry):
        pltpu.make_async_remote_copy(
            src_ref=hs.at[d], dst_ref=hr.at[d], send_sem=h_send, recv_sem=h_recv, device_id=q_peer(d), device_id_type=MESH
        ).start()
        return carry

    lax.fori_loop(1, QPEERS, send_h, 0)
    for m, device in ((2, partner), (3, diagonal), (1, twin)):
        pltpu.make_async_remote_copy(
            src_ref=wq.at[0, pl.ds(0, ROWS)],
            dst_ref=wq.at[m, pl.ds(0, ROWS)],
            send_sem=wq_send.at[m - 1],
            recv_sem=wq_recv.at[m - 1],
            device_id=device,
            device_id_type=MESH,
        ).start()

    def ring(src, dst, index, device):
        return pltpu.make_async_remote_copy(
            src_ref=wo.at[src, 0],
            dst_ref=wo.at[dst, 0],
            send_sem=ring_send.at[index],
            recv_sem=ring_recv.at[index],
            device_id=device,
            device_id_type=MESH,
        )

    up = [ring(k, k + 1, k, above) for k in range(4)]
    down = [ring((8 - k) % 8, 7 - k, 4 + k, below) for k in range(3)]
    to_twin = [
        pltpu.make_async_remote_copy(
            src_ref=wo.at[k, 0],
            dst_ref=wo.at[k, 1],
            send_sem=twin_send.at[k],
            recv_sem=twin_recv.at[k],
            device_id=twin,
            device_id_type=MESH,
        )
        for k in range(8)
    ]
    up[0].start()
    down[0].start()
    to_twin[0].start()

    token = lax.broadcasted_iota(jnp.int32, (TOKENS, HEAD_SIZE), 0)
    lane = lax.broadcasted_iota(jnp.int32, (TOKENS, HEAD_SIZE), 1)
    positions = jnp.where(lax.rem(token, 2) == 0, lengths[0], lengths[1]) + lax.div(token, 2)
    angles = positions.astype(F32) * freq_in[...]
    cosine = jnp.cos(angles)
    sine = jnp.sin(angles)
    sine = jnp.where(lane < HEAD_SIZE // 2, -sine, sine)

    def find(j, carry):
        actor = order[j] - t * 8
        return tuple(jnp.where(actor == i, j, carry[i]) for i in range(8))

    stored = lax.fori_loop(0, BLOCKS, find, tuple(jnp.int32(0) for _ in range(8)))
    for xs_ in range(4):
        source_y = lax.rem(y + xs_, 4)
        for k in range(8):
            for rr in range(2):
                j = (lax.rem(z + 8 - k, 8) * 4 + source_y) * 2 + lax.rem(r + rr, 2)
                xperm[xs_ * 16 + k * 2 + rr] = xblk[order[j]]

    pltpu.make_async_copy(hr.at[pl.ds(1, QPEERS - 1)], hr.at[pl.ds(1, QPEERS - 1)], h_recv).wait()
    wide = hr[...].astype(F32)
    left = jnp.concatenate([wide[:, 8 * m : 8 * m + 8, :].reshape(QPEERS * TOKENS, 128) for m in range(4)], axis=1).astype(BF16)
    for m in range(3):
        pltpu.make_async_copy(wq.at[0, pl.ds(0, ROWS)], wq.at[0, pl.ds(0, ROWS)], wq_recv.at[m]).wait()
    partial = jnp.dot(left, wq[...].reshape(512, IN_COLUMNS), preferred_element_type=F32).reshape(QPEERS, TOKENS, IN_COLUMNS)
    packed = jnp.concatenate([partial[:, :, :384], partial[:, :, 384:]], axis=1).astype(BF16)
    pr[0] = packed[0]
    ps[...] = packed

    def send_p(d, carry):
        pltpu.make_async_remote_copy(
            src_ref=ps.at[d],
            dst_ref=pr.at[d],
            send_sem=p_send,
            recv_sem=p_recv,
            device_id=q_peer(QPEERS - d),
            device_id_type=MESH,
        ).start()
        return carry

    lax.fori_loop(1, QPEERS, send_p, 0)
    for k in range(1, 4):
        up[k - 1].wait_recv()
        up[k].start()
        to_twin[k].start()
        down[k - 1].wait_recv()
        if k < 3:
            down[k].start()
        to_twin[8 - k].start()
    up[3].wait_recv()
    to_twin[4].start()
    pltpu.make_async_copy(pr.at[pl.ds(1, QPEERS - 1)], pr.at[pl.ds(1, QPEERS - 1)], p_recv).wait()
    projected = jnp.sum(pr[...].astype(F32), axis=0) * np.float32(1.0 / np.sqrt(np.float32(MODEL_WIDTH)))
    top, bottom = projected[0:8], projected[8:16]
    raw = jnp.concatenate(
        [top[:, 0:128], top[:, 128:256], top[:, 256:384], bottom[:, 0:128], bottom[:, 128:256]], axis=0
    )
    new_values = bottom[:, 256:384].astype(BF16)
    normed = raw * lax.rsqrt(jnp.mean(raw * raw, axis=1, keepdims=True) + norm_epsilon)
    cosine5 = jnp.concatenate([cosine] * 5, axis=0)
    sine5 = jnp.concatenate([sine] * 5, axis=0)
    rotated = (normed * cosine5 + pltpu.roll(normed, HEAD_SIZE // 2, 1) * sine5).astype(BF16)
    queries = rotated[0:32]
    new_keys = rotated[32:40]

    scale = HEAD_SIZE ** (-0.5)
    contract_last = (((1,), (1,)), ((), ()))
    loads[6].wait()
    loads[7].wait()
    q_token = lax.rem(lax.broadcasted_iota(jnp.int32, (32, TOKENS), 0), 8)
    k_token = lax.broadcasted_iota(jnp.int32, (32, TOKENS), 1)
    recent = lax.dot_general(queries, new_keys, contract_last, preferred_element_type=F32) * scale
    seen = (lax.rem(q_token, 2) == lax.rem(k_token, 2)) & (lax.div(k_token, 2) <= lax.div(q_token, 2))
    recent = jnp.where(seen, jnp.exp(recent), 0.0)
    total = jnp.sum(recent, axis=1, keepdims=True)
    heads = jnp.dot(recent.astype(BF16), new_values, preferred_element_type=F32)
    slot = lax.broadcasted_iota(jnp.int32, (32, CACHE_SLOTS), 1)
    row_of = lax.rem(lax.broadcasted_iota(jnp.int32, (32, CACHE_SLOTS), 0), 2)
    for n in range(2):
        scores = (
            lax.dot_general(queries, keys_v[n * CACHE_SLOTS : (n + 1) * CACHE_SLOTS, :], contract_last, preferred_element_type=F32)
            * scale
        )
        past = jnp.where((slot < lengths[n]) & (row_of == n), jnp.exp(scores), 0.0)
        total = total + jnp.sum(past, axis=1, keepdims=True)
        heads = heads + jnp.dot(
            past.astype(BF16), values_v[n * CACHE_SLOTS : (n + 1) * CACHE_SLOTS, :], preferred_element_type=F32
        )
    heads = (heads / total).astype(BF16)

    os[...] = heads
    orr[0] = heads
    for d in range(1, 4):
        pltpu.make_async_remote_copy(
            src_ref=os, dst_ref=orr.at[d], send_sem=o_send.at[d - 1], recv_sem=o_recv.at[d - 1], device_id=y_peer(d), device_id_type=MESH
        ).start()
    for k in range(8):
        to_twin[k].wait_recv()
    for d in range(3):
        pltpu.make_async_copy(os, os, o_recv.at[d]).wait()
    wide = orr[...].astype(F32)
    left = jnp.concatenate([wide[:, 8 * h : 8 * h + 8, :].reshape(32, 128) for h in range(4)], axis=1).astype(BF16)
    attn = lax.dot_general(left, wo[...].reshape(16 * ROWS, OUT_COLUMNS), contract_last, preferred_element_type=F32)
    attn = attn * np.float32(1.0 / np.sqrt(np.float32(KEY_VALUE_HEADS * OUT_COLUMNS)))
    attn = attn.reshape(4, 8, 1280)
    s4[...] = jnp.concatenate([attn[:, :, :640], attn[:, :, 640:]], axis=1).astype(BF16)
    for e in range(1, 4):
        pltpu.make_async_remote_copy(
            src_ref=s4.at[lax.rem(xx + e, 4)],
            dst_ref=r4.at[e - 1],
            send_sem=r4_send.at[e - 1],
            recv_sem=r4_recv.at[e - 1],
            device_id=x_peer(e),
            device_id_type=MESH,
        ).start()
    summed = s4[xx].astype(F32)
    for e in range(3):
        pltpu.make_async_copy(s4.at[0], s4.at[0], r4_recv.at[e]).wait()
        summed = summed + r4[e].astype(F32)
    s5[...] = summed.astype(BF16)
    target_y = lax.rem(y + 4 - xx, 4)

    def to_owner(e):
        there = lax.rem(t + e, 8)
        return pltpu.make_async_remote_copy(
            src_ref=s5,
            dst_ref=r5.at[t],
            send_sem=r5_send.at[e],
            recv_sem=r5_recv,
            device_id=dev(z, target_y, r, there),
            device_id_type=MESH,
        )

    def own_copy():
        return pltpu.make_async_copy(s5, r5.at[t], r5_recv)

    for e in range(1, 8):
        to_owner(e).start()

    @pl.when(xx != 0)
    def _():
        to_owner(0).start()

    @pl.when(xx == 0)
    def _():
        own_copy().start()

    pltpu.make_async_copy(r5, r5, r5_recv).wait()

    squares = jnp.zeros((TOKENS, 128), F32)
    for xs_ in range(4):
        both = r5[2 * xs_].astype(F32) + r5[2 * xs_ + 1].astype(F32)
        for b in range(8):
            block = widen(both[:, b * ROWS : (b + 1) * ROWS])
            for half in range(2):
                place = xs_ * 16 + half * 8 + b
                residual = block[half * 8 : half * 8 + 8] + xperm[place]
                zblk[place] = residual
                squares = squares + residual * residual
    rscale = lax.rsqrt(jnp.sum(squares, axis=1, keepdims=True) * np.float32(1.0 / MODEL_WIDTH) + norm_epsilon)
    pieces = []
    for i in range(8):
        j = stored[i]
        k = lax.rem(z + 8 - lax.div(j, 8), 8)
        source = lax.rem(lax.rem(lax.div(j, 2), 4) + 4 - y, 4)
        rr = lax.rem(lax.rem(j, 2) + r, 2)
        pieces.append(zblk[source * 16 + k * 2 + rr][:, :ROWS])
    mixed_out[...] = (jnp.concatenate(pieces, axis=1) * rscale * post_in[...]).astype(BF16)

    write_master.wait()
    pltpu.make_async_copy(hs.at[pl.ds(1, QPEERS - 1)], hs.at[pl.ds(1, QPEERS - 1)], h_send).wait()
    pltpu.make_async_copy(ps.at[pl.ds(1, QPEERS - 1)], ps.at[pl.ds(1, QPEERS - 1)], p_send).wait()
    for m in range(3):
        pltpu.make_async_copy(wq.at[0, pl.ds(0, ROWS)], wq.at[0, pl.ds(0, ROWS)], wq_send.at[m]).wait()
    for copy in up + down + to_twin:
        copy.wait_send()
    for d in range(3):
        pltpu.make_async_copy(os, os, o_send.at[d]).wait()
        pltpu.make_async_copy(s4.at[0], s4.at[0], r4_send.at[d]).wait()
    for e in range(1, 8):
        to_owner(e).wait_send()

    @pl.when(xx != 0)
    def _():
        to_owner(0).wait_send()


def body(
    master, adam_first_moment, adam_second_moment, gradient, resync_order, inputs, in_gain, post_gain, lengths,
    cached_key_rows, cached_value_rows,
):
    half = np.arange(HEAD_SIZE // 2, dtype=np.float64)
    freqs = (rope_theta ** (-(half * 2.0 / HEAD_SIZE))).astype(np.float32)
    freqs = jnp.asarray(np.concatenate([freqs, freqs])[None, :])
    smem = pl.BlockSpec(memory_space=pltpu.SMEM)
    vmem = pl.BlockSpec(memory_space=pltpu.VMEM)
    anywhere = pl.BlockSpec(memory_space=pl.ANY)
    dma = pltpu.SemaphoreType.DMA
    flat = (ROWS * 10, 128)
    new_master, mixed = pl.pallas_call(
        kernel,
        out_shape=(jax.ShapeDtypeStruct(flat, F32), jax.ShapeDtypeStruct((TOKENS, 640), BF16)),
        in_specs=[smem, smem, anywhere, anywhere, vmem, vmem] + [anywhere] * 6,
        out_specs=(anywhere, vmem),
        scratch_shapes=[
            pltpu.VMEM((STEPS, 2, MODEL_WIDTH), BF16),
            pltpu.VMEM((1, MODEL_WIDTH), F32),
            pltpu.VMEM((TOKENS, MODEL_WIDTH), F32),
            pltpu.VMEM((BLOCKS, TOKENS, 128), F32),
            pltpu.VMEM((BLOCKS, TOKENS, 128), F32),
            pltpu.VMEM((BLOCKS, TOKENS, 128), F32),
            pltpu.VMEM((BLOCKS, TOKENS, 128), F32),
            pltpu.VMEM(flat, F32),
            pltpu.VMEM(flat, F32),
            pltpu.VMEM(flat, F32),
            pltpu.VMEM((ROWS, 1280), BF16),
            pltpu.VMEM((2 * CACHE_SLOTS, HEAD_SIZE), BF16),
            pltpu.VMEM((2 * CACHE_SLOTS, HEAD_SIZE), BF16),
            pltpu.VMEM((QPEERS, 32, 128), BF16),
            pltpu.VMEM((QPEERS, 32, 128), BF16),
            pltpu.VMEM((4, 128, IN_COLUMNS), BF16),
            pltpu.VMEM((8, 2, ROWS, OUT_COLUMNS), BF16),
            pltpu.VMEM((QPEERS, 16, 384), BF16),
            pltpu.VMEM((QPEERS, 16, 384), BF16),
            pltpu.VMEM((32, 128), BF16),
            pltpu.VMEM((4, 32, 128), BF16),
            pltpu.VMEM((4, 16, 640), BF16),
            pltpu.VMEM((3, 16, 640), BF16),
            pltpu.VMEM((16, 640), BF16),
            pltpu.VMEM((8, 16, 640), BF16),
            dma((8,)), dma, dma, dma, dma((3,)), dma((3,)), dma((7,)), dma((7,)), dma((8,)), dma((8,)),
            dma, dma, dma((3,)), dma((3,)), dma((3,)), dma((3,)), dma((8,)), dma, dma,
        ],
        compiler_params=pltpu.CompilerParams(collective_id=0, has_side_effects=True, vmem_limit_bytes=40 << 20),
        cost_estimate=pl.CostEstimate(flops=400_000_000, bytes_accessed=4_500_000, transcendentals=200_000),
        name="adam_attention",
    )(
        resync_order, lengths, inputs, in_gain.reshape(1, MODEL_WIDTH), post_gain.reshape(1, 640), freqs,
        master.reshape(flat), adam_first_moment.reshape(flat), adam_second_moment.reshape(flat), gradient.reshape(ROWS, 1280),
        cached_key_rows.reshape(2 * CACHE_SLOTS, HEAD_SIZE), cached_value_rows.reshape(2 * CACHE_SLOTS, HEAD_SIZE),
    )
    return new_master.reshape(ROWS, 1, 1280), mixed.reshape(STEPS, 2, 640)


def solution(mesh):
    in_specs = (
        P(("learn", "rep"), "tp", None),
        P(("learn", "rep"), "tp", None),
        P(("learn", "rep"), "tp", None),
        P(("learn", "rep"), "tp", None),
        P(),
        P(None, ("learn", "rep"), None),
        P(),
        P("tp"),
        P(("learn", "rep")),
        P(("learn", "rep"), "tp", None, None),
        P(("learn", "rep"), "tp", None, None),
    )
    out_specs = (P(("learn", "rep"), "tp", None), P(None, ("learn", "rep"), "tp"))
    return jax.shard_map(body, mesh=mesh, in_specs=in_specs, out_specs=out_specs, check_vma=False)
```

```python
import functools

import jax
import jax.numpy as jnp
import numpy as np
from jax import lax
from jax.experimental import pallas as pl
from jax.experimental.pallas import tpu as pltpu
from jax.sharding import PartitionSpec as P

MODEL_WIDTH = 5120
HEAD_SIZE = 128
KEY_VALUE_HEADS = 8
QUERY_PER_GROUP = 4
STEPS = 4
CACHE_SLOTS = 2048
BLOCKS = 64
ROWS = 80
IN_COLUMNS = 768
OUT_COLUMNS = 512
TOKENS = 8
QPEERS = 16

beta_one = 0.9
beta_two = 0.95
adam_rate = 0.05
adam_decay = 0.1
adam_epsilon = 1e-08
correction_one = 1.0 - 0.9**10
correction_two = 1.0 - 0.95**10
norm_epsilon = 1e-06
rope_theta = 1000000.0

MESH = pl.DeviceIdType.MESH
F32 = jnp.float32
BF16 = jnp.bfloat16


def adam_update(master, first, second, gradient):
    first_moment = beta_one * first + (1.0 - beta_one) * gradient
    second_moment = beta_two * second + (1.0 - beta_two) * gradient * gradient
    update = (
        first_moment / correction_one / (jnp.sqrt(second_moment / correction_two) + adam_epsilon)
        + adam_decay * master
    )
    return master - adam_rate * update


def widen(block):
    return jnp.concatenate([block, jnp.zeros((block.shape[0], 128 - ROWS), block.dtype)], axis=1)


def kernel(
    order_in, lengths_in, x_in, gain_in, post_in, freq_in, master_in, first_in, second_in, gradient_in, keys_in, values_in,
    master_out, mixed_out,
    order, lengths, post_v, freq_v, x_v, gain_v, xs, xblk, hblk, xperm, zblk, master_v, first_v, second_v, gradient_v, keys_v, values_v,
    hs, hr, wq, wo, ps, pr, os, orr, s4, r4, s5, r5,
    load_sem, out_sem, h_send, h_recv, wq_send, wq_recv, ring_send, ring_recv, twin_send, twin_recv,
    p_send, p_recv, o_send, o_recv, r4_send, r4_recv, r5_send, r5_self, r5_recv,
):
    l, r, t = lax.axis_index("learn"), lax.axis_index("rep"), lax.axis_index("tp")
    z, y = lax.div(l, 4), lax.rem(l, 4)
    yp, yy = lax.div(y, 2), lax.rem(y, 2)
    c = z * 2 + yp
    xx, yh = lax.div(t, 2), lax.rem(t, 2)

    def dev(z, y, r, t):
        return {"learn": z * 4 + y, "rep": r, "tp": t}

    def q_peer(d):
        other = lax.rem(c + d, QPEERS)
        return dev(lax.div(other, 2), lax.rem(other, 2) * 2 + yy, r, t)

    twin = dev(z, y, 1 - r, t)
    partner = dev(z, yp * 2 + 1 - yy, r, t)
    diagonal = dev(z, yp * 2 + 1 - yy, 1 - r, t)
    above = dev(lax.rem(z + 1, 8), y, r, t)
    below = dev(lax.rem(z + 7, 8), y, r, t)

    def y_peer(d):
        return dev(z, lax.rem(y + d, 4), r, t)

    def x_peer(e):
        return dev(z, y, r, lax.rem(xx + e, 4) * 2 + yh)

    pending = []

    loads = [
        pltpu.make_async_copy(src, dst, load_sem.at[i])
        for i, (src, dst) in enumerate(
            [
                (x_in, x_v), (gain_in, gain_v), (master_in, master_v), (first_in, first_v), (second_in, second_v),
                (gradient_in, gradient_v), (keys_in, keys_v), (values_in, values_v),
                (order_in, order), (lengths_in, lengths), (post_in, post_v), (freq_in, freq_v),
            ]
        )
    ]
    for load in loads:
        load.start()

    barrier = pltpu.get_barrier_semaphore()

    def greet(device):
        pl.semaphore_signal(barrier, inc=1, device_id=device, device_id_type=MESH)

    def greet_q(d, carry):
        greet(q_peer(d))
        return carry

    lax.fori_loop(1, QPEERS, greet_q, 0)
    for device in (twin, partner, diagonal, above, below):
        greet(device)
    for d in range(1, 4):
        greet(y_peer(d))
        greet(x_peer(d))
    for e in range(8):
        there = lax.rem(t + e, 8)
        device = dev(z, lax.rem(y + lax.div(there, 2), 4), r, there)
        if e == 0:
            pl.when(xx != 0)(functools.partial(greet, device))
        else:
            greet(device)
    greetings = (QPEERS - 1) + 5 + 6 + 7 + jnp.where(xx != 0, 1, 0)

    loads[0].wait()
    loads[1].wait()
    loads[8].wait()
    for s in range(STEPS):
        xs[2 * s : 2 * s + 2, :] = x_v[s].astype(F32)
    stream = xs[...]
    rscale = lax.rsqrt(jnp.mean(stream * stream, axis=1, keepdims=True) + norm_epsilon)
    for b in range(BLOCKS):
        block = xs[:, b * ROWS : (b + 1) * ROWS]
        xblk[b] = widen(block)
        hblk[b] = widen(block * rscale * gain_v[:, b * ROWS : (b + 1) * ROWS])
    for d in range(QPEERS):
        other = lax.rem(c + d, QPEERS)
        parts = []
        for m in range(4):
            my, mr = m // 2, m % 2
            w = lax.rem(yy + my, 2) * 2 + lax.rem(r + mr, 2)
            parts.append(hblk[order[other * 4 + w]])
        piece = jnp.concatenate(parts, axis=0).astype(BF16)
        if d == 0:
            hr[0] = piece
        else:
            hs[d] = piece

    wq[:, ROWS:, :] = jnp.zeros((4, 128 - ROWS, IN_COLUMNS), BF16)
    for i in range(2, 6):
        loads[i].wait()
    for j in range(10):
        rows = pl.ds(j, ROWS, stride=10)
        fresh = adam_update(
            master_v[rows, :], first_v[rows, :], second_v[rows, :], gradient_v[:, j * 128 : (j + 1) * 128].astype(F32)
        )
        master_v[rows, :] = fresh
        if j < 6:
            wq[0, 0:ROWS, j * 128 : (j + 1) * 128] = fresh.astype(BF16)
        else:
            wo[0, 0, :, (j - 6) * 128 : (j - 5) * 128] = fresh.astype(BF16)
    write_master = pltpu.make_async_copy(master_v, master_out, out_sem)
    write_master.start()
    pending.append(write_master.wait)

    pl.semaphore_wait(barrier, greetings)

    def send_h(d, carry):
        pltpu.make_async_remote_copy(
            src_ref=hs.at[d], dst_ref=hr.at[d], send_sem=h_send, recv_sem=h_recv, device_id=q_peer(d), device_id_type=MESH
        ).start()
        return carry

    lax.fori_loop(1, QPEERS, send_h, 0)
    pending.append(pltpu.make_async_copy(hs.at[pl.ds(1, QPEERS - 1)], hs.at[pl.ds(1, QPEERS - 1)], h_send).wait)
    for m, device in ((2, partner), (3, diagonal), (1, twin)):
        copy = pltpu.make_async_remote_copy(
            src_ref=wq.at[0, pl.ds(0, ROWS)],
            dst_ref=wq.at[m, pl.ds(0, ROWS)],
            send_sem=wq_send.at[m - 1],
            recv_sem=wq_recv.at[m - 1],
            device_id=device,
            device_id_type=MESH,
        )
        copy.start()
        pending.append(copy.wait_send)

    def ring(src, dst, index, device):
        return pltpu.make_async_remote_copy(
            src_ref=wo.at[src, 0],
            dst_ref=wo.at[dst, 0],
            send_sem=ring_send.at[index],
            recv_sem=ring_recv.at[index],
            device_id=device,
            device_id_type=MESH,
        )

    up = [ring(k, k + 1, k, above) for k in range(4)]
    down = [ring((8 - k) % 8, 7 - k, 4 + k, below) for k in range(3)]
    to_twin = [
        pltpu.make_async_remote_copy(
            src_ref=wo.at[k, 0],
            dst_ref=wo.at[k, 1],
            send_sem=twin_send.at[k],
            recv_sem=twin_recv.at[k],
            device_id=twin,
            device_id_type=MESH,
        )
        for k in range(8)
    ]
    pending.extend(copy.wait_send for copy in up + down + to_twin)
    up[0].start()
    down[0].start()
    to_twin[0].start()

    loads[9].wait()
    loads[10].wait()
    loads[11].wait()
    token = lax.broadcasted_iota(jnp.int32, (TOKENS, HEAD_SIZE), 0)
    lane = lax.broadcasted_iota(jnp.int32, (TOKENS, HEAD_SIZE), 1)
    positions = jnp.where(lax.rem(token, 2) == 0, lengths[0], lengths[1]) + lax.div(token, 2)
    angles = positions.astype(F32) * freq_v[...]
    cosine = jnp.cos(angles)
    sine = jnp.sin(angles)
    sine = jnp.where(lane < HEAD_SIZE // 2, -sine, sine)

    def find(j, carry):
        actor = order[j] - t * 8
        return tuple(jnp.where(actor == i, j, carry[i]) for i in range(8))

    stored = lax.fori_loop(0, BLOCKS, find, tuple(jnp.int32(0) for _ in range(8)))
    for xs_ in range(4):
        source_y = lax.rem(y + xs_, 4)
        for k in range(8):
            for rr in range(2):
                j = (lax.rem(z + 8 - k, 8) * 4 + source_y) * 2 + lax.rem(r + rr, 2)
                xperm[xs_ * 16 + k * 2 + rr] = xblk[order[j]]

    pltpu.make_async_copy(hr.at[pl.ds(1, QPEERS - 1)], hr.at[pl.ds(1, QPEERS - 1)], h_recv).wait()
    wide = hr[...].astype(F32)
    left = jnp.concatenate([wide[:, 8 * m : 8 * m + 8, :].reshape(QPEERS * TOKENS, 128) for m in range(4)], axis=1).astype(BF16)
    for m in range(3):
        pltpu.make_async_copy(wq.at[0, pl.ds(0, ROWS)], wq.at[0, pl.ds(0, ROWS)], wq_recv.at[m]).wait()
    partial = jnp.dot(left, wq[...].reshape(512, IN_COLUMNS), preferred_element_type=F32).reshape(QPEERS, TOKENS, IN_COLUMNS)
    packed = jnp.concatenate([partial[:, :, :384], partial[:, :, 384:]], axis=1).astype(BF16)
    pr[0] = packed[0]
    ps[...] = packed

    def send_p(d, carry):
        pltpu.make_async_remote_copy(
            src_ref=ps.at[d],
            dst_ref=pr.at[d],
            send_sem=p_send,
            recv_sem=p_recv,
            device_id=q_peer(QPEERS - d),
            device_id_type=MESH,
        ).start()
        return carry

    lax.fori_loop(1, QPEERS, send_p, 0)
    pending.append(pltpu.make_async_copy(ps.at[pl.ds(1, QPEERS - 1)], ps.at[pl.ds(1, QPEERS - 1)], p_send).wait)
    for k in range(1, 4):
        up[k - 1].wait_recv()
        up[k].start()
        to_twin[k].start()
        down[k - 1].wait_recv()
        if k < 3:
            down[k].start()
        to_twin[8 - k].start()
    up[3].wait_recv()
    to_twin[4].start()
    pltpu.make_async_copy(pr.at[pl.ds(1, QPEERS - 1)], pr.at[pl.ds(1, QPEERS - 1)], p_recv).wait()
    projected = jnp.sum(pr[...].astype(F32), axis=0) * np.float32(1.0 / np.sqrt(np.float32(MODEL_WIDTH)))
    top, bottom = projected[0:8], projected[8:16]
    raw = jnp.concatenate(
        [top[:, 0:128], top[:, 128:256], top[:, 256:384], bottom[:, 0:128], bottom[:, 128:256]], axis=0
    )
    new_values = bottom[:, 256:384].astype(BF16)
    normed = raw * lax.rsqrt(jnp.mean(raw * raw, axis=1, keepdims=True) + norm_epsilon)
    cosine5 = jnp.concatenate([cosine] * 5, axis=0)
    sine5 = jnp.concatenate([sine] * 5, axis=0)
    rotated = (normed * cosine5 + pltpu.roll(normed, HEAD_SIZE // 2, 1) * sine5).astype(BF16)
    queries = rotated[0:32]
    new_keys = rotated[32:40]

    scale = HEAD_SIZE ** (-0.5)
    contract_last = (((1,), (1,)), ((), ()))
    loads[6].wait()
    loads[7].wait()
    q_token = lax.rem(lax.broadcasted_iota(jnp.int32, (32, TOKENS), 0), 8)
    k_token = lax.broadcasted_iota(jnp.int32, (32, TOKENS), 1)
    recent = lax.dot_general(queries, new_keys, contract_last, preferred_element_type=F32) * scale
    seen = (lax.rem(q_token, 2) == lax.rem(k_token, 2)) & (lax.div(k_token, 2) <= lax.div(q_token, 2))
    recent = jnp.where(seen, jnp.exp(recent), 0.0)
    total = jnp.sum(recent, axis=1, keepdims=True)
    heads = jnp.dot(recent.astype(BF16), new_values, preferred_element_type=F32)
    slot = lax.broadcasted_iota(jnp.int32, (32, CACHE_SLOTS), 1)
    row_of = lax.rem(lax.broadcasted_iota(jnp.int32, (32, CACHE_SLOTS), 0), 2)
    for n in range(2):
        scores = (
            lax.dot_general(queries, keys_v[n * CACHE_SLOTS : (n + 1) * CACHE_SLOTS, :], contract_last, preferred_element_type=F32)
            * scale
        )
        past = jnp.where((slot < lengths[n]) & (row_of == n), jnp.exp(scores), 0.0)
        total = total + jnp.sum(past, axis=1, keepdims=True)
        heads = heads + jnp.dot(
            past.astype(BF16), values_v[n * CACHE_SLOTS : (n + 1) * CACHE_SLOTS, :], preferred_element_type=F32
        )
    heads = (heads / total).astype(BF16)

    os[...] = heads
    orr[0] = heads
    for d in range(1, 4):
        copy = pltpu.make_async_remote_copy(
            src_ref=os, dst_ref=orr.at[d], send_sem=o_send.at[d - 1], recv_sem=o_recv.at[d - 1], device_id=y_peer(d), device_id_type=MESH
        )
        copy.start()
        pending.append(copy.wait_send)
    for k in range(8):
        to_twin[k].wait_recv()
    for d in range(3):
        pltpu.make_async_copy(os, os, o_recv.at[d]).wait()
    wide = orr[...].astype(F32)
    left = jnp.concatenate([wide[:, 8 * h : 8 * h + 8, :].reshape(32, 128) for h in range(4)], axis=1).astype(BF16)
    attn = lax.dot_general(left, wo[...].reshape(16 * ROWS, OUT_COLUMNS), contract_last, preferred_element_type=F32)
    attn = attn * np.float32(1.0 / np.sqrt(np.float32(KEY_VALUE_HEADS * OUT_COLUMNS)))
    attn = attn.reshape(4, 8, 1280)
    s4[...] = jnp.concatenate([attn[:, :, :640], attn[:, :, 640:]], axis=1).astype(BF16)
    for e in range(1, 4):
        copy = pltpu.make_async_remote_copy(
            src_ref=s4.at[lax.rem(xx + e, 4)],
            dst_ref=r4.at[e - 1],
            send_sem=r4_send.at[e - 1],
            recv_sem=r4_recv.at[e - 1],
            device_id=x_peer(e),
            device_id_type=MESH,
        )
        copy.start()
        pending.append(copy.wait_send)
    summed = s4[xx].astype(F32)
    for e in range(3):
        pltpu.make_async_copy(s4.at[0], s4.at[0], r4_recv.at[e]).wait()
        summed = summed + r4[e].astype(F32)
    s5[...] = summed.astype(BF16)
    target_y = lax.rem(y + 4 - xx, 4)

    def to_owner(e):
        there = lax.rem(t + e, 8)
        return pltpu.make_async_remote_copy(
            src_ref=s5,
            dst_ref=r5.at[t],
            send_sem=r5_send.at[e],
            recv_sem=r5_recv,
            device_id=dev(z, target_y, r, there),
            device_id_type=MESH,
        )

    def own_copy():
        return pltpu.make_async_copy(s5, r5.at[t], r5_recv)

    for e in range(1, 8):
        to_owner(e).start()
        pending.append(to_owner(e).wait_send)
    pending.append(lambda: pl.when(xx != 0)(to_owner(0).wait_send))

    @pl.when(xx != 0)
    def _():
        to_owner(0).start()

    @pl.when(xx == 0)
    def _():
        own_copy().start()

    pltpu.make_async_copy(r5, r5, r5_recv).wait()

    squares = jnp.zeros((TOKENS, 128), F32)
    for xs_ in range(4):
        both = r5[2 * xs_].astype(F32) + r5[2 * xs_ + 1].astype(F32)
        for b in range(8):
            block = widen(both[:, b * ROWS : (b + 1) * ROWS])
            for half in range(2):
                place = xs_ * 16 + half * 8 + b
                residual = block[half * 8 : half * 8 + 8] + xperm[place]
                zblk[place] = residual
                squares = squares + residual * residual
    rscale = lax.rsqrt(jnp.sum(squares, axis=1, keepdims=True) * np.float32(1.0 / MODEL_WIDTH) + norm_epsilon)
    pieces = []
    for i in range(8):
        j = stored[i]
        k = lax.rem(z + 8 - lax.div(j, 8), 8)
        source = lax.rem(lax.rem(lax.div(j, 2), 4) + 4 - y, 4)
        rr = lax.rem(lax.rem(j, 2) + r, 2)
        pieces.append(zblk[source * 16 + k * 2 + rr][:, :ROWS])
    mixed_out[...] = (jnp.concatenate(pieces, axis=1) * rscale * post_v[...].reshape(1, 640)).astype(BF16)

    for wait in pending:
        wait()


def body(
    master, adam_first_moment, adam_second_moment, gradient, resync_order, inputs, in_gain, post_gain, lengths,
    cached_key_rows, cached_value_rows,
):
    half = np.arange(HEAD_SIZE // 2, dtype=np.float64)
    freqs = (rope_theta ** (-(half * 2.0 / HEAD_SIZE))).astype(np.float32)
    freqs = jnp.asarray(np.concatenate([freqs, freqs])[None, :])
    vmem = pl.BlockSpec(memory_space=pltpu.VMEM)
    hbm = pl.BlockSpec(memory_space=pltpu.HBM)
    dma = pltpu.SemaphoreType.DMA
    flat = (ROWS * 10, 128)
    new_master, mixed = pl.pallas_call(
        kernel,
        out_shape=(jax.ShapeDtypeStruct(flat, F32), jax.ShapeDtypeStruct((TOKENS, 640), BF16)),
        in_specs=[hbm] * 12,
        out_specs=(hbm, vmem),
        scratch_shapes=[
            pltpu.SMEM((BLOCKS,), jnp.int32),
            pltpu.SMEM((2,), jnp.int32),
            pltpu.VMEM((640,), F32),
            pltpu.VMEM((1, HEAD_SIZE), F32),
            pltpu.VMEM((STEPS, 2, MODEL_WIDTH), BF16),
            pltpu.VMEM((1, MODEL_WIDTH), F32),
            pltpu.VMEM((TOKENS, MODEL_WIDTH), F32),
            pltpu.VMEM((BLOCKS, TOKENS, 128), F32),
            pltpu.VMEM((BLOCKS, TOKENS, 128), F32),
            pltpu.VMEM((BLOCKS, TOKENS, 128), F32),
            pltpu.VMEM((BLOCKS, TOKENS, 128), F32),
            pltpu.VMEM(flat, F32),
            pltpu.VMEM(flat, F32),
            pltpu.VMEM(flat, F32),
            pltpu.VMEM((ROWS, 1280), BF16),
            pltpu.VMEM((2 * CACHE_SLOTS, HEAD_SIZE), BF16),
            pltpu.VMEM((2 * CACHE_SLOTS, HEAD_SIZE), BF16),
            pltpu.VMEM((QPEERS, 32, 128), BF16),
            pltpu.VMEM((QPEERS, 32, 128), BF16),
            pltpu.VMEM((4, 128, IN_COLUMNS), BF16),
            pltpu.VMEM((8, 2, ROWS, OUT_COLUMNS), BF16),
            pltpu.VMEM((QPEERS, 16, 384), BF16),
            pltpu.VMEM((QPEERS, 16, 384), BF16),
            pltpu.VMEM((32, 128), BF16),
            pltpu.VMEM((4, 32, 128), BF16),
            pltpu.VMEM((4, 16, 640), BF16),
            pltpu.VMEM((3, 16, 640), BF16),
            pltpu.VMEM((16, 640), BF16),
            pltpu.VMEM((8, 16, 640), BF16),
            dma((12,)), dma, dma, dma, dma((3,)), dma((3,)), dma((7,)), dma((7,)), dma((8,)), dma((8,)),
            dma, dma, dma((3,)), dma((3,)), dma((3,)), dma((3,)), dma((8,)), dma, dma,
        ],
        compiler_params=pltpu.CompilerParams(collective_id=0, has_side_effects=True, vmem_limit_bytes=56 << 20),
        cost_estimate=pl.CostEstimate(flops=400_000_000, bytes_accessed=4_500_000, transcendentals=200_000),
        name="adam_attention",
    )(
        resync_order, lengths, inputs, in_gain.reshape(1, MODEL_WIDTH), post_gain, freqs,
        master.reshape(flat), adam_first_moment.reshape(flat), adam_second_moment.reshape(flat), gradient.reshape(ROWS, 1280),
        cached_key_rows.reshape(2 * CACHE_SLOTS, HEAD_SIZE), cached_value_rows.reshape(2 * CACHE_SLOTS, HEAD_SIZE),
    )
    return new_master.reshape(ROWS, 1, 1280), mixed.reshape(STEPS, 2, 640)


def solution(mesh):
    in_specs = (
        P(("learn", "rep"), "tp", None),
        P(("learn", "rep"), "tp", None),
        P(("learn", "rep"), "tp", None),
        P(("learn", "rep"), "tp", None),
        P(),
        P(None, ("learn", "rep"), None),
        P(),
        P("tp"),
        P(("learn", "rep")),
        P(("learn", "rep"), "tp", None, None),
        P(("learn", "rep"), "tp", None, None),
    )
    out_specs = (P(("learn", "rep"), "tp", None), P(None, ("learn", "rep"), "tp"))
    return jax.shard_map(body, mesh=mesh, in_specs=in_specs, out_specs=out_specs, check_vma=False)
```

```python
import functools

import jax
import jax.numpy as jnp
import numpy as np
from jax import lax
from jax.experimental import pallas as pl
from jax.experimental.pallas import tpu as pltpu
from jax.sharding import PartitionSpec as P

MODEL_WIDTH = 5120
HEAD_SIZE = 128
KEY_VALUE_HEADS = 8
QUERY_PER_GROUP = 4
STEPS = 4
CACHE_SLOTS = 2048
BLOCKS = 64
ROWS = 80
IN_COLUMNS = 768
OUT_COLUMNS = 512
TOKENS = 8
QPEERS = 16

beta_one = 0.9
beta_two = 0.95
adam_rate = 0.05
adam_decay = 0.1
adam_epsilon = 1e-08
correction_one = 1.0 - 0.9**10
correction_two = 1.0 - 0.95**10
norm_epsilon = 1e-06
rope_theta = 1000000.0

MESH = pl.DeviceIdType.MESH
F32 = jnp.float32
BF16 = jnp.bfloat16


def adam_update(master, first, second, gradient):
    first_moment = beta_one * first + (1.0 - beta_one) * gradient
    second_moment = beta_two * second + (1.0 - beta_two) * gradient * gradient
    update = (
        first_moment / correction_one / (jnp.sqrt(second_moment / correction_two) + adam_epsilon)
        + adam_decay * master
    )
    return master - adam_rate * update


def widen(block):
    return jnp.concatenate([block, jnp.zeros((block.shape[0], 128 - ROWS), block.dtype)], axis=1)


def kernel(
    order_in, lengths_in, x_in, gain_in, post_in, freq_in, master_in, first_in, second_in, gradient_in, keys_in, values_in,
    master_out, mixed_out,
    order, lengths, post_v, freq_v, x_v, gain_v, xs, qh, hh, xblk, hblk, xperm, zblk, master_v, first_v, second_v, gradient_v, keys_v, values_v,
    hs, hr, wq, wo, ps, pr, os, orr, s4, r4, s5, r5,
    load_sem, h_send, h_recv, wq_send, wq_recv, ring_send, ring_recv, twin_send, twin_recv,
    p_send, p_recv, o_send, o_recv, r4_send, r4_recv, r5_send, r5_self, r5_recv,
):
    l, r, t = lax.axis_index("learn"), lax.axis_index("rep"), lax.axis_index("tp")
    z, y = lax.div(l, 4), lax.rem(l, 4)
    yp, yy = lax.div(y, 2), lax.rem(y, 2)
    c = z * 2 + yp
    xx, yh = lax.div(t, 2), lax.rem(t, 2)

    def dev(z, y, r, t):
        return {"learn": z * 4 + y, "rep": r, "tp": t}

    def q_peer(d):
        other = lax.rem(c + d, QPEERS)
        return dev(lax.div(other, 2), lax.rem(other, 2) * 2 + yy, r, t)

    twin = dev(z, y, 1 - r, t)
    partner = dev(z, yp * 2 + 1 - yy, r, t)
    above = dev(lax.rem(z + 1, 8), y, r, t)
    below = dev(lax.rem(z + 7, 8), y, r, t)

    def y_peer(d):
        return dev(z, lax.rem(y + d, 4), r, t)

    def x_peer(e):
        return dev(z, y, r, lax.rem(xx + e, 4) * 2 + yh)

    pending = []

    loads = [
        pltpu.make_async_copy(src, dst, load_sem.at[i])
        for i, (src, dst) in enumerate(
            [
                (x_in, x_v), (gain_in, gain_v), (master_in, master_v), (first_in, first_v), (second_in, second_v),
                (gradient_in, gradient_v), (keys_in, keys_v), (values_in, values_v),
                (order_in, order), (lengths_in, lengths), (post_in, post_v), (freq_in, freq_v),
            ]
        )
    ]
    for load in loads:
        load.start()

    barrier = pltpu.get_barrier_semaphore()

    def greet(device):
        pl.semaphore_signal(barrier, inc=1, device_id=device, device_id_type=MESH)

    def greet_q(d, carry):
        greet(q_peer(d))
        return carry

    lax.fori_loop(1, QPEERS, greet_q, 0)
    for device in (twin, partner, above, below):
        greet(device)
    for d in range(1, 4):
        greet(y_peer(d))
        greet(x_peer(d))
    for e in range(8):
        there = lax.rem(t + e, 8)
        device = dev(z, lax.rem(y + lax.div(there, 2), 4), r, there)
        if e == 0:
            pl.when(xx != 0)(functools.partial(greet, device))
        else:
            greet(device)
    greetings = (QPEERS - 1) + 4 + 6 + 7 + jnp.where(xx != 0, 1, 0)

    loads[0].wait()
    loads[1].wait()
    loads[8].wait()
    for s in range(STEPS):
        xs[2 * s : 2 * s + 2, :] = x_v[s].astype(F32)
    stream = xs[...]
    rscale = lax.rsqrt(jnp.mean(stream * stream, axis=1, keepdims=True) + norm_epsilon)
    for b in range(BLOCKS):
        block = xs[:, b * ROWS : (b + 1) * ROWS]
        xblk[b] = widen(block)
        hblk[b] = widen(block * rscale * gain_v[:, b * ROWS : (b + 1) * ROWS])
    for d in range(QPEERS):
        other = lax.rem(c + d, QPEERS)
        parts = []
        for m in range(4):
            my, mr = m // 2, m % 2
            w = lax.rem(yy + my, 2) * 2 + lax.rem(r + mr, 2)
            parts.append(hblk[order[other * 4 + w]])
        piece = jnp.concatenate(parts, axis=0).astype(BF16)
        if d == 0:
            hr[0] = piece
        else:
            hs[d] = piece

    wq[:, ROWS:, :] = jnp.zeros((4, 128 - ROWS, IN_COLUMNS), BF16)
    for i in range(2, 6):
        loads[i].wait()
    for j in range(10):
        rows = pl.ds(j, ROWS, stride=10)
        fresh = adam_update(
            master_v[rows, :], first_v[rows, :], second_v[rows, :], gradient_v[:, j * 128 : (j + 1) * 128].astype(F32)
        )
        master_out[rows, :] = fresh
        if j < 6:
            wq[0, 0:ROWS, j * 128 : (j + 1) * 128] = fresh.astype(BF16)
        else:
            wo[0, 0, :, (j - 6) * 128 : (j - 5) * 128] = fresh.astype(BF16)

    pl.semaphore_wait(barrier, greetings)

    def far_first(i):
        return QPEERS // 2 + jnp.where(lax.rem(i, 2) == 1, lax.div(i + 1, 2), -lax.div(i, 2))

    def send_h(i, carry):
        d = far_first(i)
        pltpu.make_async_remote_copy(
            src_ref=hs.at[d], dst_ref=hr.at[d], send_sem=h_send, recv_sem=h_recv, device_id=q_peer(d), device_id_type=MESH
        ).start()
        return carry

    lax.fori_loop(0, QPEERS - 1, send_h, 0)
    pending.append(pltpu.make_async_copy(hs.at[pl.ds(1, QPEERS - 1)], hs.at[pl.ds(1, QPEERS - 1)], h_send).wait)

    def share(src, dst, device):
        return pltpu.make_async_remote_copy(
            src_ref=wq.at[src, pl.ds(0, ROWS)],
            dst_ref=wq.at[dst, pl.ds(0, ROWS)],
            send_sem=wq_send.at[dst - 1],
            recv_sem=wq_recv.at[dst - 1],
            device_id=device,
            device_id_type=MESH,
        )

    shares = [share(0, 1, twin), share(0, 2, partner), share(2, 3, twin)]
    pending.extend(copy.wait_send for copy in shares)
    shares[1].start()
    shares[0].start()

    def ring(src, dst, index, device):
        return pltpu.make_async_remote_copy(
            src_ref=wo.at[src, 0],
            dst_ref=wo.at[dst, 0],
            send_sem=ring_send.at[index],
            recv_sem=ring_recv.at[index],
            device_id=device,
            device_id_type=MESH,
        )

    up = [ring(k, k + 1, k, above) for k in range(4)]
    down = [ring((8 - k) % 8, 7 - k, 4 + k, below) for k in range(3)]
    to_twin = [
        pltpu.make_async_remote_copy(
            src_ref=wo.at[k, 0],
            dst_ref=wo.at[k, 1],
            send_sem=twin_send.at[k],
            recv_sem=twin_recv.at[k],
            device_id=twin,
            device_id_type=MESH,
        )
        for k in range(8)
    ]
    pending.extend(copy.wait_send for copy in up + down + to_twin)
    ring_step = [0]

    def ring_advance():
        ring_step[0] += 1
        k = ring_step[0]
        up[k - 1].wait_recv()
        if k < 4:
            up[k].start()
            down[k - 1].wait_recv()
            if k < 3:
                down[k].start()
            to_twin[8 - k].start()
        to_twin[k].start()

    up[0].start()
    down[0].start()
    to_twin[0].start()

    loads[9].wait()
    loads[10].wait()
    loads[11].wait()
    token = lax.broadcasted_iota(jnp.int32, (TOKENS, HEAD_SIZE), 0)
    lane = lax.broadcasted_iota(jnp.int32, (TOKENS, HEAD_SIZE), 1)
    positions = jnp.where(lax.rem(token, 2) == 0, lengths[0], lengths[1]) + lax.div(token, 2)
    angles = positions.astype(F32) * freq_v[...]
    cosine = jnp.cos(angles)
    sine = jnp.sin(angles)
    sine = jnp.where(lane < HEAD_SIZE // 2, -sine, sine)

    def find(j, carry):
        actor = order[j] - t * 8
        return tuple(jnp.where(actor == i, j, carry[i]) for i in range(8))

    stored = lax.fori_loop(0, BLOCKS, find, tuple(jnp.int32(0) for _ in range(8)))
    for xs_ in range(4):
        source_y = lax.rem(y + xs_, 4)
        for k in range(8):
            for rr in range(2):
                j = (lax.rem(z + 8 - k, 8) * 4 + source_y) * 2 + lax.rem(r + rr, 2)
                xperm[xs_ * 16 + k * 2 + rr] = xblk[order[j]]

    shares[1].wait_recv()
    shares[2].start()

    pltpu.make_async_copy(hr.at[pl.ds(1, QPEERS - 1)], hr.at[pl.ds(1, QPEERS - 1)], h_recv).wait()
    ring_advance()
    wide = hr[...].astype(F32)
    left = jnp.concatenate([wide[:, 8 * m : 8 * m + 8, :].reshape(QPEERS * TOKENS, 128) for m in range(4)], axis=1).astype(BF16)
    shares[0].wait_recv()
    shares[2].wait_recv()
    partial = jnp.dot(left, wq[...].reshape(512, IN_COLUMNS), preferred_element_type=F32).reshape(QPEERS, TOKENS, IN_COLUMNS)
    packed = jnp.concatenate([partial[:, :, :384], partial[:, :, 384:]], axis=1).astype(BF16)
    pr[0] = packed[0]
    ps[...] = packed

    def send_p(i, carry):
        d = far_first(i)
        pltpu.make_async_remote_copy(
            src_ref=ps.at[d],
            dst_ref=pr.at[d],
            send_sem=p_send,
            recv_sem=p_recv,
            device_id=q_peer(QPEERS - d),
            device_id_type=MESH,
        ).start()
        return carry

    lax.fori_loop(0, QPEERS - 1, send_p, 0)
    pending.append(pltpu.make_async_copy(ps.at[pl.ds(1, QPEERS - 1)], ps.at[pl.ds(1, QPEERS - 1)], p_send).wait)
    ring_advance()
    ring_advance()
    pltpu.make_async_copy(pr.at[pl.ds(1, QPEERS - 1)], pr.at[pl.ds(1, QPEERS - 1)], p_recv).wait()
    projected = jnp.sum(pr[...].astype(F32), axis=0) * np.float32(1.0 / np.sqrt(np.float32(MODEL_WIDTH)))
    top, bottom = projected[0:8], projected[8:16]
    raw = jnp.concatenate(
        [top[:, 0:128], top[:, 128:256], top[:, 256:384], bottom[:, 0:128], bottom[:, 128:256]], axis=0
    )
    new_values = bottom[:, 256:384].astype(BF16)
    normed = raw * lax.rsqrt(jnp.mean(raw * raw, axis=1, keepdims=True) + norm_epsilon)
    cosine5 = jnp.concatenate([cosine] * 5, axis=0)
    sine5 = jnp.concatenate([sine] * 5, axis=0)
    rotated = normed * cosine5 + pltpu.roll(normed, HEAD_SIZE // 2, 1) * sine5
    qh[...] = rotated[0:32]
    new_keys = rotated[32:40].astype(BF16)

    scale = HEAD_SIZE ** (-0.5)
    contract_last = (((1,), (1,)), ((), ()))
    q_step = lax.rem(lax.broadcasted_iota(jnp.int32, (16, TOKENS), 0), STEPS)
    k_token = lax.broadcasted_iota(jnp.int32, (16, TOKENS), 1)
    slot = lax.broadcasted_iota(jnp.int32, (16, CACHE_SLOTS), 1)
    loads[6].wait()
    loads[7].wait()
    for n in range(2):
        rows = pl.ds(n, 16, stride=2)
        queries = qh[rows, :].astype(BF16)
        recent = lax.dot_general(queries, new_keys, contract_last, preferred_element_type=F32) * scale
        seen = (lax.rem(k_token, 2) == n) & (lax.div(k_token, 2) <= q_step)
        recent = jnp.where(seen, jnp.exp(recent), 0.0)
        scores = (
            lax.dot_general(queries, keys_v[n * CACHE_SLOTS : (n + 1) * CACHE_SLOTS, :], contract_last, preferred_element_type=F32)
            * scale
        )
        past = jnp.where(slot < lengths[n], jnp.exp(scores), 0.0)
        total = jnp.sum(past, axis=1, keepdims=True) + jnp.sum(recent, axis=1, keepdims=True)
        heads = jnp.dot(
            past.astype(BF16), values_v[n * CACHE_SLOTS : (n + 1) * CACHE_SLOTS, :], preferred_element_type=F32
        ) + jnp.dot(recent.astype(BF16), new_values, preferred_element_type=F32)
        hh[rows, :] = heads / total
    heads = hh[...].astype(BF16)

    os[...] = heads
    orr[0] = heads
    for d in (2, 1, 3):
        copy = pltpu.make_async_remote_copy(
            src_ref=os, dst_ref=orr.at[d], send_sem=o_send.at[d - 1], recv_sem=o_recv.at[d - 1], device_id=y_peer(d), device_id_type=MESH
        )
        copy.start()
        pending.append(copy.wait_send)
    ring_advance()
    for k in range(8):
        to_twin[k].wait_recv()
    for d in range(3):
        pltpu.make_async_copy(os, os, o_recv.at[d]).wait()
    wide = orr[...].astype(F32)
    left = jnp.concatenate([wide[:, 8 * h : 8 * h + 8, :].reshape(32, 128) for h in range(4)], axis=1).astype(BF16)
    attn = lax.dot_general(left, wo[...].reshape(16 * ROWS, OUT_COLUMNS), contract_last, preferred_element_type=F32)
    attn = attn * np.float32(1.0 / np.sqrt(np.float32(KEY_VALUE_HEADS * OUT_COLUMNS)))
    attn = attn.reshape(4, 8, 1280)
    s4[...] = jnp.concatenate([attn[:, :, :640], attn[:, :, 640:]], axis=1).astype(BF16)
    for e in (2, 1, 3):
        copy = pltpu.make_async_remote_copy(
            src_ref=s4.at[lax.rem(xx + e, 4)],
            dst_ref=r4.at[e - 1],
            send_sem=r4_send.at[e - 1],
            recv_sem=r4_recv.at[e - 1],
            device_id=x_peer(e),
            device_id_type=MESH,
        )
        copy.start()
        pending.append(copy.wait_send)
    summed = s4[xx].astype(F32)
    for e in range(3):
        pltpu.make_async_copy(s4.at[0], s4.at[0], r4_recv.at[e]).wait()
        summed = summed + r4[e].astype(F32)
    s5[...] = summed.astype(BF16)
    target_y = lax.rem(y + 4 - xx, 4)

    def to_owner(e):
        there = lax.rem(t + e, 8)
        return pltpu.make_async_remote_copy(
            src_ref=s5,
            dst_ref=r5.at[t],
            send_sem=r5_send.at[e],
            recv_sem=r5_recv,
            device_id=dev(z, target_y, r, there),
            device_id_type=MESH,
        )

    def own_copy():
        return pltpu.make_async_copy(s5, r5.at[t], r5_recv)

    for e in (4, 3, 5, 2, 6, 1, 7):
        to_owner(e).start()
        pending.append(to_owner(e).wait_send)
    pending.append(lambda: pl.when(xx != 0)(to_owner(0).wait_send))

    @pl.when(xx != 0)
    def _():
        to_owner(0).start()

    @pl.when(xx == 0)
    def _():
        own_copy().start()

    pltpu.make_async_copy(r5, r5, r5_recv).wait()

    squares = jnp.zeros((TOKENS, 128), F32)
    for xs_ in range(4):
        both = r5[2 * xs_].astype(F32) + r5[2 * xs_ + 1].astype(F32)
        for b in range(8):
            block = widen(both[:, b * ROWS : (b + 1) * ROWS])
            for half in range(2):
                place = xs_ * 16 + half * 8 + b
                residual = block[half * 8 : half * 8 + 8] + xperm[place]
                zblk[place] = residual
                squares = squares + residual * residual
    rscale = lax.rsqrt(jnp.sum(squares, axis=1, keepdims=True) * np.float32(1.0 / MODEL_WIDTH) + norm_epsilon)
    pieces = []
    for i in range(8):
        j = stored[i]
        k = lax.rem(z + 8 - lax.div(j, 8), 8)
        source = lax.rem(lax.rem(lax.div(j, 2), 4) + 4 - y, 4)
        rr = lax.rem(lax.rem(j, 2) + r, 2)
        pieces.append(zblk[source * 16 + k * 2 + rr][:, :ROWS])
    mixed_out[...] = (jnp.concatenate(pieces, axis=1) * rscale * post_v[...].reshape(1, 640)).astype(BF16)

    for wait in pending:
        wait()


def finish(master_in, mixed_in, master_out, mixed_out, held, sem):
    write_master = pltpu.make_async_copy(master_in, master_out, sem.at[0])
    write_master.start()
    values = mixed_in[...].astype(F32)
    for s in range(STEPS):
        held[s] = values[2 * s : 2 * s + 2].astype(BF16)
    write_mixed = pltpu.make_async_copy(held, mixed_out, sem.at[1])
    write_mixed.start()
    write_mixed.wait()
    write_master.wait()


def body(
    master, adam_first_moment, adam_second_moment, gradient, resync_order, inputs, in_gain, post_gain, lengths,
    cached_key_rows, cached_value_rows,
):
    half = np.arange(HEAD_SIZE // 2, dtype=np.float64)
    freqs = (rope_theta ** (-(half * 2.0 / HEAD_SIZE))).astype(np.float32)
    freqs = jnp.asarray(np.concatenate([freqs, freqs])[None, :])
    vmem = pl.BlockSpec(memory_space=pltpu.VMEM)
    hbm = pl.BlockSpec(memory_space=pltpu.HBM)
    dma = pltpu.SemaphoreType.DMA
    flat = (ROWS * 10, 128)
    new_master, mixed = pl.pallas_call(
        kernel,
        out_shape=(pltpu.VMEM(flat, F32), pltpu.VMEM((TOKENS, 640), BF16)),
        in_specs=[hbm] * 12,
        out_specs=(vmem, vmem),
        scratch_shapes=[
            pltpu.SMEM((BLOCKS,), jnp.int32),
            pltpu.SMEM((2,), jnp.int32),
            pltpu.VMEM((640,), F32),
            pltpu.VMEM((1, HEAD_SIZE), F32),
            pltpu.VMEM((STEPS, 2, MODEL_WIDTH), BF16),
            pltpu.VMEM((1, MODEL_WIDTH), F32),
            pltpu.VMEM((TOKENS, MODEL_WIDTH), F32),
            pltpu.VMEM((32, HEAD_SIZE), F32),
            pltpu.VMEM((32, HEAD_SIZE), F32),
            pltpu.VMEM((BLOCKS, TOKENS, 128), F32),
            pltpu.VMEM((BLOCKS, TOKENS, 128), F32),
            pltpu.VMEM((BLOCKS, TOKENS, 128), F32),
            pltpu.VMEM((BLOCKS, TOKENS, 128), F32),
            pltpu.VMEM(flat, F32),
            pltpu.VMEM(flat, F32),
            pltpu.VMEM(flat, F32),
            pltpu.VMEM((ROWS, 1280), BF16),
            pltpu.VMEM((2 * CACHE_SLOTS, HEAD_SIZE), BF16),
            pltpu.VMEM((2 * CACHE_SLOTS, HEAD_SIZE), BF16),
            pltpu.VMEM((QPEERS, 32, 128), BF16),
            pltpu.VMEM((QPEERS, 32, 128), BF16),
            pltpu.VMEM((4, 128, IN_COLUMNS), BF16),
            pltpu.VMEM((8, 2, ROWS, OUT_COLUMNS), BF16),
            pltpu.VMEM((QPEERS, 16, 384), BF16),
            pltpu.VMEM((QPEERS, 16, 384), BF16),
            pltpu.VMEM((32, 128), BF16),
            pltpu.VMEM((4, 32, 128), BF16),
            pltpu.VMEM((4, 16, 640), BF16),
            pltpu.VMEM((3, 16, 640), BF16),
            pltpu.VMEM((16, 640), BF16),
            pltpu.VMEM((8, 16, 640), BF16),
            dma((12,)), dma, dma, dma((3,)), dma((3,)), dma((7,)), dma((7,)), dma((8,)), dma((8,)),
            dma, dma, dma((3,)), dma((3,)), dma((3,)), dma((3,)), dma((8,)), dma, dma,
        ],
        compiler_params=pltpu.CompilerParams(collective_id=0, has_side_effects=True, vmem_limit_bytes=56 << 20),
        cost_estimate=pl.CostEstimate(flops=400_000_000, bytes_accessed=4_500_000, transcendentals=200_000),
        name="adam_attention",
    )(
        resync_order, lengths, inputs, in_gain.reshape(1, MODEL_WIDTH), post_gain, freqs,
        master.reshape(flat), adam_first_moment.reshape(flat), adam_second_moment.reshape(flat), gradient.reshape(ROWS, 1280),
        cached_key_rows.reshape(2 * CACHE_SLOTS, HEAD_SIZE), cached_value_rows.reshape(2 * CACHE_SLOTS, HEAD_SIZE),
    )
    new_master, mixed = pl.pallas_call(
        finish,
        out_shape=(jax.ShapeDtypeStruct(flat, F32), jax.ShapeDtypeStruct((STEPS, 2, 640), BF16)),
        in_specs=[vmem, vmem],
        out_specs=(hbm, hbm),
        scratch_shapes=[pltpu.VMEM((STEPS, 2, 640), BF16), dma((2,))],
        name="finish",
    )(new_master, mixed)
    return new_master.reshape(ROWS, 1, 1280), mixed


def solution(mesh):
    in_specs = (
        P(("learn", "rep"), "tp", None),
        P(("learn", "rep"), "tp", None),
        P(("learn", "rep"), "tp", None),
        P(("learn", "rep"), "tp", None),
        P(),
        P(None, ("learn", "rep"), None),
        P(),
        P("tp"),
        P(("learn", "rep")),
        P(("learn", "rep"), "tp", None, None),
        P(("learn", "rep"), "tp", None, None),
    )
    out_specs = (P(("learn", "rep"), "tp", None), P(None, ("learn", "rep"), "tp"))
    return jax.shard_map(body, mesh=mesh, in_specs=in_specs, out_specs=out_specs, check_vma=False)
```

```python
import functools

import jax
import jax.numpy as jnp
import numpy as np
from jax import lax
from jax.experimental import pallas as pl
from jax.experimental.pallas import tpu as pltpu
from jax.sharding import PartitionSpec as P

MODEL_WIDTH = 5120
HEAD_SIZE = 128
KEY_VALUE_HEADS = 8
QUERY_PER_GROUP = 4
STEPS = 4
CACHE_SLOTS = 2048
BLOCKS = 64
ROWS = 80
IN_COLUMNS = 768
OUT_COLUMNS = 512
TOKENS = 8
QPEERS = 16

beta_one = 0.9
beta_two = 0.95
adam_rate = 0.05
adam_decay = 0.1
adam_epsilon = 1e-08
correction_one = 1.0 - 0.9**10
correction_two = 1.0 - 0.95**10
norm_epsilon = 1e-06
rope_theta = 1000000.0

MESH = pl.DeviceIdType.MESH
F32 = jnp.float32
BF16 = jnp.bfloat16


def adam_update(master, first, second, gradient):
    first_moment = beta_one * first + (1.0 - beta_one) * gradient
    second_moment = beta_two * second + (1.0 - beta_two) * gradient * gradient
    update = (
        first_moment / correction_one / (jnp.sqrt(second_moment / correction_two) + adam_epsilon)
        + adam_decay * master
    )
    return master - adam_rate * update


def widen(block):
    return jnp.concatenate([block, jnp.zeros((block.shape[0], 128 - ROWS), block.dtype)], axis=1)


def kernel(
    order_in, lengths_in, x_in, gain_in, post_in, freq_in, master_in, first_in, second_in, gradient_in, keys_in, values_in,
    master_out, mixed_out,
    order, lengths, post_v, freq_v, x_v, gain_v, xs, qh, hh, xblk, hblk, xperm, zblk, master_v, first_v, second_v, gradient_v, keys_v, values_v,
    hs, hr, wq, wo, ps, pr, os, orr, s4, r4, s5, r5,
    load_sem, h_send, h_recv, wq_send, wq_recv, ring_send, ring_recv, twin_send, twin_recv,
    p_send, p_recv, o_send, o_recv, r4_send, r4_recv, r5_send, r5_self, r5_recv,
):
    l, r, t = lax.axis_index("learn"), lax.axis_index("rep"), lax.axis_index("tp")
    z, y = lax.div(l, 4), lax.rem(l, 4)
    yp, yy = lax.div(y, 2), lax.rem(y, 2)
    c = z * 2 + yp
    xx, yh = lax.div(t, 2), lax.rem(t, 2)

    def dev(z, y, r, t):
        return {"learn": z * 4 + y, "rep": r, "tp": t}

    def q_peer(d):
        other = lax.rem(c + d, QPEERS)
        return dev(lax.div(other, 2), lax.rem(other, 2) * 2 + yy, r, t)

    twin = dev(z, y, 1 - r, t)
    partner = dev(z, yp * 2 + 1 - yy, r, t)
    above = dev(lax.rem(z + 1, 8), y, r, t)
    below = dev(lax.rem(z + 7, 8), y, r, t)

    def y_peer(d):
        return dev(z, lax.rem(y + d, 4), r, t)

    def x_peer(e):
        return dev(z, y, r, lax.rem(xx + e, 4) * 2 + yh)

    pending = []

    loads = [
        pltpu.make_async_copy(src, dst, load_sem.at[i])
        for i, (src, dst) in enumerate(
            [
                (x_in, x_v), (gain_in, gain_v), (master_in, master_v), (first_in, first_v), (second_in, second_v),
                (gradient_in, gradient_v), (keys_in, keys_v), (values_in, values_v),
                (order_in, order), (lengths_in, lengths), (post_in, post_v), (freq_in, freq_v),
            ]
        )
    ]
    for i in (0, 1, 8):
        loads[i].start()

    barrier = pltpu.get_barrier_semaphore()

    def greet(device):
        pl.semaphore_signal(barrier, inc=1, device_id=device, device_id_type=MESH)

    def far_first(i):
        return QPEERS // 2 + jnp.where(lax.rem(i, 2) == 1, lax.div(i + 1, 2), -lax.div(i, 2))

    def greet_q(i, carry):
        greet(q_peer(far_first(i)))
        return carry

    lax.fori_loop(0, QPEERS - 1, greet_q, 0)
    for e in (4, 3, 5, 2, 6, 1, 7, 0):
        there = lax.rem(t + e, 8)
        device = dev(z, lax.rem(y + lax.div(there, 2), 4), r, there)
        if e == 0:
            pl.when(xx != 0)(functools.partial(greet, device))
        else:
            greet(device)
    for d in (2, 1, 3):
        greet(y_peer(d))
        greet(x_peer(d))
    for device in (partner, above, below, twin):
        greet(device)
    for i in (2, 3, 4, 5, 6, 7, 9, 10, 11):
        loads[i].start()
    greetings = (QPEERS - 1) + 4 + 6 + 7 + jnp.where(xx != 0, 1, 0)

    loads[0].wait()
    loads[1].wait()
    loads[8].wait()
    for s in range(STEPS):
        xs[2 * s : 2 * s + 2, :] = x_v[s].astype(F32)
    stream = xs[...]
    rscale = lax.rsqrt(jnp.mean(stream * stream, axis=1, keepdims=True) + norm_epsilon)
    for b in range(BLOCKS):
        block = xs[:, b * ROWS : (b + 1) * ROWS]
        xblk[b] = widen(block)
        hblk[b] = widen(block * rscale * gain_v[:, b * ROWS : (b + 1) * ROWS])
    for d in range(QPEERS):
        other = lax.rem(c + d, QPEERS)
        parts = []
        for m in range(4):
            my, mr = m // 2, m % 2
            w = lax.rem(yy + my, 2) * 2 + lax.rem(r + mr, 2)
            parts.append(hblk[order[other * 4 + w]])
        piece = jnp.concatenate(parts, axis=0).astype(BF16)
        if d == 0:
            hr[0] = piece
        else:
            hs[d] = piece

    wq[:, ROWS:, :] = jnp.zeros((4, 128 - ROWS, IN_COLUMNS), BF16)
    for i in range(2, 6):
        loads[i].wait()
    for j in range(10):
        rows = pl.ds(j, ROWS, stride=10)
        fresh = adam_update(
            master_v[rows, :], first_v[rows, :], second_v[rows, :], gradient_v[:, j * 128 : (j + 1) * 128].astype(F32)
        )
        master_out[rows, :] = fresh
        if j < 6:
            wq[0, 0:ROWS, j * 128 : (j + 1) * 128] = fresh.astype(BF16)
        else:
            wo[0, 0, :, (j - 6) * 128 : (j - 5) * 128] = fresh.astype(BF16)

    pl.semaphore_wait(barrier, greetings)

    def send_h(i, carry):
        d = far_first(i)
        pltpu.make_async_remote_copy(
            src_ref=hs.at[d], dst_ref=hr.at[d], send_sem=h_send, recv_sem=h_recv, device_id=q_peer(d), device_id_type=MESH
        ).start()
        return carry

    lax.fori_loop(0, QPEERS - 1, send_h, 0)
    pending.append(pltpu.make_async_copy(hs.at[pl.ds(1, QPEERS - 1)], hs.at[pl.ds(1, QPEERS - 1)], h_send).wait)

    def share(src, dst, device):
        return pltpu.make_async_remote_copy(
            src_ref=wq.at[src, pl.ds(0, ROWS)],
            dst_ref=wq.at[dst, pl.ds(0, ROWS)],
            send_sem=wq_send.at[dst - 1],
            recv_sem=wq_recv.at[dst - 1],
            device_id=device,
            device_id_type=MESH,
        )

    shares = [share(0, 1, twin), share(0, 2, partner), share(2, 3, twin)]
    pending.extend(copy.wait_send for copy in shares)
    shares[1].start()
    shares[0].start()

    def ring(src, dst, index, device):
        return pltpu.make_async_remote_copy(
            src_ref=wo.at[src, 0],
            dst_ref=wo.at[dst, 0],
            send_sem=ring_send.at[index],
            recv_sem=ring_recv.at[index],
            device_id=device,
            device_id_type=MESH,
        )

    up = [ring(k, k + 1, k, above) for k in range(4)]
    down = [ring((8 - k) % 8, 7 - k, 4 + k, below) for k in range(3)]
    to_twin = [
        pltpu.make_async_remote_copy(
            src_ref=wo.at[k, 0],
            dst_ref=wo.at[k, 1],
            send_sem=twin_send.at[k],
            recv_sem=twin_recv.at[k],
            device_id=twin,
            device_id_type=MESH,
        )
        for k in range(8)
    ]
    pending.extend(copy.wait_send for copy in up + down + to_twin)
    ring_step = [0]

    def ring_advance():
        ring_step[0] += 1
        k = ring_step[0]
        up[k - 1].wait_recv()
        if k < 4:
            up[k].start()
            down[k - 1].wait_recv()
            if k < 3:
                down[k].start()
            to_twin[8 - k].start()
        to_twin[k].start()

    up[0].start()
    down[0].start()
    to_twin[0].start()

    loads[9].wait()
    loads[10].wait()
    loads[11].wait()
    token = lax.broadcasted_iota(jnp.int32, (TOKENS, HEAD_SIZE), 0)
    lane = lax.broadcasted_iota(jnp.int32, (TOKENS, HEAD_SIZE), 1)
    positions = jnp.where(lax.rem(token, 2) == 0, lengths[0], lengths[1]) + lax.div(token, 2)
    angles = positions.astype(F32) * freq_v[...]
    cosine = jnp.cos(angles)
    sine = jnp.sin(angles)
    sine = jnp.where(lane < HEAD_SIZE // 2, -sine, sine)

    def find(j, carry):
        actor = order[j] - t * 8
        return tuple(jnp.where(actor == i, j, carry[i]) for i in range(8))

    stored = lax.fori_loop(0, BLOCKS, find, tuple(jnp.int32(0) for _ in range(8)))
    for xs_ in range(4):
        source_y = lax.rem(y + xs_, 4)
        for k in range(8):
            for rr in range(2):
                j = (lax.rem(z + 8 - k, 8) * 4 + source_y) * 2 + lax.rem(r + rr, 2)
                xperm[xs_ * 16 + k * 2 + rr] = xblk[order[j]]

    shares[1].wait_recv()
    shares[2].start()

    ring_advance()
    pltpu.make_async_copy(hr.at[pl.ds(1, QPEERS - 1)], hr.at[pl.ds(1, QPEERS - 1)], h_recv).wait()
    wide = hr[...].astype(F32)
    left = jnp.concatenate([wide[:, 8 * m : 8 * m + 8, :].reshape(QPEERS * TOKENS, 128) for m in range(4)], axis=1).astype(BF16)
    shares[0].wait_recv()
    shares[2].wait_recv()
    partial = jnp.dot(left, wq[...].reshape(512, IN_COLUMNS), preferred_element_type=F32).reshape(QPEERS, TOKENS, IN_COLUMNS)
    packed = jnp.concatenate([partial[:, :, :384], partial[:, :, 384:]], axis=1).astype(BF16)
    pr[0] = packed[0]
    ps[...] = packed

    def send_p(i, carry):
        d = far_first(i)
        pltpu.make_async_remote_copy(
            src_ref=ps.at[d],
            dst_ref=pr.at[d],
            send_sem=p_send,
            recv_sem=p_recv,
            device_id=q_peer(QPEERS - d),
            device_id_type=MESH,
        ).start()
        return carry

    lax.fori_loop(0, QPEERS - 1, send_p, 0)
    pending.append(pltpu.make_async_copy(ps.at[pl.ds(1, QPEERS - 1)], ps.at[pl.ds(1, QPEERS - 1)], p_send).wait)
    ring_advance()
    ring_advance()
    pltpu.make_async_copy(pr.at[pl.ds(1, QPEERS - 1)], pr.at[pl.ds(1, QPEERS - 1)], p_recv).wait()
    projected = jnp.sum(pr[...].astype(F32), axis=0) * np.float32(1.0 / np.sqrt(np.float32(MODEL_WIDTH)))
    top, bottom = projected[0:8], projected[8:16]
    raw = jnp.concatenate(
        [top[:, 0:128], top[:, 128:256], top[:, 256:384], bottom[:, 0:128], bottom[:, 128:256]], axis=0
    )
    new_values = bottom[:, 256:384].astype(BF16)
    normed = raw * lax.rsqrt(jnp.mean(raw * raw, axis=1, keepdims=True) + norm_epsilon)
    cosine5 = jnp.concatenate([cosine] * 5, axis=0)
    sine5 = jnp.concatenate([sine] * 5, axis=0)
    rotated = normed * cosine5 + pltpu.roll(normed, HEAD_SIZE // 2, 1) * sine5
    qh[...] = rotated[0:32]
    new_keys = rotated[32:40].astype(BF16)

    scale = HEAD_SIZE ** (-0.5)
    contract_last = (((1,), (1,)), ((), ()))
    q_step = lax.rem(lax.broadcasted_iota(jnp.int32, (16, TOKENS), 0), STEPS)
    k_token = lax.broadcasted_iota(jnp.int32, (16, TOKENS), 1)
    slot = lax.broadcasted_iota(jnp.int32, (16, CACHE_SLOTS), 1)
    loads[6].wait()
    loads[7].wait()
    for n in range(2):
        rows = pl.ds(n, 16, stride=2)
        queries = qh[rows, :].astype(BF16)
        recent = lax.dot_general(queries, new_keys, contract_last, preferred_element_type=F32) * scale
        seen = (lax.rem(k_token, 2) == n) & (lax.div(k_token, 2) <= q_step)
        recent = jnp.where(seen, jnp.exp(recent), 0.0)
        scores = (
            lax.dot_general(queries, keys_v[n * CACHE_SLOTS : (n + 1) * CACHE_SLOTS, :], contract_last, preferred_element_type=F32)
            * scale
        )
        past = jnp.where(slot < lengths[n], jnp.exp(scores), 0.0)
        total = jnp.sum(past, axis=1, keepdims=True) + jnp.sum(recent, axis=1, keepdims=True)
        heads = jnp.dot(
            past.astype(BF16), values_v[n * CACHE_SLOTS : (n + 1) * CACHE_SLOTS, :], preferred_element_type=F32
        ) + jnp.dot(recent.astype(BF16), new_values, preferred_element_type=F32)
        hh[rows, :] = heads / total
    heads = hh[...].astype(BF16)

    os[...] = heads
    orr[0] = heads
    for d in (2, 1, 3):
        copy = pltpu.make_async_remote_copy(
            src_ref=os, dst_ref=orr.at[d], send_sem=o_send.at[d - 1], recv_sem=o_recv.at[d - 1], device_id=y_peer(d), device_id_type=MESH
        )
        copy.start()
        pending.append(copy.wait_send)
    ring_advance()
    for k in range(8):
        to_twin[k].wait_recv()
    for d in range(3):
        pltpu.make_async_copy(os, os, o_recv.at[d]).wait()
    wide = orr[...].astype(F32)
    left = jnp.concatenate([wide[:, 8 * h : 8 * h + 8, :].reshape(32, 128) for h in range(4)], axis=1).astype(BF16)
    attn = lax.dot_general(left, wo[...].reshape(16 * ROWS, OUT_COLUMNS), contract_last, preferred_element_type=F32)
    attn = attn * np.float32(1.0 / np.sqrt(np.float32(KEY_VALUE_HEADS * OUT_COLUMNS)))
    attn = attn.reshape(4, 8, 1280)
    s4[...] = jnp.concatenate([attn[:, :, :640], attn[:, :, 640:]], axis=1).astype(BF16)
    for e in (2, 1, 3):
        copy = pltpu.make_async_remote_copy(
            src_ref=s4.at[lax.rem(xx + e, 4)],
            dst_ref=r4.at[e - 1],
            send_sem=r4_send.at[e - 1],
            recv_sem=r4_recv.at[e - 1],
            device_id=x_peer(e),
            device_id_type=MESH,
        )
        copy.start()
        pending.append(copy.wait_send)
    summed = s4[xx].astype(F32)
    for e in range(3):
        pltpu.make_async_copy(s4.at[0], s4.at[0], r4_recv.at[e]).wait()
        summed = summed + r4[e].astype(F32)
    s5[...] = summed.astype(BF16)
    target_y = lax.rem(y + 4 - xx, 4)

    def to_owner(e):
        there = lax.rem(t + e, 8)
        return pltpu.make_async_remote_copy(
            src_ref=s5,
            dst_ref=r5.at[t],
            send_sem=r5_send.at[e],
            recv_sem=r5_recv,
            device_id=dev(z, target_y, r, there),
            device_id_type=MESH,
        )

    def own_copy():
        return pltpu.make_async_copy(s5, r5.at[t], r5_recv)

    for e in (4, 3, 5, 2, 6, 1, 7):
        to_owner(e).start()
        pending.append(to_owner(e).wait_send)
    pending.append(lambda: pl.when(xx != 0)(to_owner(0).wait_send))

    @pl.when(xx != 0)
    def _():
        to_owner(0).start()

    @pl.when(xx == 0)
    def _():
        own_copy().start()

    pltpu.make_async_copy(r5, r5, r5_recv).wait()

    squares = jnp.zeros((TOKENS, 128), F32)
    for xs_ in range(4):
        both = r5[2 * xs_].astype(F32) + r5[2 * xs_ + 1].astype(F32)
        for b in range(8):
            block = widen(both[:, b * ROWS : (b + 1) * ROWS])
            for half in range(2):
                place = xs_ * 16 + half * 8 + b
                residual = block[half * 8 : half * 8 + 8] + xperm[place]
                zblk[place] = residual
                squares = squares + residual * residual
    rscale = lax.rsqrt(jnp.sum(squares, axis=1, keepdims=True) * np.float32(1.0 / MODEL_WIDTH) + norm_epsilon)
    pieces = []
    for i in range(8):
        j = stored[i]
        k = lax.rem(z + 8 - lax.div(j, 8), 8)
        source = lax.rem(lax.rem(lax.div(j, 2), 4) + 4 - y, 4)
        rr = lax.rem(lax.rem(j, 2) + r, 2)
        pieces.append(zblk[source * 16 + k * 2 + rr][:, :ROWS])
    mixed_out[...] = (jnp.concatenate(pieces, axis=1) * rscale * post_v[...].reshape(1, 640)).astype(BF16)

    for wait in pending:
        wait()


def finish(master_in, mixed_in, master_out, mixed_out, held, sem):
    write_master = pltpu.make_async_copy(master_in, master_out, sem.at[0])
    write_master.start()
    values = mixed_in[...].astype(F32)
    for s in range(STEPS):
        held[s] = values[2 * s : 2 * s + 2].astype(BF16)
    write_mixed = pltpu.make_async_copy(held, mixed_out, sem.at[1])
    write_mixed.start()
    write_mixed.wait()
    write_master.wait()


def body(
    master, adam_first_moment, adam_second_moment, gradient, resync_order, inputs, in_gain, post_gain, lengths,
    cached_key_rows, cached_value_rows,
):
    half = np.arange(HEAD_SIZE // 2, dtype=np.float64)
    freqs = (rope_theta ** (-(half * 2.0 / HEAD_SIZE))).astype(np.float32)
    freqs = jnp.asarray(np.concatenate([freqs, freqs])[None, :])
    vmem = pl.BlockSpec(memory_space=pltpu.VMEM)
    hbm = pl.BlockSpec(memory_space=pltpu.HBM)
    dma = pltpu.SemaphoreType.DMA
    flat = (ROWS * 10, 128)
    new_master, mixed = pl.pallas_call(
        kernel,
        out_shape=(pltpu.VMEM(flat, F32), pltpu.VMEM((TOKENS, 640), BF16)),
        in_specs=[hbm] * 12,
        out_specs=(vmem, vmem),
        scratch_shapes=[
            pltpu.SMEM((BLOCKS,), jnp.int32),
            pltpu.SMEM((2,), jnp.int32),
            pltpu.VMEM((640,), F32),
            pltpu.VMEM((1, HEAD_SIZE), F32),
            pltpu.VMEM((STEPS, 2, MODEL_WIDTH), BF16),
            pltpu.VMEM((1, MODEL_WIDTH), F32),
            pltpu.VMEM((TOKENS, MODEL_WIDTH), F32),
            pltpu.VMEM((32, HEAD_SIZE), F32),
            pltpu.VMEM((32, HEAD_SIZE), F32),
            pltpu.VMEM((BLOCKS, TOKENS, 128), F32),
            pltpu.VMEM((BLOCKS, TOKENS, 128), F32),
            pltpu.VMEM((BLOCKS, TOKENS, 128), F32),
            pltpu.VMEM((BLOCKS, TOKENS, 128), F32),
            pltpu.VMEM(flat, F32),
            pltpu.VMEM(flat, F32),
            pltpu.VMEM(flat, F32),
            pltpu.VMEM((ROWS, 1280), BF16),
            pltpu.VMEM((2 * CACHE_SLOTS, HEAD_SIZE), BF16),
            pltpu.VMEM((2 * CACHE_SLOTS, HEAD_SIZE), BF16),
            pltpu.VMEM((QPEERS, 32, 128), BF16),
            pltpu.VMEM((QPEERS, 32, 128), BF16),
            pltpu.VMEM((4, 128, IN_COLUMNS), BF16),
            pltpu.VMEM((8, 2, ROWS, OUT_COLUMNS), BF16),
            pltpu.VMEM((QPEERS, 16, 384), BF16),
            pltpu.VMEM((QPEERS, 16, 384), BF16),
            pltpu.VMEM((32, 128), BF16),
            pltpu.VMEM((4, 32, 128), BF16),
            pltpu.VMEM((4, 16, 640), BF16),
            pltpu.VMEM((3, 16, 640), BF16),
            pltpu.VMEM((16, 640), BF16),
            pltpu.VMEM((8, 16, 640), BF16),
            dma((12,)), dma, dma, dma((3,)), dma((3,)), dma((7,)), dma((7,)), dma((8,)), dma((8,)),
            dma, dma, dma((3,)), dma((3,)), dma((3,)), dma((3,)), dma((8,)), dma, dma,
        ],
        compiler_params=pltpu.CompilerParams(collective_id=0, has_side_effects=True, vmem_limit_bytes=56 << 20),
        cost_estimate=pl.CostEstimate(flops=400_000_000, bytes_accessed=4_500_000, transcendentals=200_000),
        name="adam_attention",
    )(
        resync_order, lengths, inputs, in_gain.reshape(1, MODEL_WIDTH), post_gain, freqs,
        master.reshape(flat), adam_first_moment.reshape(flat), adam_second_moment.reshape(flat), gradient.reshape(ROWS, 1280),
        cached_key_rows.reshape(2 * CACHE_SLOTS, HEAD_SIZE), cached_value_rows.reshape(2 * CACHE_SLOTS, HEAD_SIZE),
    )
    new_master, mixed = pl.pallas_call(
        finish,
        out_shape=(jax.ShapeDtypeStruct(flat, F32), jax.ShapeDtypeStruct((STEPS, 2, 640), BF16)),
        in_specs=[vmem, vmem],
        out_specs=(hbm, hbm),
        scratch_shapes=[pltpu.VMEM((STEPS, 2, 640), BF16), dma((2,))],
        compiler_params=pltpu.CompilerParams(vmem_limit_bytes=2 << 20),
        name="finish",
    )(pltpu.with_memory_space_constraint(new_master, pltpu.VMEM), pltpu.with_memory_space_constraint(mixed, pltpu.VMEM))
    return new_master.reshape(ROWS, 1, 1280), mixed


def solution(mesh):
    in_specs = (
        P(("learn", "rep"), "tp", None),
        P(("learn", "rep"), "tp", None),
        P(("learn", "rep"), "tp", None),
        P(("learn", "rep"), "tp", None),
        P(),
        P(None, ("learn", "rep"), None),
        P(),
        P("tp"),
        P(("learn", "rep")),
        P(("learn", "rep"), "tp", None, None),
        P(("learn", "rep"), "tp", None, None),
    )
    out_specs = (P(("learn", "rep"), "tp", None), P(None, ("learn", "rep"), "tp"))
    return jax.shard_map(body, mesh=mesh, in_specs=in_specs, out_specs=out_specs, check_vma=False)
```

```python
import functools

import jax
import jax.numpy as jnp
import numpy as np
from jax import lax
from jax.experimental import pallas as pl
from jax.experimental.pallas import tpu as pltpu
from jax.sharding import PartitionSpec as P

MODEL_WIDTH = 5120
HEAD_SIZE = 128
KEY_VALUE_HEADS = 8
QUERY_PER_GROUP = 4
STEPS = 4
CACHE_SLOTS = 2048
BLOCKS = 64
ROWS = 80
IN_COLUMNS = 768
OUT_COLUMNS = 512
TOKENS = 8
QPEERS = 16

beta_one = 0.9
beta_two = 0.95
adam_rate = 0.05
adam_decay = 0.1
adam_epsilon = 1e-08
correction_one = 1.0 - 0.9**10
correction_two = 1.0 - 0.95**10
norm_epsilon = 1e-06
rope_theta = 1000000.0

MESH = pl.DeviceIdType.MESH
F32 = jnp.float32
BF16 = jnp.bfloat16


def adam_update(master, first, second, gradient):
    first_moment = beta_one * first + (1.0 - beta_one) * gradient
    second_moment = beta_two * second + (1.0 - beta_two) * gradient * gradient
    update = (
        first_moment / correction_one / (jnp.sqrt(second_moment / correction_two) + adam_epsilon)
        + adam_decay * master
    )
    return master - adam_rate * update


def widen(block):
    return jnp.concatenate([block, jnp.zeros((block.shape[0], 128 - ROWS), block.dtype)], axis=1)


def kernel(
    order_in, lengths_in, x_in, gain_in, post_in, freq_in, master_in, first_in, second_in, gradient_in, keys_in, values_in,
    master_out, mixed_out,
    order, lengths, post_v, freq_v, x_v, gain_v, xs, qh, hh, xblk, hblk, xperm, zblk, master_v, first_v, second_v, gradient_v, keys_v, values_v,
    hs, hr, wq, wo, ps, pr, os, orr, s4, r4, s5, r5,
    load_sem, h_send, h_recv, wq_send, wq_recv, ring_send, ring_recv, twin_send, twin_recv,
    p_send, p_recv, o_send, o_recv, r4_send, r4_recv, r5_send, r5_recv,
):
    l, r, t = lax.axis_index("learn"), lax.axis_index("rep"), lax.axis_index("tp")
    z, y = lax.div(l, 4), lax.rem(l, 4)
    yp, yy = lax.div(y, 2), lax.rem(y, 2)
    c = z * 2 + yp
    xx, yh = lax.div(t, 2), lax.rem(t, 2)

    def dev(z, y, r, t):
        return {"learn": z * 4 + y, "rep": r, "tp": t}

    def q_peer(d):
        other = lax.rem(c + d, QPEERS)
        return dev(lax.div(other, 2), lax.rem(other, 2) * 2 + yy, 1 - r, t)

    twin = dev(z, y, 1 - r, t)
    partner = dev(z, yp * 2 + 1 - yy, 1 - r, t)
    above = dev(lax.rem(z + 1, 8), y, 1 - r, t)
    below = dev(lax.rem(z + 7, 8), y, 1 - r, t)

    def y_peer(d):
        return dev(z, lax.rem(y + d, 4), 1 - r, t)

    def x_peer(e):
        return dev(z, y, r, lax.rem(xx + e, 4) * 2 + yh)

    pending = []

    loads = [
        pltpu.make_async_copy(src, dst, load_sem.at[i])
        for i, (src, dst) in enumerate(
            [
                (x_in, x_v), (gain_in, gain_v), (master_in, master_v), (first_in, first_v), (second_in, second_v),
                (gradient_in, gradient_v), (keys_in, keys_v), (values_in, values_v),
                (order_in, order), (lengths_in, lengths), (post_in, post_v), (freq_in, freq_v),
            ]
        )
    ]
    for i in (0, 1, 8):
        loads[i].start()

    barrier = pltpu.get_barrier_semaphore()

    def greet(device):
        pl.semaphore_signal(barrier, inc=1, device_id=device, device_id_type=MESH)

    def far_first(i):
        return lax.rem(QPEERS // 2 + jnp.where(lax.rem(i, 2) == 1, lax.div(i + 1, 2), -lax.div(i, 2)), QPEERS)

    def greet_q(i, carry):
        greet(q_peer(far_first(i)))
        return carry

    lax.fori_loop(0, QPEERS, greet_q, 0)
    for e in (4, 3, 5, 2, 6, 1, 7, 0):
        there = lax.rem(t + e, 8)
        greet(dev(z, lax.rem(y + lax.div(there, 2), 4), 1 - r, there))
    for d in (2, 1, 3):
        greet(x_peer(d))
    for device in (y_peer(1), y_peer(3), above, below, partner):
        greet(device)
    for i in (2, 3, 4, 5, 6, 7, 9, 10, 11):
        loads[i].start()
    loads[0].wait()
    loads[1].wait()
    loads[8].wait()
    for s in range(STEPS):
        xs[2 * s : 2 * s + 2, :] = x_v[s].astype(F32)
    stream = xs[...]
    rscale = lax.rsqrt(jnp.mean(stream * stream, axis=1, keepdims=True) + norm_epsilon)
    for b in range(BLOCKS):
        block = xs[:, b * ROWS : (b + 1) * ROWS]
        xblk[b] = widen(block)
        hblk[b] = widen(block * rscale * gain_v[:, b * ROWS : (b + 1) * ROWS])
    for d in range(QPEERS):
        other = lax.rem(c + d, QPEERS)
        parts = []
        for m in range(4):
            my, mr = m // 2, m % 2
            w = lax.rem(yy + my, 2) * 2 + lax.rem(1 - r + mr, 2)
            parts.append(hblk[order[other * 4 + w]])
        hs[d] = jnp.concatenate(parts, axis=0).astype(BF16)

    wq[:, ROWS:, :] = jnp.zeros((4, 128 - ROWS, IN_COLUMNS), BF16)
    for i in range(2, 6):
        loads[i].wait()
    for j in range(10):
        rows = pl.ds(j, ROWS, stride=10)
        fresh = adam_update(
            master_v[rows, :], first_v[rows, :], second_v[rows, :], gradient_v[:, j * 128 : (j + 1) * 128].astype(F32)
        )
        master_out[rows, :] = fresh
        if j < 6:
            wq[0, 0:ROWS, j * 128 : (j + 1) * 128] = fresh.astype(BF16)
        else:
            wo[0, 0, :, (j - 6) * 128 : (j - 5) * 128] = fresh.astype(BF16)

    pl.semaphore_wait(barrier, QPEERS + 8 + 3 + 5)

    def send_h(i, carry):
        d = far_first(i)
        pltpu.make_async_remote_copy(
            src_ref=hs.at[d], dst_ref=hr.at[d], send_sem=h_send, recv_sem=h_recv, device_id=q_peer(d), device_id_type=MESH
        ).start()
        return carry

    lax.fori_loop(0, QPEERS, send_h, 0)
    pending.append(pltpu.make_async_copy(hs, hs, h_send).wait)

    def share(src, dst, device):
        return pltpu.make_async_remote_copy(
            src_ref=wq.at[src, pl.ds(0, ROWS)],
            dst_ref=wq.at[dst, pl.ds(0, ROWS)],
            send_sem=wq_send.at[dst - 1],
            recv_sem=wq_recv.at[dst - 1],
            device_id=device,
            device_id_type=MESH,
        )

    shares = [share(0, 1, twin), share(0, 3, partner), share(3, 2, twin)]
    pending.extend(copy.wait_send for copy in shares)
    shares[1].start()
    shares[0].start()

    def ring(src, dst, index, device, rows=pl.ds(0, ROWS)):
        return pltpu.make_async_remote_copy(
            src_ref=wo.at[src, src % 2, rows],
            dst_ref=wo.at[dst, dst % 2, rows],
            send_sem=ring_send.at[index],
            recv_sem=ring_recv.at[index],
            device_id=device,
            device_id_type=MESH,
        )

    up = [ring(k, k + 1, k, above) for k in range(3)] + [ring(3, 4, 3, above, pl.ds(0, 48))]
    down = [ring((8 - k) % 8, 7 - k, 4 + k, below) for k in range(3)] + [ring(5, 4, 7, below, pl.ds(48, ROWS - 48))]
    to_twin = [
        pltpu.make_async_remote_copy(
            src_ref=wo.at[k, k % 2],
            dst_ref=wo.at[k, 1 - k % 2],
            send_sem=twin_send.at[k],
            recv_sem=twin_recv.at[k],
            device_id=twin,
            device_id_type=MESH,
        )
        for k in range(8)
    ]
    pending.extend(copy.wait_send for copy in up + down + to_twin)
    ring_step = [0]

    def ring_advance():
        ring_step[0] += 1
        k = ring_step[0]
        up[k - 1].wait_recv()
        if k < 4:
            up[k].start()
        down[k - 1].wait_recv()
        if k < 4:
            down[k].start()
            to_twin[8 - k].start()
        to_twin[k].start()

    up[0].start()
    down[0].start()
    to_twin[0].start()

    loads[9].wait()
    loads[10].wait()
    loads[11].wait()
    token = lax.broadcasted_iota(jnp.int32, (TOKENS, HEAD_SIZE), 0)
    lane = lax.broadcasted_iota(jnp.int32, (TOKENS, HEAD_SIZE), 1)
    positions = jnp.where(lax.rem(token, 2) == 0, lengths[0], lengths[1]) + lax.div(token, 2)
    angles = positions.astype(F32) * freq_v[...]
    cosine = jnp.cos(angles)
    sine = jnp.sin(angles)
    sine = jnp.where(lane < HEAD_SIZE // 2, -sine, sine)

    def find(j, carry):
        actor = order[j] - t * 8
        return tuple(jnp.where(actor == i, j, carry[i]) for i in range(8))

    stored = lax.fori_loop(0, BLOCKS, find, tuple(jnp.int32(0) for _ in range(8)))
    for xs_ in range(4):
        source_y = lax.rem(y + xs_, 4)
        for k in range(8):
            for rr in range(2):
                j = (lax.rem(z + 8 - k, 8) * 4 + source_y) * 2 + lax.rem(1 - r + rr, 2)
                xperm[xs_ * 16 + k * 2 + rr] = xblk[order[j]]

    shares[1].wait_recv()
    shares[2].start()

    ring_advance()
    pltpu.make_async_copy(hr, hr, h_recv).wait()
    wide = hr[...].astype(F32)
    left = jnp.concatenate([wide[:, 8 * m : 8 * m + 8, :].reshape(QPEERS * TOKENS, 128) for m in range(4)], axis=1).astype(BF16)
    shares[0].wait_recv()
    shares[2].wait_recv()
    partial = jnp.dot(left, wq[...].reshape(512, IN_COLUMNS), preferred_element_type=F32).reshape(QPEERS, TOKENS, IN_COLUMNS)
    packed = jnp.concatenate([partial[:, :, :384], partial[:, :, 384:]], axis=1).astype(BF16)
    ps[...] = packed

    def send_p(i, carry):
        d = far_first(i)
        pltpu.make_async_remote_copy(
            src_ref=ps.at[d],
            dst_ref=pr.at[d],
            send_sem=p_send,
            recv_sem=p_recv,
            device_id=q_peer(QPEERS - d),
            device_id_type=MESH,
        ).start()
        return carry

    lax.fori_loop(0, QPEERS, send_p, 0)
    pending.append(pltpu.make_async_copy(ps, ps, p_send).wait)
    ring_advance()
    ring_advance()
    pltpu.make_async_copy(pr, pr, p_recv).wait()
    projected = jnp.sum(pr[...].astype(F32), axis=0) * np.float32(1.0 / np.sqrt(np.float32(MODEL_WIDTH)))
    top, bottom = projected[0:8], projected[8:16]
    raw = jnp.concatenate(
        [top[:, 0:128], top[:, 128:256], top[:, 256:384], bottom[:, 0:128], bottom[:, 128:256]], axis=0
    )
    new_values = bottom[:, 256:384].astype(BF16)
    normed = raw * lax.rsqrt(jnp.mean(raw * raw, axis=1, keepdims=True) + norm_epsilon)
    cosine5 = jnp.concatenate([cosine] * 5, axis=0)
    sine5 = jnp.concatenate([sine] * 5, axis=0)
    rotated = normed * cosine5 + pltpu.roll(normed, HEAD_SIZE // 2, 1) * sine5
    qh[...] = rotated[0:32]
    new_keys = rotated[32:40].astype(BF16)

    scale = HEAD_SIZE ** (-0.5)
    contract_last = (((1,), (1,)), ((), ()))
    q_step = lax.rem(lax.broadcasted_iota(jnp.int32, (16, TOKENS), 0), STEPS)
    k_token = lax.broadcasted_iota(jnp.int32, (16, TOKENS), 1)
    slot = lax.broadcasted_iota(jnp.int32, (16, CACHE_SLOTS), 1)
    loads[6].wait()
    loads[7].wait()
    for n in range(2):
        rows = pl.ds(n, 16, stride=2)
        queries = qh[rows, :].astype(BF16)
        recent = lax.dot_general(queries, new_keys, contract_last, preferred_element_type=F32) * scale
        seen = (lax.rem(k_token, 2) == n) & (lax.div(k_token, 2) <= q_step)
        recent = jnp.where(seen, jnp.exp(recent), 0.0)
        scores = (
            lax.dot_general(queries, keys_v[n * CACHE_SLOTS : (n + 1) * CACHE_SLOTS, :], contract_last, preferred_element_type=F32)
            * scale
        )
        past = jnp.where(slot < lengths[n], jnp.exp(scores), 0.0)
        total = jnp.sum(past, axis=1, keepdims=True) + jnp.sum(recent, axis=1, keepdims=True)
        heads = jnp.dot(
            past.astype(BF16), values_v[n * CACHE_SLOTS : (n + 1) * CACHE_SLOTS, :], preferred_element_type=F32
        ) + jnp.dot(recent.astype(BF16), new_values, preferred_element_type=F32)
        hh[rows, :] = heads / total
    heads = hh[...].astype(BF16)

    os[...] = heads
    for d in (2, 1, 3, 0):
        copy = pltpu.make_async_remote_copy(
            src_ref=os, dst_ref=orr.at[d], send_sem=o_send.at[d], recv_sem=o_recv.at[d], device_id=y_peer(d), device_id_type=MESH
        )
        copy.start()
        pending.append(copy.wait_send)
    ring_advance()
    for k in range(8):
        to_twin[k].wait_recv()
    for d in range(4):
        pltpu.make_async_copy(os, os, o_recv.at[d]).wait()
    wide = orr[...].astype(F32)
    left = jnp.concatenate([wide[:, 8 * h : 8 * h + 8, :].reshape(32, 128) for h in range(4)], axis=1).astype(BF16)
    attn = lax.dot_general(left, wo[...].reshape(16 * ROWS, OUT_COLUMNS), contract_last, preferred_element_type=F32)
    attn = attn * np.float32(1.0 / np.sqrt(np.float32(KEY_VALUE_HEADS * OUT_COLUMNS)))
    attn = attn.reshape(4, 8, 1280)
    s4[...] = jnp.concatenate([attn[:, :, :640], attn[:, :, 640:]], axis=1).astype(BF16)
    for e in (2, 1, 3):
        copy = pltpu.make_async_remote_copy(
            src_ref=s4.at[lax.rem(xx + e, 4)],
            dst_ref=r4.at[e - 1],
            send_sem=r4_send.at[e - 1],
            recv_sem=r4_recv.at[e - 1],
            device_id=x_peer(e),
            device_id_type=MESH,
        )
        copy.start()
        pending.append(copy.wait_send)
    summed = s4[xx].astype(F32)
    for e in range(3):
        pltpu.make_async_copy(s4.at[0], s4.at[0], r4_recv.at[e]).wait()
        summed = summed + r4[e].astype(F32)
    s5[...] = summed.astype(BF16)
    target_y = lax.rem(y + 4 - xx, 4)

    def to_owner(e):
        there = lax.rem(t + e, 8)
        return pltpu.make_async_remote_copy(
            src_ref=s5,
            dst_ref=r5.at[t],
            send_sem=r5_send.at[e],
            recv_sem=r5_recv,
            device_id=dev(z, target_y, 1 - r, there),
            device_id_type=MESH,
        )

    for e in (4, 3, 5, 2, 6, 1, 7, 0):
        to_owner(e).start()
        pending.append(to_owner(e).wait_send)
    pltpu.make_async_copy(r5, r5, r5_recv).wait()

    squares = jnp.zeros((TOKENS, 128), F32)
    for xs_ in range(4):
        both = r5[2 * xs_].astype(F32) + r5[2 * xs_ + 1].astype(F32)
        for b in range(8):
            block = widen(both[:, b * ROWS : (b + 1) * ROWS])
            for half in range(2):
                place = xs_ * 16 + half * 8 + b
                residual = block[half * 8 : half * 8 + 8] + xperm[place]
                zblk[place] = residual
                squares = squares + residual * residual
    rscale = lax.rsqrt(jnp.sum(squares, axis=1, keepdims=True) * np.float32(1.0 / MODEL_WIDTH) + norm_epsilon)
    pieces = []
    for i in range(8):
        j = stored[i]
        k = lax.rem(z + 8 - lax.div(j, 8), 8)
        source = lax.rem(lax.rem(lax.div(j, 2), 4) + 4 - y, 4)
        rr = lax.rem(lax.rem(j, 2) + 1 - r, 2)
        pieces.append(zblk[source * 16 + k * 2 + rr][:, :ROWS])
    mixed_out[...] = (jnp.concatenate(pieces, axis=1) * rscale * post_v[...].reshape(1, 640)).astype(BF16)

    for wait in pending:
        wait()


def finish(master_in, mixed_in, master_out, mixed_out, held, sem):
    write_master = pltpu.make_async_copy(master_in, master_out, sem.at[0])
    write_master.start()
    values = mixed_in[...].astype(F32)
    for s in range(STEPS):
        held[s] = values[2 * s : 2 * s + 2].astype(BF16)
    write_mixed = pltpu.make_async_copy(held, mixed_out, sem.at[1])
    write_mixed.start()
    write_mixed.wait()
    write_master.wait()


def body(
    master, adam_first_moment, adam_second_moment, gradient, resync_order, inputs, in_gain, post_gain, lengths,
    cached_key_rows, cached_value_rows,
):
    half = np.arange(HEAD_SIZE // 2, dtype=np.float64)
    freqs = (rope_theta ** (-(half * 2.0 / HEAD_SIZE))).astype(np.float32)
    freqs = jnp.asarray(np.concatenate([freqs, freqs])[None, :])
    vmem = pl.BlockSpec(memory_space=pltpu.VMEM)
    hbm = pl.BlockSpec(memory_space=pltpu.HBM)
    dma = pltpu.SemaphoreType.DMA
    flat = (ROWS * 10, 128)
    new_master, mixed = pl.pallas_call(
        kernel,
        out_shape=(pltpu.VMEM(flat, F32), pltpu.VMEM((TOKENS, 640), BF16)),
        in_specs=[hbm] * 12,
        out_specs=(vmem, vmem),
        scratch_shapes=[
            pltpu.SMEM((BLOCKS,), jnp.int32),
            pltpu.SMEM((2,), jnp.int32),
            pltpu.VMEM((640,), F32),
            pltpu.VMEM((1, HEAD_SIZE), F32),
            pltpu.VMEM((STEPS, 2, MODEL_WIDTH), BF16),
            pltpu.VMEM((1, MODEL_WIDTH), F32),
            pltpu.VMEM((TOKENS, MODEL_WIDTH), F32),
            pltpu.VMEM((32, HEAD_SIZE), F32),
            pltpu.VMEM((32, HEAD_SIZE), F32),
            pltpu.VMEM((BLOCKS, TOKENS, 128), F32),
            pltpu.VMEM((BLOCKS, TOKENS, 128), F32),
            pltpu.VMEM((BLOCKS, TOKENS, 128), F32),
            pltpu.VMEM((BLOCKS, TOKENS, 128), F32),
            pltpu.VMEM(flat, F32),
            pltpu.VMEM(flat, F32),
            pltpu.VMEM(flat, F32),
            pltpu.VMEM((ROWS, 1280), BF16),
            pltpu.VMEM((2 * CACHE_SLOTS, HEAD_SIZE), BF16),
            pltpu.VMEM((2 * CACHE_SLOTS, HEAD_SIZE), BF16),
            pltpu.VMEM((QPEERS, 32, 128), BF16),
            pltpu.VMEM((QPEERS, 32, 128), BF16),
            pltpu.VMEM((4, 128, IN_COLUMNS), BF16),
            pltpu.VMEM((8, 2, ROWS, OUT_COLUMNS), BF16),
            pltpu.VMEM((QPEERS, 16, 384), BF16),
            pltpu.VMEM((QPEERS, 16, 384), BF16),
            pltpu.VMEM((32, 128), BF16),
            pltpu.VMEM((4, 32, 128), BF16),
            pltpu.VMEM((4, 16, 640), BF16),
            pltpu.VMEM((3, 16, 640), BF16),
            pltpu.VMEM((16, 640), BF16),
            pltpu.VMEM((8, 16, 640), BF16),
            dma((12,)), dma, dma, dma((3,)), dma((3,)), dma((8,)), dma((8,)), dma((8,)), dma((8,)),
            dma, dma, dma((4,)), dma((4,)), dma((3,)), dma((3,)), dma((8,)), dma,
        ],
        compiler_params=pltpu.CompilerParams(collective_id=0, has_side_effects=True, vmem_limit_bytes=56 << 20),
        cost_estimate=pl.CostEstimate(flops=400_000_000, bytes_accessed=4_500_000, transcendentals=200_000),
        name="adam_attention",
    )(
        resync_order, lengths, inputs, in_gain.reshape(1, MODEL_WIDTH), post_gain, freqs,
        master.reshape(flat), adam_first_moment.reshape(flat), adam_second_moment.reshape(flat), gradient.reshape(ROWS, 1280),
        cached_key_rows.reshape(2 * CACHE_SLOTS, HEAD_SIZE), cached_value_rows.reshape(2 * CACHE_SLOTS, HEAD_SIZE),
    )
    new_master, mixed = pl.pallas_call(
        finish,
        out_shape=(jax.ShapeDtypeStruct(flat, F32), jax.ShapeDtypeStruct((STEPS, 2, 640), BF16)),
        in_specs=[vmem, vmem],
        out_specs=(hbm, hbm),
        scratch_shapes=[pltpu.VMEM((STEPS, 2, 640), BF16), dma((2,))],
        compiler_params=pltpu.CompilerParams(vmem_limit_bytes=2 << 20),
        name="finish",
    )(pltpu.with_memory_space_constraint(new_master, pltpu.VMEM), pltpu.with_memory_space_constraint(mixed, pltpu.VMEM))
    return new_master.reshape(ROWS, 1, 1280), mixed


def solution(mesh):
    in_specs = (
        P(("learn", "rep"), "tp", None),
        P(("learn", "rep"), "tp", None),
        P(("learn", "rep"), "tp", None),
        P(("learn", "rep"), "tp", None),
        P(),
        P(None, ("learn", "rep"), None),
        P(),
        P("tp"),
        P(("learn", "rep")),
        P(("learn", "rep"), "tp", None, None),
        P(("learn", "rep"), "tp", None, None),
    )
    out_specs = (P(("learn", "rep"), "tp", None), P(None, ("learn", "rep"), "tp"))
    return jax.shard_map(body, mesh=mesh, in_specs=in_specs, out_specs=out_specs, check_vma=False)
```

```python
import functools

import jax
import jax.numpy as jnp
import numpy as np
from jax import lax
from jax.experimental import pallas as pl
from jax.experimental.pallas import tpu as pltpu
from jax.sharding import PartitionSpec as P

MODEL_WIDTH = 5120
HEAD_SIZE = 128
KEY_VALUE_HEADS = 8
QUERY_PER_GROUP = 4
STEPS = 4
CACHE_SLOTS = 2048
BLOCKS = 64
ROWS = 80
IN_COLUMNS = 768
OUT_COLUMNS = 512
TOKENS = 8
QPEERS = 16

beta_one = 0.9
beta_two = 0.95
adam_rate = 0.05
adam_decay = 0.1
adam_epsilon = 1e-08
correction_one = 1.0 - 0.9**10
correction_two = 1.0 - 0.95**10
norm_epsilon = 1e-06
rope_theta = 1000000.0

MESH = pl.DeviceIdType.MESH
F32 = jnp.float32
BF16 = jnp.bfloat16


def adam_update(master, first, second, gradient):
    first_moment = beta_one * first + (1.0 - beta_one) * gradient
    second_moment = beta_two * second + (1.0 - beta_two) * gradient * gradient
    update = (
        first_moment / correction_one / (jnp.sqrt(second_moment / correction_two) + adam_epsilon)
        + adam_decay * master
    )
    return master - adam_rate * update


def widen(block):
    return jnp.concatenate([block, jnp.zeros((block.shape[0], 128 - ROWS), block.dtype)], axis=1)


def kernel(
    order_in, lengths_in, x_in, gain_in, post_in, freq_in, master_in, first_in, second_in, gradient_in, keys_in, values_in,
    master_out, mixed_out,
    order, lengths, post_v, freq_v, x_v, gain_v, xs, qh, hh, xblk, hblk, xperm, zblk, master_v, first_v, second_v, gradient_v, keys_v, values_v,
    hs, hr, wq, wo, ps, pr, os, orr, s4, r4, s5, r5,
    load_sem, h_send, h_recv, wq_send, wq_recv, ring_send, ring_recv, twin_send, twin_recv,
    p_send, p_recv, o_send, o_recv, r4_send, r4_recv, r5_send, r5_recv,
):
    l, r, t = lax.axis_index("learn"), lax.axis_index("rep"), lax.axis_index("tp")
    z, y = lax.div(l, 4), lax.rem(l, 4)
    yp, yy = lax.div(y, 2), lax.rem(y, 2)
    c = z * 2 + yp
    xx, yh = lax.div(t, 2), lax.rem(t, 2)

    def dev(z, y, r, t):
        return {"learn": z * 4 + y, "rep": r, "tp": t}

    def q_peer(d):
        other = lax.rem(c + d, QPEERS)
        return dev(lax.div(other, 2), lax.rem(other, 2) * 2 + yy, 1 - r, t)

    twin = dev(z, y, 1 - r, t)
    partner = dev(z, yp * 2 + 1 - yy, 1 - r, t)
    above = dev(lax.rem(z + 1, 8), y, 1 - r, t)
    below = dev(lax.rem(z + 7, 8), y, 1 - r, t)

    def y_peer(d):
        return dev(z, lax.rem(y + d, 4), r, t)

    def x_peer(e):
        return dev(z, y, r, lax.rem(xx + e, 4) * 2 + yh)

    pending = []

    loads = [
        pltpu.make_async_copy(src, dst, load_sem.at[i])
        for i, (src, dst) in enumerate(
            [
                (x_in, x_v), (gain_in, gain_v), (master_in, master_v), (first_in, first_v), (second_in, second_v),
                (gradient_in, gradient_v), (keys_in, keys_v), (values_in, values_v),
                (order_in, order), (lengths_in, lengths), (post_in, post_v), (freq_in, freq_v),
            ]
        )
    ]
    for i in (0, 1, 8):
        loads[i].start()

    barrier = pltpu.get_barrier_semaphore()

    def greet(device):
        pl.semaphore_signal(barrier, inc=1, device_id=device, device_id_type=MESH)

    def far_first(i):
        return lax.rem(QPEERS // 2 + jnp.where(lax.rem(i, 2) == 1, lax.div(i + 1, 2), -lax.div(i, 2)), QPEERS)

    def greet_q(i, carry):
        greet(q_peer(far_first(i)))
        return carry

    lax.fori_loop(0, QPEERS, greet_q, 0)
    for e in (4, 3, 5, 2, 6, 1, 7, 0):
        there = lax.rem(t + e, 8)
        device = dev(z, lax.rem(y + lax.div(there, 2), 4), r, there)
        if e == 0:
            pl.when(xx != 0)(functools.partial(greet, device))
        else:
            greet(device)
    for d in (2, 1, 3):
        greet(y_peer(d))
        greet(x_peer(d))
    for device in (above, below, partner):
        greet(device)
    for i in (2, 3, 4, 5, 6, 7, 9, 10, 11):
        loads[i].start()
    loads[0].wait()
    loads[1].wait()
    loads[8].wait()
    for s in range(STEPS):
        xs[2 * s : 2 * s + 2, :] = x_v[s].astype(F32)
    stream = xs[...]
    rscale = lax.rsqrt(jnp.mean(stream * stream, axis=1, keepdims=True) + norm_epsilon)
    for b in range(BLOCKS):
        block = xs[:, b * ROWS : (b + 1) * ROWS]
        xblk[b] = widen(block)
        hblk[b] = widen(block * rscale * gain_v[:, b * ROWS : (b + 1) * ROWS])
    for d in range(QPEERS):
        other = lax.rem(c + d, QPEERS)
        parts = []
        for m in range(4):
            my, mr = m // 2, m % 2
            w = lax.rem(yy + my, 2) * 2 + lax.rem(1 - r + mr, 2)
            parts.append(hblk[order[other * 4 + w]])
        hs[d] = jnp.concatenate(parts, axis=0).astype(BF16)

    wq[:, ROWS:, :] = jnp.zeros((4, 128 - ROWS, IN_COLUMNS), BF16)
    for i in range(2, 6):
        loads[i].wait()
    for j in range(10):
        rows = pl.ds(j, ROWS, stride=10)
        fresh = adam_update(
            master_v[rows, :], first_v[rows, :], second_v[rows, :], gradient_v[:, j * 128 : (j + 1) * 128].astype(F32)
        )
        master_out[rows, :] = fresh
        if j < 6:
            wq[0, 0:ROWS, j * 128 : (j + 1) * 128] = fresh.astype(BF16)
        else:
            wo[0, 0, :, (j - 6) * 128 : (j - 5) * 128] = fresh.astype(BF16)

    pl.semaphore_wait(barrier, QPEERS + 7 + 6 + 3 + jnp.where(xx != 0, 1, 0))

    def send_h(i, carry):
        d = far_first(i)
        pltpu.make_async_remote_copy(
            src_ref=hs.at[d], dst_ref=hr.at[d], send_sem=h_send, recv_sem=h_recv, device_id=q_peer(d), device_id_type=MESH
        ).start()
        return carry

    lax.fori_loop(0, QPEERS, send_h, 0)
    pending.append(pltpu.make_async_copy(hs, hs, h_send).wait)

    def share(src, dst, device):
        return pltpu.make_async_remote_copy(
            src_ref=wq.at[src, pl.ds(0, ROWS)],
            dst_ref=wq.at[dst, pl.ds(0, ROWS)],
            send_sem=wq_send.at[dst - 1],
            recv_sem=wq_recv.at[dst - 1],
            device_id=device,
            device_id_type=MESH,
        )

    shares = [share(0, 1, twin), share(0, 3, partner), share(3, 2, twin)]
    pending.extend(copy.wait_send for copy in shares)
    shares[1].start()
    shares[0].start()

    def ring(src, dst, index, device, rows=pl.ds(0, ROWS)):
        return pltpu.make_async_remote_copy(
            src_ref=wo.at[src, src % 2, rows],
            dst_ref=wo.at[dst, dst % 2, rows],
            send_sem=ring_send.at[index],
            recv_sem=ring_recv.at[index],
            device_id=device,
            device_id_type=MESH,
        )

    up = [ring(k, k + 1, k, above) for k in range(3)] + [ring(3, 4, 3, above, pl.ds(0, 48))]
    down = [ring((8 - k) % 8, 7 - k, 4 + k, below) for k in range(3)] + [ring(5, 4, 7, below, pl.ds(48, ROWS - 48))]
    to_twin = [
        pltpu.make_async_remote_copy(
            src_ref=wo.at[k, k % 2],
            dst_ref=wo.at[k, 1 - k % 2],
            send_sem=twin_send.at[k],
            recv_sem=twin_recv.at[k],
            device_id=twin,
            device_id_type=MESH,
        )
        for k in range(8)
    ]
    pending.extend(copy.wait_send for copy in up + down + to_twin)
    ring_step = [0]

    def ring_advance():
        ring_step[0] += 1
        k = ring_step[0]
        up[k - 1].wait_recv()
        if k < 4:
            up[k].start()
        down[k - 1].wait_recv()
        if k < 4:
            down[k].start()
            to_twin[8 - k].start()
        to_twin[k].start()

    up[0].start()
    down[0].start()
    to_twin[0].start()

    loads[9].wait()
    loads[10].wait()
    loads[11].wait()
    token = lax.broadcasted_iota(jnp.int32, (TOKENS, HEAD_SIZE), 0)
    lane = lax.broadcasted_iota(jnp.int32, (TOKENS, HEAD_SIZE), 1)
    positions = jnp.where(lax.rem(token, 2) == 0, lengths[0], lengths[1]) + lax.div(token, 2)
    angles = positions.astype(F32) * freq_v[...]
    cosine = jnp.cos(angles)
    sine = jnp.sin(angles)
    sine = jnp.where(lane < HEAD_SIZE // 2, -sine, sine)

    def find(j, carry):
        actor = order[j] - t * 8
        return tuple(jnp.where(actor == i, j, carry[i]) for i in range(8))

    stored = lax.fori_loop(0, BLOCKS, find, tuple(jnp.int32(0) for _ in range(8)))
    for xs_ in range(4):
        source_y = lax.rem(y + xs_, 4)
        for k in range(8):
            for rr in range(2):
                j = (lax.rem(z + 8 - k, 8) * 4 + source_y) * 2 + lax.rem(r + rr, 2)
                xperm[xs_ * 16 + k * 2 + rr] = xblk[order[j]]

    shares[1].wait_recv()
    shares[2].start()

    ring_advance()
    pltpu.make_async_copy(hr, hr, h_recv).wait()
    wide = hr[...].astype(F32)
    left = jnp.concatenate([wide[:, 8 * m : 8 * m + 8, :].reshape(QPEERS * TOKENS, 128) for m in range(4)], axis=1).astype(BF16)
    shares[0].wait_recv()
    shares[2].wait_recv()
    partial = jnp.dot(left, wq[...].reshape(512, IN_COLUMNS), preferred_element_type=F32).reshape(QPEERS, TOKENS, IN_COLUMNS)
    packed = jnp.concatenate([partial[:, :, :384], partial[:, :, 384:]], axis=1).astype(BF16)
    ps[...] = packed

    def send_p(i, carry):
        d = far_first(i)
        pltpu.make_async_remote_copy(
            src_ref=ps.at[d],
            dst_ref=pr.at[d],
            send_sem=p_send,
            recv_sem=p_recv,
            device_id=q_peer(QPEERS - d),
            device_id_type=MESH,
        ).start()
        return carry

    lax.fori_loop(0, QPEERS, send_p, 0)
    pending.append(pltpu.make_async_copy(ps, ps, p_send).wait)
    ring_advance()
    ring_advance()
    pltpu.make_async_copy(pr, pr, p_recv).wait()
    projected = jnp.sum(pr[...].astype(F32), axis=0) * np.float32(1.0 / np.sqrt(np.float32(MODEL_WIDTH)))
    top, bottom = projected[0:8], projected[8:16]
    raw = jnp.concatenate(
        [top[:, 0:128], top[:, 128:256], top[:, 256:384], bottom[:, 0:128], bottom[:, 128:256]], axis=0
    )
    new_values = bottom[:, 256:384].astype(BF16)
    normed = raw * lax.rsqrt(jnp.mean(raw * raw, axis=1, keepdims=True) + norm_epsilon)
    cosine5 = jnp.concatenate([cosine] * 5, axis=0)
    sine5 = jnp.concatenate([sine] * 5, axis=0)
    rotated = normed * cosine5 + pltpu.roll(normed, HEAD_SIZE // 2, 1) * sine5
    qh[...] = rotated[0:32]
    new_keys = rotated[32:40].astype(BF16)

    scale = HEAD_SIZE ** (-0.5)
    contract_last = (((1,), (1,)), ((), ()))
    q_step = lax.rem(lax.broadcasted_iota(jnp.int32, (16, TOKENS), 0), STEPS)
    k_token = lax.broadcasted_iota(jnp.int32, (16, TOKENS), 1)
    slot = lax.broadcasted_iota(jnp.int32, (16, CACHE_SLOTS), 1)
    loads[6].wait()
    loads[7].wait()
    for n in range(2):
        rows = pl.ds(n, 16, stride=2)
        queries = qh[rows, :].astype(BF16)
        recent = lax.dot_general(queries, new_keys, contract_last, preferred_element_type=F32) * scale
        seen = (lax.rem(k_token, 2) == n) & (lax.div(k_token, 2) <= q_step)
        recent = jnp.where(seen, jnp.exp(recent), 0.0)
        scores = (
            lax.dot_general(queries, keys_v[n * CACHE_SLOTS : (n + 1) * CACHE_SLOTS, :], contract_last, preferred_element_type=F32)
            * scale
        )
        past = jnp.where(slot < lengths[n], jnp.exp(scores), 0.0)
        total = jnp.sum(past, axis=1, keepdims=True) + jnp.sum(recent, axis=1, keepdims=True)
        heads = jnp.dot(
            past.astype(BF16), values_v[n * CACHE_SLOTS : (n + 1) * CACHE_SLOTS, :], preferred_element_type=F32
        ) + jnp.dot(recent.astype(BF16), new_values, preferred_element_type=F32)
        hh[rows, :] = heads / total
    heads = hh[...].astype(BF16)

    os[...] = heads
    orr[0] = heads
    for d in (2, 1, 3):
        copy = pltpu.make_async_remote_copy(
            src_ref=os, dst_ref=orr.at[d], send_sem=o_send.at[d - 1], recv_sem=o_recv.at[d - 1], device_id=y_peer(d), device_id_type=MESH
        )
        copy.start()
        pending.append(copy.wait_send)
    ring_advance()
    for k in range(8):
        to_twin[k].wait_recv()
    for d in range(3):
        pltpu.make_async_copy(os, os, o_recv.at[d]).wait()
    wide = orr[...].astype(F32)
    left = jnp.concatenate([wide[:, 8 * h : 8 * h + 8, :].reshape(32, 128) for h in range(4)], axis=1).astype(BF16)
    attn = lax.dot_general(left, wo[...].reshape(16 * ROWS, OUT_COLUMNS), contract_last, preferred_element_type=F32)
    attn = attn * np.float32(1.0 / np.sqrt(np.float32(KEY_VALUE_HEADS * OUT_COLUMNS)))
    attn = attn.reshape(4, 8, 1280)
    s4[...] = jnp.concatenate([attn[:, :, :640], attn[:, :, 640:]], axis=1).astype(BF16)
    for e in (2, 1, 3):
        copy = pltpu.make_async_remote_copy(
            src_ref=s4.at[lax.rem(xx + e, 4)],
            dst_ref=r4.at[e - 1],
            send_sem=r4_send.at[e - 1],
            recv_sem=r4_recv.at[e - 1],
            device_id=x_peer(e),
            device_id_type=MESH,
        )
        copy.start()
        pending.append(copy.wait_send)
    summed = s4[xx].astype(F32)
    for e in range(3):
        pltpu.make_async_copy(s4.at[0], s4.at[0], r4_recv.at[e]).wait()
        summed = summed + r4[e].astype(F32)
    s5[...] = summed.astype(BF16)
    target_y = lax.rem(y + 4 - xx, 4)

    def to_owner(e):
        there = lax.rem(t + e, 8)
        return pltpu.make_async_remote_copy(
            src_ref=s5,
            dst_ref=r5.at[t],
            send_sem=r5_send.at[e],
            recv_sem=r5_recv,
            device_id=dev(z, target_y, r, there),
            device_id_type=MESH,
        )

    for e in (4, 3, 5, 2, 6, 1, 7):
        to_owner(e).start()
        pending.append(to_owner(e).wait_send)
    pending.append(lambda: pl.when(xx != 0)(to_owner(0).wait_send))

    @pl.when(xx != 0)
    def _():
        to_owner(0).start()

    @pl.when(xx == 0)
    def _():
        pltpu.make_async_copy(s5, r5.at[t], r5_recv).start()

    pltpu.make_async_copy(r5, r5, r5_recv).wait()

    squares = jnp.zeros((TOKENS, 128), F32)
    for xs_ in range(4):
        both = r5[2 * xs_].astype(F32) + r5[2 * xs_ + 1].astype(F32)
        for b in range(8):
            block = widen(both[:, b * ROWS : (b + 1) * ROWS])
            for half in range(2):
                place = xs_ * 16 + half * 8 + b
                residual = block[half * 8 : half * 8 + 8] + xperm[place]
                zblk[place] = residual
                squares = squares + residual * residual
    rscale = lax.rsqrt(jnp.sum(squares, axis=1, keepdims=True) * np.float32(1.0 / MODEL_WIDTH) + norm_epsilon)
    pieces = []
    for i in range(8):
        j = stored[i]
        k = lax.rem(z + 8 - lax.div(j, 8), 8)
        source = lax.rem(lax.rem(lax.div(j, 2), 4) + 4 - y, 4)
        rr = lax.rem(lax.rem(j, 2) + r, 2)
        pieces.append(zblk[source * 16 + k * 2 + rr][:, :ROWS])
    mixed_out[...] = (jnp.concatenate(pieces, axis=1) * rscale * post_v[...].reshape(1, 640)).astype(BF16)

    for wait in pending:
        wait()


def finish(master_in, mixed_in, master_out, mixed_out, held, sem):
    write_master = pltpu.make_async_copy(master_in, master_out, sem.at[0])
    write_master.start()
    values = mixed_in[...].astype(F32)
    for s in range(STEPS):
        held[s] = values[2 * s : 2 * s + 2].astype(BF16)
    write_mixed = pltpu.make_async_copy(held, mixed_out, sem.at[1])
    write_mixed.start()
    write_mixed.wait()
    write_master.wait()


def body(
    master, adam_first_moment, adam_second_moment, gradient, resync_order, inputs, in_gain, post_gain, lengths,
    cached_key_rows, cached_value_rows,
):
    half = np.arange(HEAD_SIZE // 2, dtype=np.float64)
    freqs = (rope_theta ** (-(half * 2.0 / HEAD_SIZE))).astype(np.float32)
    freqs = jnp.asarray(np.concatenate([freqs, freqs])[None, :])
    vmem = pl.BlockSpec(memory_space=pltpu.VMEM)
    hbm = pl.BlockSpec(memory_space=pltpu.HBM)
    dma = pltpu.SemaphoreType.DMA
    flat = (ROWS * 10, 128)
    new_master, mixed = pl.pallas_call(
        kernel,
        out_shape=(pltpu.VMEM(flat, F32), pltpu.VMEM((TOKENS, 640), BF16)),
        in_specs=[hbm] * 12,
        out_specs=(vmem, vmem),
        scratch_shapes=[
            pltpu.SMEM((BLOCKS,), jnp.int32),
            pltpu.SMEM((2,), jnp.int32),
            pltpu.VMEM((640,), F32),
            pltpu.VMEM((1, HEAD_SIZE), F32),
            pltpu.VMEM((STEPS, 2, MODEL_WIDTH), BF16),
            pltpu.VMEM((1, MODEL_WIDTH), F32),
            pltpu.VMEM((TOKENS, MODEL_WIDTH), F32),
            pltpu.VMEM((32, HEAD_SIZE), F32),
            pltpu.VMEM((32, HEAD_SIZE), F32),
            pltpu.VMEM((BLOCKS, TOKENS, 128), F32),
            pltpu.VMEM((BLOCKS, TOKENS, 128), F32),
            pltpu.VMEM((BLOCKS, TOKENS, 128), F32),
            pltpu.VMEM((BLOCKS, TOKENS, 128), F32),
            pltpu.VMEM(flat, F32),
            pltpu.VMEM(flat, F32),
            pltpu.VMEM(flat, F32),
            pltpu.VMEM((ROWS, 1280), BF16),
            pltpu.VMEM((2 * CACHE_SLOTS, HEAD_SIZE), BF16),
            pltpu.VMEM((2 * CACHE_SLOTS, HEAD_SIZE), BF16),
            pltpu.VMEM((QPEERS, 32, 128), BF16),
            pltpu.VMEM((QPEERS, 32, 128), BF16),
            pltpu.VMEM((4, 128, IN_COLUMNS), BF16),
            pltpu.VMEM((8, 2, ROWS, OUT_COLUMNS), BF16),
            pltpu.VMEM((QPEERS, 16, 384), BF16),
            pltpu.VMEM((QPEERS, 16, 384), BF16),
            pltpu.VMEM((32, 128), BF16),
            pltpu.VMEM((4, 32, 128), BF16),
            pltpu.VMEM((4, 16, 640), BF16),
            pltpu.VMEM((3, 16, 640), BF16),
            pltpu.VMEM((16, 640), BF16),
            pltpu.VMEM((8, 16, 640), BF16),
            dma((12,)), dma, dma, dma((3,)), dma((3,)), dma((8,)), dma((8,)), dma((8,)), dma((8,)),
            dma, dma, dma((3,)), dma((3,)), dma((3,)), dma((3,)), dma((8,)), dma,
        ],
        compiler_params=pltpu.CompilerParams(collective_id=0, has_side_effects=True, vmem_limit_bytes=56 << 20),
        cost_estimate=pl.CostEstimate(flops=400_000_000, bytes_accessed=4_500_000, transcendentals=200_000),
        name="adam_attention",
    )(
        resync_order, lengths, inputs, in_gain.reshape(1, MODEL_WIDTH), post_gain, freqs,
        master.reshape(flat), adam_first_moment.reshape(flat), adam_second_moment.reshape(flat), gradient.reshape(ROWS, 1280),
        cached_key_rows.reshape(2 * CACHE_SLOTS, HEAD_SIZE), cached_value_rows.reshape(2 * CACHE_SLOTS, HEAD_SIZE),
    )
    new_master, mixed = pl.pallas_call(
        finish,
        out_shape=(jax.ShapeDtypeStruct(flat, F32), jax.ShapeDtypeStruct((STEPS, 2, 640), BF16)),
        in_specs=[vmem, vmem],
        out_specs=(hbm, hbm),
        scratch_shapes=[pltpu.VMEM((STEPS, 2, 640), BF16), dma((2,))],
        compiler_params=pltpu.CompilerParams(vmem_limit_bytes=2 << 20),
        name="finish",
    )(pltpu.with_memory_space_constraint(new_master, pltpu.VMEM), pltpu.with_memory_space_constraint(mixed, pltpu.VMEM))
    return new_master.reshape(ROWS, 1, 1280), mixed


def solution(mesh):
    in_specs = (
        P(("learn", "rep"), "tp", None),
        P(("learn", "rep"), "tp", None),
        P(("learn", "rep"), "tp", None),
        P(("learn", "rep"), "tp", None),
        P(),
        P(None, ("learn", "rep"), None),
        P(),
        P("tp"),
        P(("learn", "rep")),
        P(("learn", "rep"), "tp", None, None),
        P(("learn", "rep"), "tp", None, None),
    )
    out_specs = (P(("learn", "rep"), "tp", None), P(None, ("learn", "rep"), "tp"))
    return jax.shard_map(body, mesh=mesh, in_specs=in_specs, out_specs=out_specs, check_vma=False)
```

```python
import functools

import jax
import jax.numpy as jnp
import numpy as np
from jax import lax
from jax.experimental import pallas as pl
from jax.experimental.pallas import tpu as pltpu
from jax.sharding import PartitionSpec as P

MODEL_WIDTH = 5120
HEAD_SIZE = 128
KEY_VALUE_HEADS = 8
QUERY_PER_GROUP = 4
STEPS = 4
CACHE_SLOTS = 2048
BLOCKS = 64
ROWS = 80
IN_COLUMNS = 768
OUT_COLUMNS = 512
TOKENS = 8
RING = (0, 1, 7, 2, 6, 3, 5, 4)
PLACE = tuple(RING.index(k) for k in range(8))
QPEERS = 16

beta_one = 0.9
beta_two = 0.95
adam_rate = 0.05
adam_decay = 0.1
adam_epsilon = 1e-08
correction_one = 1.0 - 0.9**10
correction_two = 1.0 - 0.95**10
norm_epsilon = 1e-06
rope_theta = 1000000.0

MESH = pl.DeviceIdType.MESH
F32 = jnp.float32
BF16 = jnp.bfloat16


def adam_update(master, first, second, gradient):
    first_moment = beta_one * first + (1.0 - beta_one) * gradient
    second_moment = beta_two * second + (1.0 - beta_two) * gradient * gradient
    update = (
        first_moment / correction_one / (jnp.sqrt(second_moment / correction_two) + adam_epsilon)
        + adam_decay * master
    )
    return master - adam_rate * update


def widen(block):
    return jnp.concatenate([block, jnp.zeros((block.shape[0], 128 - ROWS), block.dtype)], axis=1)


def kernel(
    order_in, lengths_in, x_in, gain_in, post_in, freq_in, master_in, first_in, second_in, gradient_in, keys_in, values_in,
    master_out, mixed_out,
    order, lengths, post_v, freq_v, x_v, gain_v, xs, qh, hh, xblk, hblk, xperm, zblk, master_v, first_v, second_v, gradient_v, keys_v, values_v,
    hs, hr, wq, wo, ps, pr, ps2, pr2, os, orr, attn, s4, r4, s5, r5,
    load_sem, h_send, h_recv, wq_send, wq_recv, ring_send, ring_recv, twin_send, twin_recv,
    p_send, p_recv, p2_send, p2_recv, o_send, o_recv, r4_send, r4_recv, r5_send, r5_recv,
):
    l, r, t = lax.axis_index("learn"), lax.axis_index("rep"), lax.axis_index("tp")
    z, y = lax.div(l, 4), lax.rem(l, 4)
    yp, yy = lax.div(y, 2), lax.rem(y, 2)
    c = z * 2 + yp
    xx, yh = lax.div(t, 2), lax.rem(t, 2)

    def dev(z, y, r, t):
        return {"learn": z * 4 + y, "rep": r, "tp": t}

    def q_peer(d):
        other = lax.rem(c + d, QPEERS)
        return dev(lax.div(other, 2), lax.rem(other, 2) * 2 + yy, 1 - r, t)

    twin = dev(z, y, 1 - r, t)
    partner = dev(z, yp * 2 + 1 - yy, 1 - r, t)
    above = dev(lax.rem(z + 1, 8), y, 1 - r, t)
    below = dev(lax.rem(z + 7, 8), y, 1 - r, t)

    def y_peer(d):
        return dev(z, lax.rem(y + d, 4), r, t)

    def x_peer(e):
        return dev(z, y, r, lax.rem(xx + e, 4) * 2 + yh)

    pending = []

    loads = [
        pltpu.make_async_copy(src, dst, load_sem.at[i])
        for i, (src, dst) in enumerate(
            [
                (x_in, x_v), (gain_in, gain_v), (master_in, master_v), (first_in, first_v), (second_in, second_v),
                (gradient_in, gradient_v), (keys_in, keys_v), (values_in, values_v),
                (order_in, order), (lengths_in, lengths), (post_in, post_v), (freq_in, freq_v),
            ]
        )
    ]
    for i in (0, 1, 8):
        loads[i].start()

    barrier = pltpu.get_barrier_semaphore()

    def greet(device):
        pl.semaphore_signal(barrier, inc=1, device_id=device, device_id_type=MESH)

    def far_first(i):
        return lax.rem(QPEERS // 2 + jnp.where(lax.rem(i, 2) == 1, lax.div(i + 1, 2), -lax.div(i, 2)), QPEERS)

    def greet_q(i, carry):
        greet(q_peer(far_first(i)))
        return carry

    lax.fori_loop(0, QPEERS, greet_q, 0)
    for e in (4, 3, 5, 2, 6, 1, 7, 0):
        there = lax.rem(t + e, 8)
        device = dev(z, lax.rem(y + lax.div(there, 2), 4), r, there)
        if e == 0:
            pl.when(xx != 0)(functools.partial(greet, device))
        else:
            greet(device)
    for d in (2, 1, 3):
        greet(y_peer(d))
        greet(x_peer(d))
    for device in (above, below, partner):
        greet(device)
    for i in (2, 3, 4, 5, 6, 7, 9, 10, 11):
        loads[i].start()
    loads[0].wait()
    loads[1].wait()
    loads[8].wait()
    for s in range(STEPS):
        xs[2 * s : 2 * s + 2, :] = x_v[s].astype(F32)
    stream = xs[...]
    rscale = lax.rsqrt(jnp.mean(stream * stream, axis=1, keepdims=True) + norm_epsilon)
    for b in range(BLOCKS):
        block = xs[:, b * ROWS : (b + 1) * ROWS]
        xblk[b] = widen(block)
        hblk[b] = widen(block * rscale * gain_v[:, b * ROWS : (b + 1) * ROWS])
    for d in range(QPEERS):
        other = lax.rem(c + d, QPEERS)
        parts = []
        for m in range(4):
            my, mr = m // 2, m % 2
            w = lax.rem(yy + my, 2) * 2 + lax.rem(1 - r + mr, 2)
            parts.append(hblk[order[other * 4 + w]])
        hs[d] = jnp.concatenate(parts, axis=0).astype(BF16)

    wq[:, ROWS:, :] = jnp.zeros((4, 128 - ROWS, IN_COLUMNS), BF16)
    for i in range(2, 6):
        loads[i].wait()
    for j in range(10):
        rows = pl.ds(j, ROWS, stride=10)
        fresh = adam_update(
            master_v[rows, :], first_v[rows, :], second_v[rows, :], gradient_v[:, j * 128 : (j + 1) * 128].astype(F32)
        )
        master_out[rows, :] = fresh
        if j < 6:
            wq[0, 0:ROWS, j * 128 : (j + 1) * 128] = fresh.astype(BF16)
        else:
            wo[0, 0, :, (j - 6) * 128 : (j - 5) * 128] = fresh.astype(BF16)

    pl.semaphore_wait(barrier, QPEERS + 7 + 6 + 3 + jnp.where(xx != 0, 1, 0))

    def send_h(i, carry):
        d = far_first(i)
        pltpu.make_async_remote_copy(
            src_ref=hs.at[d], dst_ref=hr.at[d], send_sem=h_send, recv_sem=h_recv, device_id=q_peer(d), device_id_type=MESH
        ).start()
        return carry

    lax.fori_loop(0, QPEERS, send_h, 0)
    pending.append(pltpu.make_async_copy(hs, hs, h_send).wait)

    def share(src, dst, device):
        return pltpu.make_async_remote_copy(
            src_ref=wq.at[src, pl.ds(0, ROWS)],
            dst_ref=wq.at[dst, pl.ds(0, ROWS)],
            send_sem=wq_send.at[dst - 1],
            recv_sem=wq_recv.at[dst - 1],
            device_id=device,
            device_id_type=MESH,
        )

    shares = [share(0, 1, twin), share(0, 3, partner), share(3, 2, twin)]
    pending.extend(copy.wait_send for copy in shares)
    shares[1].start()
    shares[0].start()

    parts = (pl.ds(0, 48), pl.ds(48, ROWS - 48))

    def ring(src, dst, index, device, part):
        return pltpu.make_async_remote_copy(
            src_ref=wo.at[PLACE[src], src % 2, parts[part]],
            dst_ref=wo.at[PLACE[dst], dst % 2, parts[part]],
            send_sem=ring_send.at[2 * index + part],
            recv_sem=ring_recv.at[2 * index + part],
            device_id=device,
            device_id_type=MESH,
        )

    up = {(k, part): ring(k, k + 1, k, above, part) for k in range(4) for part in range(2) if (k, part) != (3, 1)}
    down = {(k, part): ring((8 - k) % 8, 7 - k, 4 + k, below, part) for k in range(4) for part in range(2) if (k, part) != (3, 0)}
    to_twin = [
        pltpu.make_async_remote_copy(
            src_ref=wo.at[PLACE[k], k % 2],
            dst_ref=wo.at[PLACE[k], 1 - k % 2],
            send_sem=twin_send.at[k],
            recv_sem=twin_recv.at[k],
            device_id=twin,
            device_id_type=MESH,
        )
        for k in range(8)
    ]
    pending.extend(copy.wait_send for copy in list(up.values()) + list(down.values()) + to_twin)
    ring_step = [0]

    def ring_advance():
        ring_step[0] += 1
        k = ring_step[0]
        for part in range(2):
            for copies in (up, down):
                if (k - 1, part) in copies:
                    copies[k - 1, part].wait_recv()
                if (k, part) in copies:
                    copies[k, part].start()
        to_twin[k].start()
        if k < 4:
            to_twin[8 - k].start()

    for part in range(2):
        up[0, part].start()
        down[0, part].start()
    to_twin[0].start()

    loads[9].wait()
    loads[10].wait()
    loads[11].wait()
    token = lax.broadcasted_iota(jnp.int32, (TOKENS, HEAD_SIZE), 0)
    lane = lax.broadcasted_iota(jnp.int32, (TOKENS, HEAD_SIZE), 1)
    positions = jnp.where(lax.rem(token, 2) == 0, lengths[0], lengths[1]) + lax.div(token, 2)
    angles = positions.astype(F32) * freq_v[...]
    cosine = jnp.cos(angles)
    sine = jnp.sin(angles)
    sine = jnp.where(lane < HEAD_SIZE // 2, -sine, sine)

    def find(j, carry):
        actor = order[j] - t * 8
        return tuple(jnp.where(actor == i, j, carry[i]) for i in range(8))

    stored = lax.fori_loop(0, BLOCKS, find, tuple(jnp.int32(0) for _ in range(8)))
    places = []
    for j in stored:
        k = lax.rem(z + 8 - lax.div(j, 8), 8)
        source = lax.rem(lax.rem(lax.div(j, 2), 4) + 4 - y, 4)
        rr = lax.rem(lax.rem(j, 2) + r, 2)
        slot = jnp.int32(0)
        for i in range(1, 8):
            slot = jnp.where(k == RING[i], i, slot)
        places.append(source * 16 + slot * 2 + rr)
    for xs_ in range(4):
        source_y = lax.rem(y + xs_, 4)
        for k in range(8):
            for rr in range(2):
                j = (lax.rem(z + 8 - k, 8) * 4 + source_y) * 2 + lax.rem(r + rr, 2)
                xperm[xs_ * 16 + PLACE[k] * 2 + rr] = xblk[order[j]]

    shares[1].wait_recv()
    shares[2].start()

    ring_advance()
    pltpu.make_async_copy(hr, hr, h_recv).wait()
    wide = hr[...].astype(F32)
    left = jnp.concatenate([wide[:, 8 * m : 8 * m + 8, :].reshape(QPEERS * TOKENS, 128) for m in range(4)], axis=1).astype(BF16)
    shares[0].wait_recv()
    shares[2].wait_recv()
    partial = jnp.dot(left, wq[...].reshape(512, IN_COLUMNS), preferred_element_type=F32).reshape(QPEERS, TOKENS, IN_COLUMNS)
    ps[...] = jnp.concatenate([partial[:, :, :256], partial[:, :, 256:512]], axis=1).astype(BF16)
    ps2[...] = jnp.concatenate([partial[:, :, 512:640], partial[:, :, 640:]], axis=1).astype(BF16)

    for source, target, left_sem, got_sem in ((ps, pr, p_send, p_recv), (ps2, pr2, p2_send, p2_recv)):

        def send_p(i, carry):
            d = far_first(i)
            pltpu.make_async_remote_copy(
                src_ref=source.at[d],
                dst_ref=target.at[d],
                send_sem=left_sem,
                recv_sem=got_sem,
                device_id=q_peer(QPEERS - d),
                device_id_type=MESH,
            ).start()
            return carry

        lax.fori_loop(0, QPEERS, send_p, 0)
        pending.append(pltpu.make_async_copy(source, source, left_sem).wait)
    ring_advance()
    ring_advance()
    pltpu.make_async_copy(pr, pr, p_recv).wait()
    in_scale = np.float32(1.0 / np.sqrt(np.float32(MODEL_WIDTH)))

    def rotate(raw, count):
        normed = raw * lax.rsqrt(jnp.mean(raw * raw, axis=1, keepdims=True) + norm_epsilon)
        cosines = jnp.concatenate([cosine] * count, axis=0)
        sines = jnp.concatenate([sine] * count, axis=0)
        return normed * cosines + pltpu.roll(normed, HEAD_SIZE // 2, 1) * sines

    both = jnp.sum(pr[...].astype(F32), axis=0) * in_scale
    qh[...] = rotate(jnp.concatenate([both[0:8, 0:128], both[0:8, 128:], both[8:16, 0:128], both[8:16, 128:]], axis=0), QUERY_PER_GROUP)

    scale = HEAD_SIZE ** (-0.5)
    contract_last = (((1,), (1,)), ((), ()))
    q_step = lax.rem(lax.broadcasted_iota(jnp.int32, (16, TOKENS), 0), STEPS)
    k_token = lax.broadcasted_iota(jnp.int32, (16, TOKENS), 1)
    slot = lax.broadcasted_iota(jnp.int32, (16, CACHE_SLOTS), 1)
    loads[6].wait()
    loads[7].wait()
    held = []
    for n in range(2):
        queries = qh[pl.ds(n, 16, stride=2), :].astype(BF16)
        scores = (
            lax.dot_general(queries, keys_v[n * CACHE_SLOTS : (n + 1) * CACHE_SLOTS, :], contract_last, preferred_element_type=F32)
            * scale
        )
        past = jnp.where(slot < lengths[n], jnp.exp(scores), 0.0)
        heads = jnp.dot(
            past.astype(BF16), values_v[n * CACHE_SLOTS : (n + 1) * CACHE_SLOTS, :], preferred_element_type=F32
        )
        held.append((queries, jnp.sum(past, axis=1, keepdims=True), heads))
    pltpu.make_async_copy(pr2, pr2, p2_recv).wait()
    both = jnp.sum(pr2[...].astype(F32), axis=0) * in_scale
    new_keys = rotate(both[0:8], 1).astype(BF16)
    new_values = both[8:16].astype(BF16)
    for n in range(2):
        queries, total, heads = held[n]
        recent = lax.dot_general(queries, new_keys, contract_last, preferred_element_type=F32) * scale
        seen = (lax.rem(k_token, 2) == n) & (lax.div(k_token, 2) <= q_step)
        recent = jnp.where(seen, jnp.exp(recent), 0.0)
        total = total + jnp.sum(recent, axis=1, keepdims=True)
        heads = heads + jnp.dot(recent.astype(BF16), new_values, preferred_element_type=F32)
        hh[pl.ds(n, 16, stride=2), :] = heads / total
    heads = hh[...].astype(BF16)

    os[...] = heads
    orr[0] = heads
    for d in (2, 1, 3):
        copy = pltpu.make_async_remote_copy(
            src_ref=os, dst_ref=orr.at[d], send_sem=o_send.at[d - 1], recv_sem=o_recv.at[d - 1], device_id=y_peer(d), device_id_type=MESH
        )
        copy.start()
        pending.append(copy.wait_send)
    ring_advance()
    for d in range(3):
        pltpu.make_async_copy(os, os, o_recv.at[d]).wait()
    wide = orr[...].astype(F32)
    left = jnp.concatenate([wide[:, 8 * h : 8 * h + 8, :].reshape(32, 128) for h in range(4)], axis=1).astype(BF16)
    out_scale = np.float32(1.0 / np.sqrt(np.float32(KEY_VALUE_HEADS * OUT_COLUMNS)))

    def project(half):
        weights = wo[4 * half : 4 * half + 4].reshape(8 * ROWS, OUT_COLUMNS)
        product = lax.dot_general(left, weights, contract_last, preferred_element_type=F32) * out_scale
        return product.reshape(4, 8, 640)

    for k in RING[:4]:
        to_twin[k].wait_recv()
    attn[...] = project(0)
    for k in RING[4:]:
        to_twin[k].wait_recv()
    s4[...] = jnp.concatenate([attn[...], project(1)], axis=1).astype(BF16)
    for e in (2, 1, 3):
        copy = pltpu.make_async_remote_copy(
            src_ref=s4.at[lax.rem(xx + e, 4)],
            dst_ref=r4.at[e - 1],
            send_sem=r4_send.at[e - 1],
            recv_sem=r4_recv.at[e - 1],
            device_id=x_peer(e),
            device_id_type=MESH,
        )
        copy.start()
        pending.append(copy.wait_send)
    summed = s4[xx].astype(F32)
    for e in range(3):
        pltpu.make_async_copy(s4.at[0], s4.at[0], r4_recv.at[e]).wait()
        summed = summed + r4[e].astype(F32)
    s5[...] = summed.astype(BF16)
    target_y = lax.rem(y + 4 - xx, 4)

    def to_owner(dx, flip):
        return pltpu.make_async_remote_copy(
            src_ref=s5,
            dst_ref=r5.at[t],
            send_sem=r5_send.at[2 * dx + flip],
            recv_sem=r5_recv.at[t],
            device_id=dev(z, target_y, r, lax.rem(xx + dx, 4) * 2 + lax.rem(yh + flip, 2)),
            device_id_type=MESH,
        )

    for dx, flip in ((2, 1), (2, 0), (1, 1), (3, 1), (1, 0), (3, 0), (0, 1)):
        to_owner(dx, flip).start()
        pending.append(to_owner(dx, flip).wait_send)
    pending.append(lambda: pl.when(xx != 0)(to_owner(0, 0).wait_send))

    @pl.when(xx != 0)
    def _():
        to_owner(0, 0).start()

    @pl.when(xx == 0)
    def _():
        pltpu.make_async_copy(s5, r5.at[t], r5_recv.at[t]).start()


    squares = jnp.zeros((TOKENS, 128), F32)
    for xs_ in range(4):
        for i in (2 * xs_, 2 * xs_ + 1):
            pltpu.make_async_copy(s5, r5.at[i], r5_recv.at[i]).wait()
        both = r5[2 * xs_].astype(F32) + r5[2 * xs_ + 1].astype(F32)
        for b in range(8):
            block = widen(both[:, b * ROWS : (b + 1) * ROWS])
            for half in range(2):
                place = xs_ * 16 + half * 8 + b
                residual = block[half * 8 : half * 8 + 8] + xperm[place]
                zblk[place] = residual
                squares = squares + residual * residual
    rscale = lax.rsqrt(jnp.sum(squares, axis=1, keepdims=True) * np.float32(1.0 / MODEL_WIDTH) + norm_epsilon)
    pieces = [zblk[place][:, :ROWS] for place in places]
    mixed_out[...] = (jnp.concatenate(pieces, axis=1) * rscale * post_v[...].reshape(1, 640)).astype(BF16)

    for wait in pending:
        wait()


def finish(master_in, mixed_in, master_out, mixed_out, held, sem):
    write_master = pltpu.make_async_copy(master_in, master_out, sem.at[0])
    write_master.start()
    values = mixed_in[...].astype(F32)
    for s in range(STEPS):
        held[s] = values[2 * s : 2 * s + 2].astype(BF16)
    write_mixed = pltpu.make_async_copy(held, mixed_out, sem.at[1])
    write_mixed.start()
    write_mixed.wait()
    write_master.wait()


def body(
    master, adam_first_moment, adam_second_moment, gradient, resync_order, inputs, in_gain, post_gain, lengths,
    cached_key_rows, cached_value_rows,
):
    half = np.arange(HEAD_SIZE // 2, dtype=np.float64)
    freqs = (rope_theta ** (-(half * 2.0 / HEAD_SIZE))).astype(np.float32)
    freqs = jnp.asarray(np.concatenate([freqs, freqs])[None, :])
    vmem = pl.BlockSpec(memory_space=pltpu.VMEM)
    hbm = pl.BlockSpec(memory_space=pltpu.HBM)
    dma = pltpu.SemaphoreType.DMA
    flat = (ROWS * 10, 128)
    new_master, mixed = pl.pallas_call(
        kernel,
        out_shape=(pltpu.VMEM(flat, F32), pltpu.VMEM((TOKENS, 640), BF16)),
        in_specs=[hbm] * 12,
        out_specs=(vmem, vmem),
        scratch_shapes=[
            pltpu.SMEM((BLOCKS,), jnp.int32),
            pltpu.SMEM((2,), jnp.int32),
            pltpu.VMEM((640,), F32),
            pltpu.VMEM((1, HEAD_SIZE), F32),
            pltpu.VMEM((STEPS, 2, MODEL_WIDTH), BF16),
            pltpu.VMEM((1, MODEL_WIDTH), F32),
            pltpu.VMEM((TOKENS, MODEL_WIDTH), F32),
            pltpu.VMEM((32, HEAD_SIZE), F32),
            pltpu.VMEM((32, HEAD_SIZE), F32),
            pltpu.VMEM((BLOCKS, TOKENS, 128), F32),
            pltpu.VMEM((BLOCKS, TOKENS, 128), F32),
            pltpu.VMEM((BLOCKS, TOKENS, 128), F32),
            pltpu.VMEM((BLOCKS, TOKENS, 128), F32),
            pltpu.VMEM(flat, F32),
            pltpu.VMEM(flat, F32),
            pltpu.VMEM(flat, F32),
            pltpu.VMEM((ROWS, 1280), BF16),
            pltpu.VMEM((2 * CACHE_SLOTS, HEAD_SIZE), BF16),
            pltpu.VMEM((2 * CACHE_SLOTS, HEAD_SIZE), BF16),
            pltpu.VMEM((QPEERS, 32, 128), BF16),
            pltpu.VMEM((QPEERS, 32, 128), BF16),
            pltpu.VMEM((4, 128, IN_COLUMNS), BF16),
            pltpu.VMEM((8, 2, ROWS, OUT_COLUMNS), BF16),
            pltpu.VMEM((QPEERS, 16, 256), BF16),
            pltpu.VMEM((QPEERS, 16, 256), BF16),
            pltpu.VMEM((QPEERS, 16, 128), BF16),
            pltpu.VMEM((QPEERS, 16, 128), BF16),
            pltpu.VMEM((32, 128), BF16),
            pltpu.VMEM((4, 32, 128), BF16),
            pltpu.VMEM((4, 8, 640), F32),
            pltpu.VMEM((4, 16, 640), BF16),
            pltpu.VMEM((3, 16, 640), BF16),
            pltpu.VMEM((16, 640), BF16),
            pltpu.VMEM((8, 16, 640), BF16),
            dma((12,)), dma, dma, dma((3,)), dma((3,)), dma((16,)), dma((16,)), dma((8,)), dma((8,)),
            dma, dma, dma, dma, dma((3,)), dma((3,)), dma((3,)), dma((3,)), dma((8,)), dma((8,)),
        ],
        compiler_params=pltpu.CompilerParams(collective_id=0, has_side_effects=True, vmem_limit_bytes=56 << 20),
        cost_estimate=pl.CostEstimate(flops=400_000_000, bytes_accessed=4_500_000, transcendentals=200_000),
        name="adam_attention",
    )(
        resync_order, lengths, inputs, in_gain.reshape(1, MODEL_WIDTH), post_gain, freqs,
        master.reshape(flat), adam_first_moment.reshape(flat), adam_second_moment.reshape(flat), gradient.reshape(ROWS, 1280),
        cached_key_rows.reshape(2 * CACHE_SLOTS, HEAD_SIZE), cached_value_rows.reshape(2 * CACHE_SLOTS, HEAD_SIZE),
    )
    new_master, mixed = pl.pallas_call(
        finish,
        out_shape=(jax.ShapeDtypeStruct(flat, F32), jax.ShapeDtypeStruct((STEPS, 2, 640), BF16)),
        in_specs=[vmem, vmem],
        out_specs=(hbm, hbm),
        scratch_shapes=[pltpu.VMEM((STEPS, 2, 640), BF16), dma((2,))],
        compiler_params=pltpu.CompilerParams(vmem_limit_bytes=2 << 20),
        name="finish",
    )(pltpu.with_memory_space_constraint(new_master, pltpu.VMEM), pltpu.with_memory_space_constraint(mixed, pltpu.VMEM))
    return new_master.reshape(ROWS, 1, 1280), mixed


def solution(mesh):
    in_specs = (
        P(("learn", "rep"), "tp", None),
        P(("learn", "rep"), "tp", None),
        P(("learn", "rep"), "tp", None),
        P(("learn", "rep"), "tp", None),
        P(),
        P(None, ("learn", "rep"), None),
        P(),
        P("tp"),
        P(("learn", "rep")),
        P(("learn", "rep"), "tp", None, None),
        P(("learn", "rep"), "tp", None, None),
    )
    out_specs = (P(("learn", "rep"), "tp", None), P(None, ("learn", "rep"), "tp"))
    return jax.shard_map(body, mesh=mesh, in_specs=in_specs, out_specs=out_specs, check_vma=False)
```

```python
import functools

import jax
import jax.numpy as jnp
import numpy as np
from jax import lax
from jax.experimental import pallas as pl
from jax.experimental.pallas import tpu as pltpu
from jax.sharding import PartitionSpec as P

MODEL_WIDTH = 5120
HEAD_SIZE = 128
KEY_VALUE_HEADS = 8
QUERY_PER_GROUP = 4
STEPS = 4
CACHE_SLOTS = 2048
BLOCKS = 64
ROWS = 80
IN_COLUMNS = 768
OUT_COLUMNS = 512
TOKENS = 8
RING = (0, 1, 7, 2, 6, 3, 5, 4)
PLACE = tuple(RING.index(k) for k in range(8))
QPEERS = 16

beta_one = 0.9
beta_two = 0.95
adam_rate = 0.05
adam_decay = 0.1
adam_epsilon = 1e-08
correction_one = 1.0 - 0.9**10
correction_two = 1.0 - 0.95**10
norm_epsilon = 1e-06
rope_theta = 1000000.0

MESH = pl.DeviceIdType.MESH
F32 = jnp.float32
BF16 = jnp.bfloat16


def adam_update(master, first, second, gradient):
    first_moment = beta_one * first + (1.0 - beta_one) * gradient
    second_moment = beta_two * second + (1.0 - beta_two) * gradient * gradient
    update = (
        first_moment / correction_one / (jnp.sqrt(second_moment / correction_two) + adam_epsilon)
        + adam_decay * master
    )
    return master - adam_rate * update


def widen(block):
    return jnp.concatenate([block, jnp.zeros((block.shape[0], 128 - ROWS), block.dtype)], axis=1)


def kernel(
    order_in, lengths_in, x_in, gain_in, post_in, freq_in, master_in, first_in, second_in, gradient_in, keys_in, values_in,
    master_out, mixed_out,
    order, lengths, post_v, freq_v, x_v, gain_v, xs, qh, hh, xblk, hblk, xperm, zblk, master_v, first_v, second_v, gradient_v, keys_v, values_v,
    hs, hr, wq, wo, ps, pr, ps2, pr2, os, orr, attn, s4, r4, s5, r5,
    load_sem, h_send, h_recv, wq_send, wq_recv, ring_send, ring_recv, twin_send, twin_recv,
    p_send, p_recv, p2_send, p2_recv, o_send, o_recv, r4_send, r4_recv, r5_send, r5_recv,
):
    l, r, t = lax.axis_index("learn"), lax.axis_index("rep"), lax.axis_index("tp")
    z, y = lax.div(l, 4), lax.rem(l, 4)
    yp, yy = lax.div(y, 2), lax.rem(y, 2)
    c = z * 2 + yp
    xx, yh = lax.div(t, 2), lax.rem(t, 2)

    def dev(z, y, r, t):
        return {"learn": z * 4 + y, "rep": r, "tp": t}

    def q_peer(d):
        other = lax.rem(c + d, QPEERS)
        return dev(lax.div(other, 2), lax.rem(other, 2) * 2 + yy, 1 - r, t)

    twin = dev(z, y, 1 - r, t)
    partner = dev(z, yp * 2 + 1 - yy, 1 - r, t)
    above = dev(lax.rem(z + 1, 8), y, 1 - r, t)
    below = dev(lax.rem(z + 7, 8), y, 1 - r, t)

    def paired(d):
        return lax.rem(yp + lax.div(d, 2), 2) * 2 + lax.rem(yy + lax.rem(d, 2), 2)

    def y_peer(d):
        return dev(z, paired(jnp.int32(d)), r, t)

    def x_peer(e):
        return dev(z, y, r, lax.rem(xx + e, 4) * 2 + yh)

    pending = []

    loads = [
        pltpu.make_async_copy(src, dst, load_sem.at[i])
        for i, (src, dst) in enumerate(
            [
                (x_in, x_v), (gain_in, gain_v), (master_in, master_v), (first_in, first_v), (second_in, second_v),
                (gradient_in, gradient_v), (keys_in, keys_v), (values_in, values_v),
                (order_in, order), (lengths_in, lengths), (post_in, post_v), (freq_in, freq_v),
            ]
        )
    ]
    for i in (0, 1, 8):
        loads[i].start()

    barrier = pltpu.get_barrier_semaphore()

    def greet(device):
        pl.semaphore_signal(barrier, inc=1, device_id=device, device_id_type=MESH)

    def far_first(i):
        return lax.rem(QPEERS // 2 + jnp.where(lax.rem(i, 2) == 1, lax.div(i + 1, 2), -lax.div(i, 2)), QPEERS)

    def greet_q(i, carry):
        greet(q_peer(far_first(i)))
        return carry

    lax.fori_loop(0, QPEERS, greet_q, 0)
    for e in (4, 3, 5, 2, 6, 1, 7, 0):
        there = lax.rem(t + e, 8)
        device = dev(z, paired(lax.div(there, 2)), r, there)
        if e == 0:
            pl.when(xx != 0)(functools.partial(greet, device))
        else:
            greet(device)
    for d in (2, 1, 3):
        greet(y_peer(d))
        greet(x_peer(d))
    for device in (above, below, partner):
        greet(device)
    for i in (2, 3, 4, 5, 6, 7, 9, 10, 11):
        loads[i].start()
    loads[0].wait()
    loads[1].wait()
    loads[8].wait()
    for s in range(STEPS):
        xs[2 * s : 2 * s + 2, :] = x_v[s].astype(F32)
    stream = xs[...]
    rscale = lax.rsqrt(jnp.mean(stream * stream, axis=1, keepdims=True) + norm_epsilon)
    for b in range(BLOCKS):
        block = xs[:, b * ROWS : (b + 1) * ROWS]
        xblk[b] = widen(block)
        hblk[b] = widen(block * rscale * gain_v[:, b * ROWS : (b + 1) * ROWS])
    for d in range(QPEERS):
        other = lax.rem(c + d, QPEERS)
        parts = []
        for m in range(4):
            my, mr = m // 2, m % 2
            w = lax.rem(yy + my, 2) * 2 + lax.rem(1 - r + mr, 2)
            parts.append(hblk[order[other * 4 + w]])
        hs[d] = jnp.concatenate(parts, axis=0).astype(BF16)

    wq[:, ROWS:, :] = jnp.zeros((4, 128 - ROWS, IN_COLUMNS), BF16)
    for i in range(2, 6):
        loads[i].wait()
    for j in range(10):
        rows = pl.ds(j, ROWS, stride=10)
        fresh = adam_update(
            master_v[rows, :], first_v[rows, :], second_v[rows, :], gradient_v[:, j * 128 : (j + 1) * 128].astype(F32)
        )
        master_out[rows, :] = fresh
        if j < 6:
            wq[0, 0:ROWS, j * 128 : (j + 1) * 128] = fresh.astype(BF16)
        else:
            wo[0, 0, :, (j - 6) * 128 : (j - 5) * 128] = fresh.astype(BF16)

    pl.semaphore_wait(barrier, QPEERS + 7 + 6 + 3 + jnp.where(xx != 0, 1, 0))

    def send_h(i, carry):
        d = far_first(i)
        pltpu.make_async_remote_copy(
            src_ref=hs.at[d], dst_ref=hr.at[d], send_sem=h_send, recv_sem=h_recv, device_id=q_peer(d), device_id_type=MESH
        ).start()
        return carry

    lax.fori_loop(0, QPEERS, send_h, 0)
    pending.append(pltpu.make_async_copy(hs, hs, h_send).wait)

    def share(src, dst, device):
        return pltpu.make_async_remote_copy(
            src_ref=wq.at[src, pl.ds(0, ROWS)],
            dst_ref=wq.at[dst, pl.ds(0, ROWS)],
            send_sem=wq_send.at[dst - 1],
            recv_sem=wq_recv.at[dst - 1],
            device_id=device,
            device_id_type=MESH,
        )

    shares = [share(0, 1, twin), share(0, 3, partner), share(3, 2, twin)]
    pending.extend(copy.wait_send for copy in shares)
    shares[1].start()
    shares[0].start()

    parts = (pl.ds(0, 48), pl.ds(48, ROWS - 48))

    def ring(src, dst, index, device, part):
        return pltpu.make_async_remote_copy(
            src_ref=wo.at[PLACE[src], src % 2, parts[part]],
            dst_ref=wo.at[PLACE[dst], dst % 2, parts[part]],
            send_sem=ring_send.at[2 * index + part],
            recv_sem=ring_recv.at[2 * index + part],
            device_id=device,
            device_id_type=MESH,
        )

    up = {(k, part): ring(k, k + 1, k, above, part) for k in range(4) for part in range(2) if (k, part) != (3, 1)}
    down = {(k, part): ring((8 - k) % 8, 7 - k, 4 + k, below, part) for k in range(4) for part in range(2) if (k, part) != (3, 0)}
    to_twin = [
        pltpu.make_async_remote_copy(
            src_ref=wo.at[PLACE[k], k % 2],
            dst_ref=wo.at[PLACE[k], 1 - k % 2],
            send_sem=twin_send.at[k],
            recv_sem=twin_recv.at[k],
            device_id=twin,
            device_id_type=MESH,
        )
        for k in range(8)
    ]
    pending.extend(copy.wait_send for copy in list(up.values()) + list(down.values()) + to_twin)
    ring_step = [0]

    def ring_advance():
        ring_step[0] += 1
        k = ring_step[0]
        for part in range(2):
            for copies in (up, down):
                if (k - 1, part) in copies:
                    copies[k - 1, part].wait_recv()
                if (k, part) in copies:
                    copies[k, part].start()
        to_twin[k].start()
        if k < 4:
            to_twin[8 - k].start()

    for part in range(2):
        up[0, part].start()
        down[0, part].start()
    to_twin[0].start()

    loads[9].wait()
    loads[10].wait()
    loads[11].wait()
    token = lax.broadcasted_iota(jnp.int32, (TOKENS, HEAD_SIZE), 0)
    lane = lax.broadcasted_iota(jnp.int32, (TOKENS, HEAD_SIZE), 1)
    positions = jnp.where(lax.rem(token, 2) == 0, lengths[0], lengths[1]) + lax.div(token, 2)
    angles = positions.astype(F32) * freq_v[...]
    cosine = jnp.cos(angles)
    sine = jnp.sin(angles)
    sine = jnp.where(lane < HEAD_SIZE // 2, -sine, sine)

    def find(j, carry):
        actor = order[j] - t * 8
        return tuple(jnp.where(actor == i, j, carry[i]) for i in range(8))

    stored = lax.fori_loop(0, BLOCKS, find, tuple(jnp.int32(0) for _ in range(8)))
    places = []
    for j in stored:
        k = lax.rem(z + 8 - lax.div(j, 8), 8)
        source = paired(lax.rem(lax.div(j, 2), 4))
        rr = lax.rem(lax.rem(j, 2) + r, 2)
        slot = jnp.int32(0)
        for i in range(1, 8):
            slot = jnp.where(k == RING[i], i, slot)
        places.append(source * 16 + slot * 2 + rr)
    for xs_ in range(4):
        source_y = paired(jnp.int32(xs_))
        for k in range(8):
            for rr in range(2):
                j = (lax.rem(z + 8 - k, 8) * 4 + source_y) * 2 + lax.rem(r + rr, 2)
                xperm[xs_ * 16 + PLACE[k] * 2 + rr] = xblk[order[j]]

    shares[1].wait_recv()
    shares[2].start()

    ring_advance()
    pltpu.make_async_copy(hr, hr, h_recv).wait()
    wide = hr[...].astype(F32)
    left = jnp.concatenate([wide[:, 8 * m : 8 * m + 8, :].reshape(QPEERS * TOKENS, 128) for m in range(4)], axis=1).astype(BF16)
    shares[0].wait_recv()
    shares[2].wait_recv()
    partial = jnp.dot(left, wq[...].reshape(512, IN_COLUMNS), preferred_element_type=F32).reshape(QPEERS, TOKENS, IN_COLUMNS)
    ps[...] = jnp.concatenate([partial[:, :, :256], partial[:, :, 256:512]], axis=1).astype(BF16)
    ps2[...] = jnp.concatenate([partial[:, :, 512:640], partial[:, :, 640:]], axis=1).astype(BF16)

    for source, target, left_sem, got_sem in ((ps, pr, p_send, p_recv), (ps2, pr2, p2_send, p2_recv)):

        def send_p(i, carry):
            d = far_first(i)
            pltpu.make_async_remote_copy(
                src_ref=source.at[d],
                dst_ref=target.at[d],
                send_sem=left_sem,
                recv_sem=got_sem,
                device_id=q_peer(QPEERS - d),
                device_id_type=MESH,
            ).start()
            return carry

        lax.fori_loop(0, QPEERS, send_p, 0)
        pending.append(pltpu.make_async_copy(source, source, left_sem).wait)
    ring_advance()
    ring_advance()
    pltpu.make_async_copy(pr, pr, p_recv).wait()
    in_scale = np.float32(1.0 / np.sqrt(np.float32(MODEL_WIDTH)))

    def rotate(raw, count):
        normed = raw * lax.rsqrt(jnp.mean(raw * raw, axis=1, keepdims=True) + norm_epsilon)
        cosines = jnp.concatenate([cosine] * count, axis=0)
        sines = jnp.concatenate([sine] * count, axis=0)
        return normed * cosines + pltpu.roll(normed, HEAD_SIZE // 2, 1) * sines

    both = jnp.sum(pr[...].astype(F32), axis=0) * in_scale
    qh[...] = rotate(jnp.concatenate([both[0:8, 0:128], both[0:8, 128:], both[8:16, 0:128], both[8:16, 128:]], axis=0), QUERY_PER_GROUP)

    scale = HEAD_SIZE ** (-0.5)
    contract_last = (((1,), (1,)), ((), ()))
    q_step = lax.rem(lax.broadcasted_iota(jnp.int32, (16, TOKENS), 0), STEPS)
    k_token = lax.broadcasted_iota(jnp.int32, (16, TOKENS), 1)
    slot = lax.broadcasted_iota(jnp.int32, (16, CACHE_SLOTS), 1)
    loads[6].wait()
    loads[7].wait()
    held = []
    for n in range(2):
        queries = qh[pl.ds(n, 16, stride=2), :].astype(BF16)
        scores = (
            lax.dot_general(queries, keys_v[n * CACHE_SLOTS : (n + 1) * CACHE_SLOTS, :], contract_last, preferred_element_type=F32)
            * scale
        )
        past = jnp.where(slot < lengths[n], jnp.exp(scores), 0.0)
        heads = jnp.dot(
            past.astype(BF16), values_v[n * CACHE_SLOTS : (n + 1) * CACHE_SLOTS, :], preferred_element_type=F32
        )
        held.append((queries, jnp.sum(past, axis=1, keepdims=True), heads))
    pltpu.make_async_copy(pr2, pr2, p2_recv).wait()
    both = jnp.sum(pr2[...].astype(F32), axis=0) * in_scale
    new_keys = rotate(both[0:8], 1).astype(BF16)
    new_values = both[8:16].astype(BF16)
    for n in range(2):
        queries, total, heads = held[n]
        recent = lax.dot_general(queries, new_keys, contract_last, preferred_element_type=F32) * scale
        seen = (lax.rem(k_token, 2) == n) & (lax.div(k_token, 2) <= q_step)
        recent = jnp.where(seen, jnp.exp(recent), 0.0)
        total = total + jnp.sum(recent, axis=1, keepdims=True)
        heads = heads + jnp.dot(recent.astype(BF16), new_values, preferred_element_type=F32)
        hh[pl.ds(n, 16, stride=2), :] = heads / total
    heads = hh[...].astype(BF16)

    os[...] = heads
    orr[0] = heads
    for d in (2, 1, 3):
        copy = pltpu.make_async_remote_copy(
            src_ref=os, dst_ref=orr.at[d], send_sem=o_send.at[d - 1], recv_sem=o_recv.at[d - 1], device_id=y_peer(d), device_id_type=MESH
        )
        copy.start()
        pending.append(copy.wait_send)
    ring_advance()
    for d in range(3):
        pltpu.make_async_copy(os, os, o_recv.at[d]).wait()
    wide = orr[...].astype(F32)
    left = jnp.concatenate([wide[:, 8 * h : 8 * h + 8, :].reshape(32, 128) for h in range(4)], axis=1).astype(BF16)
    out_scale = np.float32(1.0 / np.sqrt(np.float32(KEY_VALUE_HEADS * OUT_COLUMNS)))

    def project(half):
        weights = wo[4 * half : 4 * half + 4].reshape(8 * ROWS, OUT_COLUMNS)
        product = lax.dot_general(left, weights, contract_last, preferred_element_type=F32) * out_scale
        return product.reshape(4, 8, 640)

    for k in RING[:4]:
        to_twin[k].wait_recv()
    attn[...] = project(0)
    for k in RING[4:]:
        to_twin[k].wait_recv()
    s4[...] = jnp.concatenate([attn[...], project(1)], axis=1).astype(BF16)
    for e in (2, 1, 3):
        copy = pltpu.make_async_remote_copy(
            src_ref=s4.at[lax.rem(xx + e, 4)],
            dst_ref=r4.at[e - 1],
            send_sem=r4_send.at[e - 1],
            recv_sem=r4_recv.at[e - 1],
            device_id=x_peer(e),
            device_id_type=MESH,
        )
        copy.start()
        pending.append(copy.wait_send)
    summed = s4[xx].astype(F32)
    for e in range(3):
        pltpu.make_async_copy(s4.at[0], s4.at[0], r4_recv.at[e]).wait()
        summed = summed + r4[e].astype(F32)
    s5[...] = summed.astype(BF16)
    target_y = paired(xx)

    def to_owner(dx, flip):
        return pltpu.make_async_remote_copy(
            src_ref=s5,
            dst_ref=r5.at[t],
            send_sem=r5_send.at[2 * dx + flip],
            recv_sem=r5_recv.at[t],
            device_id=dev(z, target_y, r, lax.rem(xx + dx, 4) * 2 + lax.rem(yh + flip, 2)),
            device_id_type=MESH,
        )

    for dx, flip in ((2, 1), (2, 0), (1, 1), (3, 1), (1, 0), (3, 0), (0, 1)):
        to_owner(dx, flip).start()
        pending.append(to_owner(dx, flip).wait_send)
    pending.append(lambda: pl.when(xx != 0)(to_owner(0, 0).wait_send))

    @pl.when(xx != 0)
    def _():
        to_owner(0, 0).start()

    @pl.when(xx == 0)
    def _():
        pltpu.make_async_copy(s5, r5.at[t], r5_recv.at[t]).start()


    squares = jnp.zeros((TOKENS, 128), F32)
    for xs_ in range(4):
        for i in (2 * xs_, 2 * xs_ + 1):
            pltpu.make_async_copy(s5, r5.at[i], r5_recv.at[i]).wait()
        both = r5[2 * xs_].astype(F32) + r5[2 * xs_ + 1].astype(F32)
        for b in range(8):
            block = widen(both[:, b * ROWS : (b + 1) * ROWS])
            for half in range(2):
                place = xs_ * 16 + half * 8 + b
                residual = block[half * 8 : half * 8 + 8] + xperm[place]
                zblk[place] = residual
                squares = squares + residual * residual
    rscale = lax.rsqrt(jnp.sum(squares, axis=1, keepdims=True) * np.float32(1.0 / MODEL_WIDTH) + norm_epsilon)
    pieces = [zblk[place][:, :ROWS] for place in places]
    mixed_out[...] = (jnp.concatenate(pieces, axis=1) * rscale * post_v[...].reshape(1, 640)).astype(BF16)

    for wait in pending:
        wait()


def finish(master_in, mixed_in, master_out, mixed_out, held, sem):
    write_master = pltpu.make_async_copy(master_in, master_out, sem.at[0])
    write_master.start()
    values = mixed_in[...].astype(F32)
    for s in range(STEPS):
        held[s] = values[2 * s : 2 * s + 2].astype(BF16)
    write_mixed = pltpu.make_async_copy(held, mixed_out, sem.at[1])
    write_mixed.start()
    write_mixed.wait()
    write_master.wait()


def body(
    master, adam_first_moment, adam_second_moment, gradient, resync_order, inputs, in_gain, post_gain, lengths,
    cached_key_rows, cached_value_rows,
):
    half = np.arange(HEAD_SIZE // 2, dtype=np.float64)
    freqs = (rope_theta ** (-(half * 2.0 / HEAD_SIZE))).astype(np.float32)
    freqs = jnp.asarray(np.concatenate([freqs, freqs])[None, :])
    vmem = pl.BlockSpec(memory_space=pltpu.VMEM)
    hbm = pl.BlockSpec(memory_space=pltpu.HBM)
    dma = pltpu.SemaphoreType.DMA
    flat = (ROWS * 10, 128)
    new_master, mixed = pl.pallas_call(
        kernel,
        out_shape=(pltpu.VMEM(flat, F32), pltpu.VMEM((TOKENS, 640), BF16)),
        in_specs=[hbm] * 12,
        out_specs=(vmem, vmem),
        scratch_shapes=[
            pltpu.SMEM((BLOCKS,), jnp.int32),
            pltpu.SMEM((2,), jnp.int32),
            pltpu.VMEM((640,), F32),
            pltpu.VMEM((1, HEAD_SIZE), F32),
            pltpu.VMEM((STEPS, 2, MODEL_WIDTH), BF16),
            pltpu.VMEM((1, MODEL_WIDTH), F32),
            pltpu.VMEM((TOKENS, MODEL_WIDTH), F32),
            pltpu.VMEM((32, HEAD_SIZE), F32),
            pltpu.VMEM((32, HEAD_SIZE), F32),
            pltpu.VMEM((BLOCKS, TOKENS, 128), F32),
            pltpu.VMEM((BLOCKS, TOKENS, 128), F32),
            pltpu.VMEM((BLOCKS, TOKENS, 128), F32),
            pltpu.VMEM((BLOCKS, TOKENS, 128), F32),
            pltpu.VMEM(flat, F32),
            pltpu.VMEM(flat, F32),
            pltpu.VMEM(flat, F32),
            pltpu.VMEM((ROWS, 1280), BF16),
            pltpu.VMEM((2 * CACHE_SLOTS, HEAD_SIZE), BF16),
            pltpu.VMEM((2 * CACHE_SLOTS, HEAD_SIZE), BF16),
            pltpu.VMEM((QPEERS, 32, 128), BF16),
            pltpu.VMEM((QPEERS, 32, 128), BF16),
            pltpu.VMEM((4, 128, IN_COLUMNS), BF16),
            pltpu.VMEM((8, 2, ROWS, OUT_COLUMNS), BF16),
            pltpu.VMEM((QPEERS, 16, 256), BF16),
            pltpu.VMEM((QPEERS, 16, 256), BF16),
            pltpu.VMEM((QPEERS, 16, 128), BF16),
            pltpu.VMEM((QPEERS, 16, 128), BF16),
            pltpu.VMEM((32, 128), BF16),
            pltpu.VMEM((4, 32, 128), BF16),
            pltpu.VMEM((4, 8, 640), F32),
            pltpu.VMEM((4, 16, 640), BF16),
            pltpu.VMEM((3, 16, 640), BF16),
            pltpu.VMEM((16, 640), BF16),
            pltpu.VMEM((8, 16, 640), BF16),
            dma((12,)), dma, dma, dma((3,)), dma((3,)), dma((16,)), dma((16,)), dma((8,)), dma((8,)),
            dma, dma, dma, dma, dma((3,)), dma((3,)), dma((3,)), dma((3,)), dma((8,)), dma((8,)),
        ],
        compiler_params=pltpu.CompilerParams(collective_id=0, has_side_effects=True, vmem_limit_bytes=56 << 20),
        cost_estimate=pl.CostEstimate(flops=400_000_000, bytes_accessed=4_500_000, transcendentals=200_000),
        name="adam_attention",
    )(
        resync_order, lengths, inputs, in_gain.reshape(1, MODEL_WIDTH), post_gain, freqs,
        master.reshape(flat), adam_first_moment.reshape(flat), adam_second_moment.reshape(flat), gradient.reshape(ROWS, 1280),
        cached_key_rows.reshape(2 * CACHE_SLOTS, HEAD_SIZE), cached_value_rows.reshape(2 * CACHE_SLOTS, HEAD_SIZE),
    )
    new_master, mixed = pl.pallas_call(
        finish,
        out_shape=(jax.ShapeDtypeStruct(flat, F32), jax.ShapeDtypeStruct((STEPS, 2, 640), BF16)),
        in_specs=[vmem, vmem],
        out_specs=(hbm, hbm),
        scratch_shapes=[pltpu.VMEM((STEPS, 2, 640), BF16), dma((2,))],
        compiler_params=pltpu.CompilerParams(vmem_limit_bytes=2 << 20),
        name="finish",
    )(pltpu.with_memory_space_constraint(new_master, pltpu.VMEM), pltpu.with_memory_space_constraint(mixed, pltpu.VMEM))
    return new_master.reshape(ROWS, 1, 1280), mixed


def solution(mesh):
    in_specs = (
        P(("learn", "rep"), "tp", None),
        P(("learn", "rep"), "tp", None),
        P(("learn", "rep"), "tp", None),
        P(("learn", "rep"), "tp", None),
        P(),
        P(None, ("learn", "rep"), None),
        P(),
        P("tp"),
        P(("learn", "rep")),
        P(("learn", "rep"), "tp", None, None),
        P(("learn", "rep"), "tp", None, None),
    )
    out_specs = (P(("learn", "rep"), "tp", None), P(None, ("learn", "rep"), "tp"))
    return jax.shard_map(body, mesh=mesh, in_specs=in_specs, out_specs=out_specs, check_vma=False)
```

```python
import functools

import jax
import jax.numpy as jnp
import numpy as np
from jax import lax
from jax.experimental import pallas as pl
from jax.experimental.pallas import tpu as pltpu
from jax.sharding import PartitionSpec as P

MODEL_WIDTH = 5120
HEAD_SIZE = 128
KEY_VALUE_HEADS = 8
QUERY_PER_GROUP = 4
STEPS = 4
CACHE_SLOTS = 2048
BLOCKS = 64
ROWS = 80
IN_COLUMNS = 768
OUT_COLUMNS = 512
TOKENS = 8
RING = (0, 1, 7, 2, 6, 3, 5, 4)
PLACE = tuple(RING.index(k) for k in range(8))
QPEERS = 16

beta_one = 0.9
beta_two = 0.95
adam_rate = 0.05
adam_decay = 0.1
adam_epsilon = 1e-08
correction_one = 1.0 - 0.9**10
correction_two = 1.0 - 0.95**10
norm_epsilon = 1e-06
rope_theta = 1000000.0

MESH = pl.DeviceIdType.MESH
F32 = jnp.float32
BF16 = jnp.bfloat16


def adam_update(master, first, second, gradient):
    first_moment = beta_one * first + (1.0 - beta_one) * gradient
    second_moment = beta_two * second + (1.0 - beta_two) * gradient * gradient
    update = (
        first_moment / correction_one / (jnp.sqrt(second_moment / correction_two) + adam_epsilon)
        + adam_decay * master
    )
    return master - adam_rate * update


def widen(block):
    return jnp.concatenate([block, jnp.zeros((block.shape[0], 128 - ROWS), block.dtype)], axis=1)


def kernel(
    order_in, lengths_in, x_in, gain_in, post_in, freq_in, master_in, first_in, second_in, gradient_in, keys_in, values_in,
    master_out, mixed_out,
    order, lengths, post_v, freq_v, x_v, gain_v, xs, qh, hh, xblk, hblk, xperm, zblk, master_v, first_v, second_v, gradient_v, keys_v, values_v,
    hs, hr, wq, wo, ps, pr, ps2, pr2, os, orr, attn, s4, r4, s5, r5,
    load_sem, h_send, h_recv, wq_send, wq_recv, ring_send, ring_recv, twin_send, twin_recv,
    p_send, p_recv, p2_send, p2_recv, o_send, o_recv, r4_send, r4_recv, r5_send, r5_recv,
):
    l, r, t = lax.axis_index("learn"), lax.axis_index("rep"), lax.axis_index("tp")
    z, y = lax.div(l, 4), lax.rem(l, 4)
    yp, yy = lax.div(y, 2), lax.rem(y, 2)
    c = z * 2 + yp
    xx, yh = lax.div(t, 2), lax.rem(t, 2)

    def dev(z, y, r, t):
        return {"learn": z * 4 + y, "rep": r, "tp": t}

    def q_peer(d):
        other = lax.rem(c + d, QPEERS)
        return dev(lax.div(other, 2), lax.rem(other, 2) * 2 + yy, 1 - r, t)

    twin = dev(z, y, 1 - r, t)
    partner = dev(z, yp * 2 + 1 - yy, 1 - r, t)
    above = dev(lax.rem(z + 1, 8), y, 1 - r, t)
    below = dev(lax.rem(z + 7, 8), y, 1 - r, t)

    def paired(d):
        return lax.rem(yp + lax.div(d, 2), 2) * 2 + lax.rem(yy + lax.rem(d, 2), 2)

    def y_peer(d):
        return dev(z, paired(jnp.int32(d)), r, t)

    def x_peer(e):
        return dev(z, y, r, lax.rem(xx + e, 4) * 2 + yh)

    pending = []

    loads = [
        pltpu.make_async_copy(src, dst, load_sem.at[i])
        for i, (src, dst) in enumerate(
            [
                (x_in, x_v), (gain_in, gain_v), (master_in, master_v), (first_in, first_v), (second_in, second_v),
                (gradient_in, gradient_v), (keys_in, keys_v), (values_in, values_v),
                (order_in, order), (lengths_in, lengths), (post_in, post_v), (freq_in, freq_v),
            ]
        )
    ]
    for i in (0, 1, 8):
        loads[i].start()

    barrier = pltpu.get_barrier_semaphore()

    def greet(device):
        pl.semaphore_signal(barrier, inc=1, device_id=device, device_id_type=MESH)

    far_first = [(QPEERS // 2 + ((i + 1) // 2 if i % 2 else -(i // 2))) % QPEERS for i in range(QPEERS)]

    for d in far_first:
        greet(q_peer(d))
    for e in (4, 3, 5, 2, 6, 1, 7, 0):
        there = lax.rem(t + e, 8)
        device = dev(z, paired(lax.div(there, 2)), r, there)
        if e == 0:
            pl.when(xx != 0)(functools.partial(greet, device))
        else:
            greet(device)
    for d in (2, 1, 3):
        greet(y_peer(d))
        greet(x_peer(d))
    for device in (above, below, partner):
        greet(device)
    for i in (2, 3, 4, 5, 6, 7, 9, 10, 11):
        loads[i].start()
    loads[0].wait()
    loads[1].wait()
    loads[8].wait()
    for s in range(STEPS):
        xs[2 * s : 2 * s + 2, :] = x_v[s].astype(F32)
    stream = xs[...]
    rscale = lax.rsqrt(jnp.mean(stream * stream, axis=1, keepdims=True) + norm_epsilon)
    for b in range(BLOCKS):
        block = xs[:, b * ROWS : (b + 1) * ROWS]
        xblk[b] = widen(block)
        hblk[b] = widen(block * rscale * gain_v[:, b * ROWS : (b + 1) * ROWS])
    for d in range(QPEERS):
        other = lax.rem(c + d, QPEERS)
        parts = []
        for m in range(4):
            my, mr = m // 2, m % 2
            w = lax.rem(yy + my, 2) * 2 + lax.rem(1 - r + mr, 2)
            parts.append(hblk[order[other * 4 + w]])
        hs[d] = jnp.concatenate(parts, axis=0).astype(BF16)

    wq[:, ROWS:, :] = jnp.zeros((4, 128 - ROWS, IN_COLUMNS), BF16)
    for i in range(2, 6):
        loads[i].wait()
    for j in range(10):
        rows = pl.ds(j, ROWS, stride=10)
        fresh = adam_update(
            master_v[rows, :], first_v[rows, :], second_v[rows, :], gradient_v[:, j * 128 : (j + 1) * 128].astype(F32)
        )
        master_out[rows, :] = fresh
        if j < 6:
            wq[0, 0:ROWS, j * 128 : (j + 1) * 128] = fresh.astype(BF16)
        else:
            wo[0, 0, :, (j - 6) * 128 : (j - 5) * 128] = fresh.astype(BF16)

    pl.semaphore_wait(barrier, QPEERS + 7 + 6 + 3 + jnp.where(xx != 0, 1, 0))

    for d in far_first:
        pltpu.make_async_remote_copy(
            src_ref=hs.at[d], dst_ref=hr.at[d], send_sem=h_send, recv_sem=h_recv, device_id=q_peer(d), device_id_type=MESH
        ).start()
    pending.append(pltpu.make_async_copy(hs, hs, h_send).wait)

    def share(src, dst, device):
        return pltpu.make_async_remote_copy(
            src_ref=wq.at[src, pl.ds(0, ROWS)],
            dst_ref=wq.at[dst, pl.ds(0, ROWS)],
            send_sem=wq_send.at[dst - 1],
            recv_sem=wq_recv.at[dst - 1],
            device_id=device,
            device_id_type=MESH,
        )

    shares = [share(0, 1, twin), share(0, 3, partner), share(3, 2, twin)]
    pending.extend(copy.wait_send for copy in shares)
    shares[1].start()
    shares[0].start()

    parts = (pl.ds(0, 48), pl.ds(48, ROWS - 48))

    def ring(src, dst, index, device, part):
        return pltpu.make_async_remote_copy(
            src_ref=wo.at[PLACE[src], src % 2, parts[part]],
            dst_ref=wo.at[PLACE[dst], dst % 2, parts[part]],
            send_sem=ring_send.at[2 * index + part],
            recv_sem=ring_recv.at[2 * index + part],
            device_id=device,
            device_id_type=MESH,
        )

    up = {(k, part): ring(k, k + 1, k, above, part) for k in range(4) for part in range(2) if (k, part) != (3, 1)}
    down = {(k, part): ring((8 - k) % 8, 7 - k, 4 + k, below, part) for k in range(4) for part in range(2) if (k, part) != (3, 0)}
    to_twin = [
        pltpu.make_async_remote_copy(
            src_ref=wo.at[PLACE[k], k % 2],
            dst_ref=wo.at[PLACE[k], 1 - k % 2],
            send_sem=twin_send.at[k],
            recv_sem=twin_recv.at[k],
            device_id=twin,
            device_id_type=MESH,
        )
        for k in range(8)
    ]
    pending.extend(copy.wait_send for copy in list(up.values()) + list(down.values()) + to_twin)
    ring_step = [0]

    def ring_advance():
        ring_step[0] += 1
        k = ring_step[0]
        for part in range(2):
            for copies in (up, down):
                if (k - 1, part) in copies:
                    copies[k - 1, part].wait_recv()
                if (k, part) in copies:
                    copies[k, part].start()
        to_twin[k].start()
        if k < 4:
            to_twin[8 - k].start()

    for part in range(2):
        up[0, part].start()
        down[0, part].start()
    to_twin[0].start()

    loads[9].wait()
    loads[10].wait()
    loads[11].wait()
    token = lax.broadcasted_iota(jnp.int32, (TOKENS, HEAD_SIZE), 0)
    lane = lax.broadcasted_iota(jnp.int32, (TOKENS, HEAD_SIZE), 1)
    positions = jnp.where(lax.rem(token, 2) == 0, lengths[0], lengths[1]) + lax.div(token, 2)
    angles = positions.astype(F32) * freq_v[...]
    cosine = jnp.cos(angles)
    sine = jnp.sin(angles)
    sine = jnp.where(lane < HEAD_SIZE // 2, -sine, sine)

    def find(j, carry):
        actor = order[j] - t * 8
        return tuple(jnp.where(actor == i, j, carry[i]) for i in range(8))

    stored = lax.fori_loop(0, BLOCKS, find, tuple(jnp.int32(0) for _ in range(8)))
    places = []
    for j in stored:
        k = lax.rem(z + 8 - lax.div(j, 8), 8)
        source = paired(lax.rem(lax.div(j, 2), 4))
        rr = lax.rem(lax.rem(j, 2) + r, 2)
        slot = jnp.int32(0)
        for i in range(1, 8):
            slot = jnp.where(k == RING[i], i, slot)
        places.append(source * 16 + slot * 2 + rr)
    for xs_ in range(4):
        source_y = paired(jnp.int32(xs_))
        for k in range(8):
            for rr in range(2):
                j = (lax.rem(z + 8 - k, 8) * 4 + source_y) * 2 + lax.rem(r + rr, 2)
                xperm[xs_ * 16 + PLACE[k] * 2 + rr] = xblk[order[j]]

    shares[1].wait_recv()
    shares[2].start()

    ring_advance()
    pltpu.make_async_copy(hr, hr, h_recv).wait()
    wide = hr[...].astype(F32)
    left = jnp.concatenate([wide[:, 8 * m : 8 * m + 8, :].reshape(QPEERS * TOKENS, 128) for m in range(4)], axis=1).astype(BF16)
    shares[0].wait_recv()
    shares[2].wait_recv()
    partial = jnp.dot(left, wq[...].reshape(512, IN_COLUMNS), preferred_element_type=F32).reshape(QPEERS, TOKENS, IN_COLUMNS)
    ps[...] = jnp.concatenate([partial[:, :, :256], partial[:, :, 256:512]], axis=1).astype(BF16)
    ps2[...] = jnp.concatenate([partial[:, :, 512:640], partial[:, :, 640:]], axis=1).astype(BF16)

    for source, target, left_sem, got_sem in ((ps, pr, p_send, p_recv), (ps2, pr2, p2_send, p2_recv)):
        for d in far_first:
            pltpu.make_async_remote_copy(
                src_ref=source.at[d],
                dst_ref=target.at[d],
                send_sem=left_sem,
                recv_sem=got_sem,
                device_id=q_peer(QPEERS - d),
                device_id_type=MESH,
            ).start()
        pending.append(pltpu.make_async_copy(source, source, left_sem).wait)
    ring_advance()
    ring_advance()
    pltpu.make_async_copy(pr, pr, p_recv).wait()
    in_scale = np.float32(1.0 / np.sqrt(np.float32(MODEL_WIDTH)))

    def rotate(raw, count):
        normed = raw * lax.rsqrt(jnp.mean(raw * raw, axis=1, keepdims=True) + norm_epsilon)
        cosines = jnp.concatenate([cosine] * count, axis=0)
        sines = jnp.concatenate([sine] * count, axis=0)
        return normed * cosines + pltpu.roll(normed, HEAD_SIZE // 2, 1) * sines

    both = jnp.sum(pr[...].astype(F32), axis=0) * in_scale
    qh[...] = rotate(jnp.concatenate([both[0:8, 0:128], both[0:8, 128:], both[8:16, 0:128], both[8:16, 128:]], axis=0), QUERY_PER_GROUP)

    scale = HEAD_SIZE ** (-0.5)
    contract_last = (((1,), (1,)), ((), ()))
    q_step = lax.rem(lax.broadcasted_iota(jnp.int32, (16, TOKENS), 0), STEPS)
    k_token = lax.broadcasted_iota(jnp.int32, (16, TOKENS), 1)
    slot = lax.broadcasted_iota(jnp.int32, (16, CACHE_SLOTS), 1)
    loads[6].wait()
    loads[7].wait()
    held = []
    for n in range(2):
        queries = qh[pl.ds(n, 16, stride=2), :].astype(BF16)
        scores = (
            lax.dot_general(queries, keys_v[n * CACHE_SLOTS : (n + 1) * CACHE_SLOTS, :], contract_last, preferred_element_type=F32)
            * scale
        )
        past = jnp.where(slot < lengths[n], jnp.exp(scores), 0.0)
        heads = jnp.dot(
            past.astype(BF16), values_v[n * CACHE_SLOTS : (n + 1) * CACHE_SLOTS, :], preferred_element_type=F32
        )
        held.append((queries, jnp.sum(past, axis=1, keepdims=True), heads))
    pltpu.make_async_copy(pr2, pr2, p2_recv).wait()
    both = jnp.sum(pr2[...].astype(F32), axis=0) * in_scale
    new_keys = rotate(both[0:8], 1).astype(BF16)
    new_values = both[8:16].astype(BF16)
    for n in range(2):
        queries, total, heads = held[n]
        recent = lax.dot_general(queries, new_keys, contract_last, preferred_element_type=F32) * scale
        seen = (lax.rem(k_token, 2) == n) & (lax.div(k_token, 2) <= q_step)
        recent = jnp.where(seen, jnp.exp(recent), 0.0)
        total = total + jnp.sum(recent, axis=1, keepdims=True)
        heads = heads + jnp.dot(recent.astype(BF16), new_values, preferred_element_type=F32)
        hh[pl.ds(n, 16, stride=2), :] = heads / total
    heads = hh[...].astype(BF16)

    os[...] = heads
    orr[0] = heads
    for d in (2, 1, 3):
        copy = pltpu.make_async_remote_copy(
            src_ref=os, dst_ref=orr.at[d], send_sem=o_send.at[d - 1], recv_sem=o_recv.at[d - 1], device_id=y_peer(d), device_id_type=MESH
        )
        copy.start()
        pending.append(copy.wait_send)
    ring_advance()
    for d in range(3):
        pltpu.make_async_copy(os, os, o_recv.at[d]).wait()
    wide = orr[...].astype(F32)
    left = jnp.concatenate([wide[:, 8 * h : 8 * h + 8, :].reshape(32, 128) for h in range(4)], axis=1).astype(BF16)
    out_scale = np.float32(1.0 / np.sqrt(np.float32(KEY_VALUE_HEADS * OUT_COLUMNS)))

    def project(half):
        weights = wo[4 * half : 4 * half + 4].reshape(8 * ROWS, OUT_COLUMNS)
        product = lax.dot_general(left, weights, contract_last, preferred_element_type=F32) * out_scale
        return product.reshape(4, 8, 640)

    for k in RING[:4]:
        to_twin[k].wait_recv()
    attn[...] = project(0)
    for k in RING[4:]:
        to_twin[k].wait_recv()
    s4[...] = jnp.concatenate([attn[...], project(1)], axis=1).astype(BF16)
    for e in (2, 1, 3):
        copy = pltpu.make_async_remote_copy(
            src_ref=s4.at[lax.rem(xx + e, 4)],
            dst_ref=r4.at[e - 1],
            send_sem=r4_send.at[e - 1],
            recv_sem=r4_recv.at[e - 1],
            device_id=x_peer(e),
            device_id_type=MESH,
        )
        copy.start()
        pending.append(copy.wait_send)
    summed = s4[xx].astype(F32)
    for e in range(3):
        pltpu.make_async_copy(s4.at[0], s4.at[0], r4_recv.at[e]).wait()
        summed = summed + r4[e].astype(F32)
    s5[...] = summed.astype(BF16)
    target_y = paired(xx)

    def to_owner(dx, flip):
        return pltpu.make_async_remote_copy(
            src_ref=s5,
            dst_ref=r5.at[t],
            send_sem=r5_send.at[2 * dx + flip],
            recv_sem=r5_recv.at[t],
            device_id=dev(z, target_y, r, lax.rem(xx + dx, 4) * 2 + lax.rem(yh + flip, 2)),
            device_id_type=MESH,
        )

    for dx, flip in ((2, 1), (2, 0), (1, 1), (3, 1), (1, 0), (3, 0), (0, 1)):
        to_owner(dx, flip).start()
        pending.append(to_owner(dx, flip).wait_send)
    pending.append(lambda: pl.when(xx != 0)(to_owner(0, 0).wait_send))

    @pl.when(xx != 0)
    def _():
        to_owner(0, 0).start()

    @pl.when(xx == 0)
    def _():
        pltpu.make_async_copy(s5, r5.at[t], r5_recv.at[t]).start()


    squares = jnp.zeros((TOKENS, 128), F32)
    for xs_ in range(4):
        for i in (2 * xs_, 2 * xs_ + 1):
            pltpu.make_async_copy(s5, r5.at[i], r5_recv.at[i]).wait()
        both = r5[2 * xs_].astype(F32) + r5[2 * xs_ + 1].astype(F32)
        for b in range(8):
            block = widen(both[:, b * ROWS : (b + 1) * ROWS])
            for half in range(2):
                place = xs_ * 16 + half * 8 + b
                residual = block[half * 8 : half * 8 + 8] + xperm[place]
                zblk[place] = residual
                squares = squares + residual * residual
    rscale = lax.rsqrt(jnp.sum(squares, axis=1, keepdims=True) * np.float32(1.0 / MODEL_WIDTH) + norm_epsilon)
    pieces = [zblk[place][:, :ROWS] for place in places]
    mixed_out[...] = (jnp.concatenate(pieces, axis=1) * rscale * post_v[...].reshape(1, 640)).astype(BF16)

    for wait in pending:
        wait()


def finish(master_in, mixed_in, master_out, mixed_out, held, sem):
    write_master = pltpu.make_async_copy(master_in, master_out, sem.at[0])
    write_master.start()
    values = mixed_in[...].astype(F32)
    for s in range(STEPS):
        held[s] = values[2 * s : 2 * s + 2].astype(BF16)
    write_mixed = pltpu.make_async_copy(held, mixed_out, sem.at[1])
    write_mixed.start()
    write_mixed.wait()
    write_master.wait()


def body(
    master, adam_first_moment, adam_second_moment, gradient, resync_order, inputs, in_gain, post_gain, lengths,
    cached_key_rows, cached_value_rows,
):
    half = np.arange(HEAD_SIZE // 2, dtype=np.float64)
    freqs = (rope_theta ** (-(half * 2.0 / HEAD_SIZE))).astype(np.float32)
    freqs = jnp.asarray(np.concatenate([freqs, freqs])[None, :])
    vmem = pl.BlockSpec(memory_space=pltpu.VMEM)
    hbm = pl.BlockSpec(memory_space=pltpu.HBM)
    dma = pltpu.SemaphoreType.DMA
    flat = (ROWS * 10, 128)
    new_master, mixed = pl.pallas_call(
        kernel,
        out_shape=(pltpu.VMEM(flat, F32), pltpu.VMEM((TOKENS, 640), BF16)),
        in_specs=[hbm] * 12,
        out_specs=(vmem, vmem),
        scratch_shapes=[
            pltpu.SMEM((BLOCKS,), jnp.int32),
            pltpu.SMEM((2,), jnp.int32),
            pltpu.VMEM((640,), F32),
            pltpu.VMEM((1, HEAD_SIZE), F32),
            pltpu.VMEM((STEPS, 2, MODEL_WIDTH), BF16),
            pltpu.VMEM((1, MODEL_WIDTH), F32),
            pltpu.VMEM((TOKENS, MODEL_WIDTH), F32),
            pltpu.VMEM((32, HEAD_SIZE), F32),
            pltpu.VMEM((32, HEAD_SIZE), F32),
            pltpu.VMEM((BLOCKS, TOKENS, 128), F32),
            pltpu.VMEM((BLOCKS, TOKENS, 128), F32),
            pltpu.VMEM((BLOCKS, TOKENS, 128), F32),
            pltpu.VMEM((BLOCKS, TOKENS, 128), F32),
            pltpu.VMEM(flat, F32),
            pltpu.VMEM(flat, F32),
            pltpu.VMEM(flat, F32),
            pltpu.VMEM((ROWS, 1280), BF16),
            pltpu.VMEM((2 * CACHE_SLOTS, HEAD_SIZE), BF16),
            pltpu.VMEM((2 * CACHE_SLOTS, HEAD_SIZE), BF16),
            pltpu.VMEM((QPEERS, 32, 128), BF16),
            pltpu.VMEM((QPEERS, 32, 128), BF16),
            pltpu.VMEM((4, 128, IN_COLUMNS), BF16),
            pltpu.VMEM((8, 2, ROWS, OUT_COLUMNS), BF16),
            pltpu.VMEM((QPEERS, 16, 256), BF16),
            pltpu.VMEM((QPEERS, 16, 256), BF16),
            pltpu.VMEM((QPEERS, 16, 128), BF16),
            pltpu.VMEM((QPEERS, 16, 128), BF16),
            pltpu.VMEM((32, 128), BF16),
            pltpu.VMEM((4, 32, 128), BF16),
            pltpu.VMEM((4, 8, 640), F32),
            pltpu.VMEM((4, 16, 640), BF16),
            pltpu.VMEM((3, 16, 640), BF16),
            pltpu.VMEM((16, 640), BF16),
            pltpu.VMEM((8, 16, 640), BF16),
            dma((12,)), dma, dma, dma((3,)), dma((3,)), dma((16,)), dma((16,)), dma((8,)), dma((8,)),
            dma, dma, dma, dma, dma((3,)), dma((3,)), dma((3,)), dma((3,)), dma((8,)), dma((8,)),
        ],
        compiler_params=pltpu.CompilerParams(collective_id=0, has_side_effects=True, vmem_limit_bytes=56 << 20),
        cost_estimate=pl.CostEstimate(flops=400_000_000, bytes_accessed=4_500_000, transcendentals=200_000),
        name="adam_attention",
    )(
        resync_order, lengths, inputs, in_gain.reshape(1, MODEL_WIDTH), post_gain, freqs,
        master.reshape(flat), adam_first_moment.reshape(flat), adam_second_moment.reshape(flat), gradient.reshape(ROWS, 1280),
        cached_key_rows.reshape(2 * CACHE_SLOTS, HEAD_SIZE), cached_value_rows.reshape(2 * CACHE_SLOTS, HEAD_SIZE),
    )
    new_master, mixed = pl.pallas_call(
        finish,
        out_shape=(jax.ShapeDtypeStruct(flat, F32), jax.ShapeDtypeStruct((STEPS, 2, 640), BF16)),
        in_specs=[vmem, vmem],
        out_specs=(hbm, hbm),
        scratch_shapes=[pltpu.VMEM((STEPS, 2, 640), BF16), dma((2,))],
        compiler_params=pltpu.CompilerParams(vmem_limit_bytes=2 << 20),
        name="finish",
    )(pltpu.with_memory_space_constraint(new_master, pltpu.VMEM), pltpu.with_memory_space_constraint(mixed, pltpu.VMEM))
    return new_master.reshape(ROWS, 1, 1280), mixed


def solution(mesh):
    in_specs = (
        P(("learn", "rep"), "tp", None),
        P(("learn", "rep"), "tp", None),
        P(("learn", "rep"), "tp", None),
        P(("learn", "rep"), "tp", None),
        P(),
        P(None, ("learn", "rep"), None),
        P(),
        P("tp"),
        P(("learn", "rep")),
        P(("learn", "rep"), "tp", None, None),
        P(("learn", "rep"), "tp", None, None),
    )
    out_specs = (P(("learn", "rep"), "tp", None), P(None, ("learn", "rep"), "tp"))
    return jax.shard_map(body, mesh=mesh, in_specs=in_specs, out_specs=out_specs, check_vma=False)
```

```python
import functools

import jax
import jax.numpy as jnp
import numpy as np
from jax import lax
from jax.experimental import pallas as pl
from jax.experimental.pallas import tpu as pltpu
from jax.sharding import PartitionSpec as P

MODEL_WIDTH = 5120
HEAD_SIZE = 128
KEY_VALUE_HEADS = 8
QUERY_PER_GROUP = 4
STEPS = 4
CACHE_SLOTS = 2048
BLOCKS = 64
ROWS = 80
IN_COLUMNS = 768
OUT_COLUMNS = 512
TOKENS = 8
RING = (0, 1, 7, 2, 6, 3, 5, 4)
PLACE = tuple(RING.index(k) for k in range(8))
QPEERS = 16

beta_one = 0.9
beta_two = 0.95
adam_rate = 0.05
adam_decay = 0.1
adam_epsilon = 1e-08
correction_one = 1.0 - 0.9**10
correction_two = 1.0 - 0.95**10
norm_epsilon = 1e-06
rope_theta = 1000000.0

MESH = pl.DeviceIdType.MESH
F32 = jnp.float32
BF16 = jnp.bfloat16


def adam_update(master, first, second, gradient):
    first_moment = beta_one * first + (1.0 - beta_one) * gradient
    second_moment = beta_two * second + (1.0 - beta_two) * gradient * gradient
    update = (
        first_moment / correction_one / (jnp.sqrt(second_moment / correction_two) + adam_epsilon)
        + adam_decay * master
    )
    return master - adam_rate * update


def widen(block):
    return jnp.concatenate([block, jnp.zeros((block.shape[0], 128 - ROWS), block.dtype)], axis=1)


def kernel(
    order_in, lengths_in, x_in, gain_in, post_in, freq_in, master_in, first_in, second_in, gradient_in, keys_in, values_in,
    master_out, mixed_out,
    order, lengths, post_v, freq_v, x_v, gain_v, xs, qh, hh, xblk, hblk, xperm, zblk, master_v, first_v, second_v, gradient_v, keys_v, values_v,
    hs, hr, wq, wo, ps, pr, ps2, pr2, os, orr, attn, s4, r4, s5, r5,
    load_sem, h_send, h_recv, wq_send, wq_recv, ring_send, ring_recv, twin_send, twin_recv,
    p_send, p_recv, p2_send, p2_recv, o_send, o_recv, r4_send, r4_recv, r5_send, r5_recv,
):
    l, r, t = lax.axis_index("learn"), lax.axis_index("rep"), lax.axis_index("tp")
    z, y = lax.div(l, 4), lax.rem(l, 4)
    yp, yy = lax.div(y, 2), lax.rem(y, 2)
    c = z * 2 + yp
    xx, yh = lax.div(t, 2), lax.rem(t, 2)

    def dev(z, y, r, t):
        return {"learn": z * 4 + y, "rep": r, "tp": t}

    def q_peer(d):
        other = lax.rem(c + d, QPEERS)
        return dev(lax.div(other, 2), lax.rem(other, 2) * 2 + yy, 1 - r, t)

    twin = dev(z, y, 1 - r, t)
    partner = dev(z, yp * 2 + 1 - yy, 1 - r, t)
    above = dev(lax.rem(z + 1, 8), y, 1 - r, t)
    below = dev(lax.rem(z + 7, 8), y, 1 - r, t)

    def paired(d):
        return lax.rem(yp + lax.div(d, 2), 2) * 2 + lax.rem(yy + lax.rem(d, 2), 2)

    def y_peer(d):
        return dev(z, paired(jnp.int32(d)), r, t)

    def x_peer(e):
        return dev(z, y, r, lax.rem(xx + e, 4) * 2 + yh)

    pending = []

    loads = [
        pltpu.make_async_copy(src, dst, load_sem.at[i])
        for i, (src, dst) in enumerate(
            [
                (x_in, x_v), (gain_in, gain_v), (master_in, master_v), (first_in, first_v), (second_in, second_v),
                (gradient_in, gradient_v), (keys_in, keys_v), (values_in, values_v),
                (order_in, order), (lengths_in, lengths), (post_in, post_v), (freq_in, freq_v),
            ]
        )
    ]
    for i in (0, 1, 8):
        loads[i].start()

    barrier = pltpu.get_barrier_semaphore()

    def greet(device):
        pl.semaphore_signal(barrier, inc=1, device_id=device, device_id_type=MESH)

    far_first = [(QPEERS // 2 + ((i + 1) // 2 if i % 2 else -(i // 2))) % QPEERS for i in range(QPEERS)]

    for d in far_first:
        greet(q_peer(d))
    for e in (4, 3, 5, 2, 6, 1, 7, 0):
        there = lax.rem(t + e, 8)
        device = dev(z, paired(lax.div(there, 2)), r, there)
        if e == 0:
            pl.when(xx != 0)(functools.partial(greet, device))
        else:
            greet(device)
    for d in (2, 1, 3):
        greet(y_peer(d))
        greet(x_peer(d))
    for device in (above, below, partner):
        greet(device)
    for i in (2, 3, 4, 5, 6, 7, 9, 10, 11):
        loads[i].start()
    loads[0].wait()
    loads[1].wait()
    loads[8].wait()
    for s in range(STEPS):
        xs[2 * s : 2 * s + 2, :] = x_v[s].astype(F32)
    stream = xs[...]
    rscale = lax.rsqrt(jnp.mean(stream * stream, axis=1, keepdims=True) + norm_epsilon)
    for b in range(BLOCKS):
        block = xs[:, b * ROWS : (b + 1) * ROWS]
        xblk[b] = widen(block)
        hblk[b] = widen(block * rscale * gain_v[:, b * ROWS : (b + 1) * ROWS])
    for d in range(QPEERS):
        other = lax.rem(c + d, QPEERS)
        parts = []
        for m in range(4):
            my, mr = m // 2, m % 2
            w = lax.rem(yy + my, 2) * 2 + lax.rem(1 - r + mr, 2)
            parts.append(hblk[order[other * 4 + w]])
        hs[d] = jnp.concatenate(parts, axis=0).astype(BF16)

    wq[:, ROWS:, :] = jnp.zeros((4, 128 - ROWS, IN_COLUMNS), BF16)
    for i in range(2, 6):
        loads[i].wait()
    for j in range(10):
        rows = pl.ds(j, ROWS, stride=10)
        fresh = adam_update(
            master_v[rows, :], first_v[rows, :], second_v[rows, :], gradient_v[:, j * 128 : (j + 1) * 128].astype(F32)
        )
        master_out[rows, :] = fresh
        if j < 6:
            wq[0, 0:ROWS, j * 128 : (j + 1) * 128] = fresh.astype(BF16)
        else:
            wo[0, 0, :, (j - 6) * 128 : (j - 5) * 128] = fresh.astype(BF16)

    pl.semaphore_wait(barrier, QPEERS + 7 + 6 + 3 + jnp.where(xx != 0, 1, 0))

    def send_h(ds):
        for d in ds:
            pltpu.make_async_remote_copy(
                src_ref=hs.at[d], dst_ref=hr.at[d], send_sem=h_send, recv_sem=h_recv, device_id=q_peer(d), device_id_type=MESH
            ).start()

    send_h(far_first[:9])
    pending.append(pltpu.make_async_copy(hs, hs, h_send).wait)

    def share(src, dst, device):
        return pltpu.make_async_remote_copy(
            src_ref=wq.at[src, pl.ds(0, ROWS)],
            dst_ref=wq.at[dst, pl.ds(0, ROWS)],
            send_sem=wq_send.at[dst - 1],
            recv_sem=wq_recv.at[dst - 1],
            device_id=device,
            device_id_type=MESH,
        )

    shares = [share(0, 1, twin), share(0, 3, partner), share(3, 2, twin)]
    pending.extend(copy.wait_send for copy in shares)
    shares[1].start()
    shares[0].start()

    parts = (pl.ds(0, 48), pl.ds(48, ROWS - 48))

    def ring(src, dst, index, device, part):
        return pltpu.make_async_remote_copy(
            src_ref=wo.at[PLACE[src], src % 2, parts[part]],
            dst_ref=wo.at[PLACE[dst], dst % 2, parts[part]],
            send_sem=ring_send.at[2 * index + part],
            recv_sem=ring_recv.at[2 * index + part],
            device_id=device,
            device_id_type=MESH,
        )

    up = {(k, part): ring(k, k + 1, k, above, part) for k in range(4) for part in range(2) if (k, part) != (3, 1)}
    down = {(k, part): ring((8 - k) % 8, 7 - k, 4 + k, below, part) for k in range(4) for part in range(2) if (k, part) != (3, 0)}
    to_twin = [
        pltpu.make_async_remote_copy(
            src_ref=wo.at[PLACE[k], k % 2],
            dst_ref=wo.at[PLACE[k], 1 - k % 2],
            send_sem=twin_send.at[k],
            recv_sem=twin_recv.at[k],
            device_id=twin,
            device_id_type=MESH,
        )
        for k in range(8)
    ]
    pending.extend(copy.wait_send for copy in list(up.values()) + list(down.values()) + to_twin)
    ring_step = [0]

    def ring_advance():
        ring_step[0] += 1
        k = ring_step[0]
        for part in range(2):
            for copies in (up, down):
                if (k - 1, part) in copies:
                    copies[k - 1, part].wait_recv()
                if (k, part) in copies:
                    copies[k, part].start()
        to_twin[k].start()
        if k < 4:
            to_twin[8 - k].start()

    for part in range(2):
        up[0, part].start()
        down[0, part].start()
    send_h(far_first[9:])
    to_twin[0].start()

    loads[9].wait()
    loads[10].wait()
    loads[11].wait()
    token = lax.broadcasted_iota(jnp.int32, (TOKENS, HEAD_SIZE), 0)
    lane = lax.broadcasted_iota(jnp.int32, (TOKENS, HEAD_SIZE), 1)
    positions = jnp.where(lax.rem(token, 2) == 0, lengths[0], lengths[1]) + lax.div(token, 2)
    angles = positions.astype(F32) * freq_v[...]
    cosine = jnp.cos(angles)
    sine = jnp.sin(angles)
    sine = jnp.where(lane < HEAD_SIZE // 2, -sine, sine)

    def find(j, carry):
        actor = order[j] - t * 8
        return tuple(jnp.where(actor == i, j, carry[i]) for i in range(8))

    stored = lax.fori_loop(0, BLOCKS, find, tuple(jnp.int32(0) for _ in range(8)))
    places = []
    for j in stored:
        k = lax.rem(z + 8 - lax.div(j, 8), 8)
        source = paired(lax.rem(lax.div(j, 2), 4))
        rr = lax.rem(lax.rem(j, 2) + r, 2)
        slot = jnp.int32(0)
        for i in range(1, 8):
            slot = jnp.where(k == RING[i], i, slot)
        places.append(source * 16 + slot * 2 + rr)
    for xs_ in range(4):
        source_y = paired(jnp.int32(xs_))
        for k in range(8):
            for rr in range(2):
                j = (lax.rem(z + 8 - k, 8) * 4 + source_y) * 2 + lax.rem(r + rr, 2)
                xperm[xs_ * 16 + PLACE[k] * 2 + rr] = xblk[order[j]]

    shares[1].wait_recv()
    shares[2].start()

    ring_advance()
    pltpu.make_async_copy(hr, hr, h_recv).wait()
    wide = hr[...].astype(F32)
    left = jnp.concatenate([wide[:, 8 * m : 8 * m + 8, :].reshape(QPEERS * TOKENS, 128) for m in range(4)], axis=1).astype(BF16)
    shares[0].wait_recv()
    shares[2].wait_recv()
    partial = jnp.dot(left, wq[...].reshape(512, IN_COLUMNS), preferred_element_type=F32).reshape(QPEERS, TOKENS, IN_COLUMNS)
    ps[...] = jnp.concatenate([partial[:, :, :256], partial[:, :, 256:512]], axis=1).astype(BF16)
    ps2[...] = jnp.concatenate([partial[:, :, 512:640], partial[:, :, 640:]], axis=1).astype(BF16)

    for source, target, left_sem, got_sem in ((ps, pr, p_send, p_recv), (ps2, pr2, p2_send, p2_recv)):
        for d in far_first:
            pltpu.make_async_remote_copy(
                src_ref=source.at[d],
                dst_ref=target.at[d],
                send_sem=left_sem,
                recv_sem=got_sem,
                device_id=q_peer(QPEERS - d),
                device_id_type=MESH,
            ).start()
        pending.append(pltpu.make_async_copy(source, source, left_sem).wait)
    ring_advance()
    ring_advance()
    pltpu.make_async_copy(pr, pr, p_recv).wait()
    in_scale = np.float32(1.0 / np.sqrt(np.float32(MODEL_WIDTH)))

    def rotate(raw, count):
        normed = raw * lax.rsqrt(jnp.mean(raw * raw, axis=1, keepdims=True) + norm_epsilon)
        cosines = jnp.concatenate([cosine] * count, axis=0)
        sines = jnp.concatenate([sine] * count, axis=0)
        return normed * cosines + pltpu.roll(normed, HEAD_SIZE // 2, 1) * sines

    both = jnp.sum(pr[...].astype(F32), axis=0) * in_scale
    qh[...] = rotate(jnp.concatenate([both[0:8, 0:128], both[0:8, 128:], both[8:16, 0:128], both[8:16, 128:]], axis=0), QUERY_PER_GROUP)

    scale = HEAD_SIZE ** (-0.5)
    contract_last = (((1,), (1,)), ((), ()))
    q_step = lax.rem(lax.broadcasted_iota(jnp.int32, (16, TOKENS), 0), STEPS)
    k_token = lax.broadcasted_iota(jnp.int32, (16, TOKENS), 1)
    slot = lax.broadcasted_iota(jnp.int32, (16, CACHE_SLOTS), 1)
    loads[6].wait()
    loads[7].wait()
    held = []
    for n in range(2):
        queries = qh[pl.ds(n, 16, stride=2), :].astype(BF16)
        scores = (
            lax.dot_general(queries, keys_v[n * CACHE_SLOTS : (n + 1) * CACHE_SLOTS, :], contract_last, preferred_element_type=F32)
            * scale
        )
        past = jnp.where(slot < lengths[n], jnp.exp(scores), 0.0)
        heads = jnp.dot(
            past.astype(BF16), values_v[n * CACHE_SLOTS : (n + 1) * CACHE_SLOTS, :], preferred_element_type=F32
        )
        held.append((queries, jnp.sum(past, axis=1, keepdims=True), heads))
    pltpu.make_async_copy(pr2, pr2, p2_recv).wait()
    both = jnp.sum(pr2[...].astype(F32), axis=0) * in_scale
    new_keys = rotate(both[0:8], 1).astype(BF16)
    new_values = both[8:16].astype(BF16)
    for n in range(2):
        queries, total, heads = held[n]
        recent = lax.dot_general(queries, new_keys, contract_last, preferred_element_type=F32) * scale
        seen = (lax.rem(k_token, 2) == n) & (lax.div(k_token, 2) <= q_step)
        recent = jnp.where(seen, jnp.exp(recent), 0.0)
        total = total + jnp.sum(recent, axis=1, keepdims=True)
        heads = heads + jnp.dot(recent.astype(BF16), new_values, preferred_element_type=F32)
        hh[pl.ds(n, 16, stride=2), :] = heads / total
    heads = hh[...].astype(BF16)

    os[...] = heads
    orr[0] = heads
    for d in (2, 1, 3):
        copy = pltpu.make_async_remote_copy(
            src_ref=os, dst_ref=orr.at[d], send_sem=o_send.at[d - 1], recv_sem=o_recv.at[d - 1], device_id=y_peer(d), device_id_type=MESH
        )
        copy.start()
        pending.append(copy.wait_send)
    ring_advance()
    for d in range(3):
        pltpu.make_async_copy(os, os, o_recv.at[d]).wait()
    wide = orr[...].astype(F32)
    left = jnp.concatenate([wide[:, 8 * h : 8 * h + 8, :].reshape(32, 128) for h in range(4)], axis=1).astype(BF16)
    out_scale = np.float32(1.0 / np.sqrt(np.float32(KEY_VALUE_HEADS * OUT_COLUMNS)))

    def project(half):
        weights = wo[4 * half : 4 * half + 4].reshape(8 * ROWS, OUT_COLUMNS)
        product = lax.dot_general(left, weights, contract_last, preferred_element_type=F32) * out_scale
        return product.reshape(4, 8, 640)

    for k in RING[:4]:
        to_twin[k].wait_recv()
    attn[...] = project(0)
    for k in RING[4:]:
        to_twin[k].wait_recv()
    s4[...] = jnp.concatenate([attn[...], project(1)], axis=1).astype(BF16)
    for e in (2, 1, 3):
        copy = pltpu.make_async_remote_copy(
            src_ref=s4.at[lax.rem(xx + e, 4)],
            dst_ref=r4.at[e - 1],
            send_sem=r4_send.at[e - 1],
            recv_sem=r4_recv.at[e - 1],
            device_id=x_peer(e),
            device_id_type=MESH,
        )
        copy.start()
        pending.append(copy.wait_send)
    summed = s4[xx].astype(F32)
    for e in range(3):
        pltpu.make_async_copy(s4.at[0], s4.at[0], r4_recv.at[e]).wait()
        summed = summed + r4[e].astype(F32)
    s5[...] = summed.astype(BF16)
    target_y = paired(xx)

    def to_owner(dx, flip):
        return pltpu.make_async_remote_copy(
            src_ref=s5,
            dst_ref=r5.at[t],
            send_sem=r5_send.at[2 * dx + flip],
            recv_sem=r5_recv.at[t],
            device_id=dev(z, target_y, r, lax.rem(xx + dx, 4) * 2 + lax.rem(yh + flip, 2)),
            device_id_type=MESH,
        )

    for dx, flip in ((2, 1), (2, 0), (1, 1), (3, 1), (1, 0), (3, 0), (0, 1)):
        to_owner(dx, flip).start()
        pending.append(to_owner(dx, flip).wait_send)
    pending.append(lambda: pl.when(xx != 0)(to_owner(0, 0).wait_send))

    @pl.when(xx != 0)
    def _():
        to_owner(0, 0).start()

    @pl.when(xx == 0)
    def _():
        pltpu.make_async_copy(s5, r5.at[t], r5_recv.at[t]).start()


    squares = jnp.zeros((TOKENS, 128), F32)
    for xs_ in range(4):
        for i in (2 * xs_, 2 * xs_ + 1):
            pltpu.make_async_copy(s5, r5.at[i], r5_recv.at[i]).wait()
        both = r5[2 * xs_].astype(F32) + r5[2 * xs_ + 1].astype(F32)
        for b in range(8):
            block = widen(both[:, b * ROWS : (b + 1) * ROWS])
            for half in range(2):
                place = xs_ * 16 + half * 8 + b
                residual = block[half * 8 : half * 8 + 8] + xperm[place]
                zblk[place] = residual
                squares = squares + residual * residual
    rscale = lax.rsqrt(jnp.sum(squares, axis=1, keepdims=True) * np.float32(1.0 / MODEL_WIDTH) + norm_epsilon)
    pieces = [zblk[place][:, :ROWS] for place in places]
    mixed_out[...] = (jnp.concatenate(pieces, axis=1) * rscale * post_v[...].reshape(1, 640)).astype(BF16)

    for wait in pending:
        wait()


def finish(master_in, mixed_in, master_out, mixed_out, held, sem):
    write_master = pltpu.make_async_copy(master_in, master_out, sem.at[0])
    write_master.start()
    values = mixed_in[...].astype(F32)
    for s in range(STEPS):
        held[s] = values[2 * s : 2 * s + 2].astype(BF16)
    write_mixed = pltpu.make_async_copy(held, mixed_out, sem.at[1])
    write_mixed.start()
    write_mixed.wait()
    write_master.wait()


def body(
    master, adam_first_moment, adam_second_moment, gradient, resync_order, inputs, in_gain, post_gain, lengths,
    cached_key_rows, cached_value_rows,
):
    half = np.arange(HEAD_SIZE // 2, dtype=np.float64)
    freqs = (rope_theta ** (-(half * 2.0 / HEAD_SIZE))).astype(np.float32)
    freqs = jnp.asarray(np.concatenate([freqs, freqs])[None, :])
    vmem = pl.BlockSpec(memory_space=pltpu.VMEM)
    hbm = pl.BlockSpec(memory_space=pltpu.HBM)
    dma = pltpu.SemaphoreType.DMA
    flat = (ROWS * 10, 128)
    new_master, mixed = pl.pallas_call(
        kernel,
        out_shape=(pltpu.VMEM(flat, F32), pltpu.VMEM((TOKENS, 640), BF16)),
        in_specs=[hbm] * 12,
        out_specs=(vmem, vmem),
        scratch_shapes=[
            pltpu.SMEM((BLOCKS,), jnp.int32),
            pltpu.SMEM((2,), jnp.int32),
            pltpu.VMEM((640,), F32),
            pltpu.VMEM((1, HEAD_SIZE), F32),
            pltpu.VMEM((STEPS, 2, MODEL_WIDTH), BF16),
            pltpu.VMEM((1, MODEL_WIDTH), F32),
            pltpu.VMEM((TOKENS, MODEL_WIDTH), F32),
            pltpu.VMEM((32, HEAD_SIZE), F32),
            pltpu.VMEM((32, HEAD_SIZE), F32),
            pltpu.VMEM((BLOCKS, TOKENS, 128), F32),
            pltpu.VMEM((BLOCKS, TOKENS, 128), F32),
            pltpu.VMEM((BLOCKS, TOKENS, 128), F32),
            pltpu.VMEM((BLOCKS, TOKENS, 128), F32),
            pltpu.VMEM(flat, F32),
            pltpu.VMEM(flat, F32),
            pltpu.VMEM(flat, F32),
            pltpu.VMEM((ROWS, 1280), BF16),
            pltpu.VMEM((2 * CACHE_SLOTS, HEAD_SIZE), BF16),
            pltpu.VMEM((2 * CACHE_SLOTS, HEAD_SIZE), BF16),
            pltpu.VMEM((QPEERS, 32, 128), BF16),
            pltpu.VMEM((QPEERS, 32, 128), BF16),
            pltpu.VMEM((4, 128, IN_COLUMNS), BF16),
            pltpu.VMEM((8, 2, ROWS, OUT_COLUMNS), BF16),
            pltpu.VMEM((QPEERS, 16, 256), BF16),
            pltpu.VMEM((QPEERS, 16, 256), BF16),
            pltpu.VMEM((QPEERS, 16, 128), BF16),
            pltpu.VMEM((QPEERS, 16, 128), BF16),
            pltpu.VMEM((32, 128), BF16),
            pltpu.VMEM((4, 32, 128), BF16),
            pltpu.VMEM((4, 8, 640), F32),
            pltpu.VMEM((4, 16, 640), BF16),
            pltpu.VMEM((3, 16, 640), BF16),
            pltpu.VMEM((16, 640), BF16),
            pltpu.VMEM((8, 16, 640), BF16),
            dma((12,)), dma, dma, dma((3,)), dma((3,)), dma((16,)), dma((16,)), dma((8,)), dma((8,)),
            dma, dma, dma, dma, dma((3,)), dma((3,)), dma((3,)), dma((3,)), dma((8,)), dma((8,)),
        ],
        compiler_params=pltpu.CompilerParams(collective_id=0, has_side_effects=True, vmem_limit_bytes=56 << 20),
        cost_estimate=pl.CostEstimate(flops=400_000_000, bytes_accessed=4_500_000, transcendentals=200_000),
        name="adam_attention",
    )(
        resync_order, lengths, inputs, in_gain.reshape(1, MODEL_WIDTH), post_gain, freqs,
        master.reshape(flat), adam_first_moment.reshape(flat), adam_second_moment.reshape(flat), gradient.reshape(ROWS, 1280),
        cached_key_rows.reshape(2 * CACHE_SLOTS, HEAD_SIZE), cached_value_rows.reshape(2 * CACHE_SLOTS, HEAD_SIZE),
    )
    new_master, mixed = pl.pallas_call(
        finish,
        out_shape=(jax.ShapeDtypeStruct(flat, F32), jax.ShapeDtypeStruct((STEPS, 2, 640), BF16)),
        in_specs=[vmem, vmem],
        out_specs=(hbm, hbm),
        scratch_shapes=[pltpu.VMEM((STEPS, 2, 640), BF16), dma((2,))],
        compiler_params=pltpu.CompilerParams(vmem_limit_bytes=2 << 20),
        name="finish",
    )(pltpu.with_memory_space_constraint(new_master, pltpu.VMEM), pltpu.with_memory_space_constraint(mixed, pltpu.VMEM))
    return new_master.reshape(ROWS, 1, 1280), mixed


def solution(mesh):
    in_specs = (
        P(("learn", "rep"), "tp", None),
        P(("learn", "rep"), "tp", None),
        P(("learn", "rep"), "tp", None),
        P(("learn", "rep"), "tp", None),
        P(),
        P(None, ("learn", "rep"), None),
        P(),
        P("tp"),
        P(("learn", "rep")),
        P(("learn", "rep"), "tp", None, None),
        P(("learn", "rep"), "tp", None, None),
    )
    out_specs = (P(("learn", "rep"), "tp", None), P(None, ("learn", "rep"), "tp"))
    return jax.shard_map(body, mesh=mesh, in_specs=in_specs, out_specs=out_specs, check_vma=False)
```
